256 devices in a mesh: foot: 32 (over z, x_lo, core), layer: 8 (over x_hi, y).
Axes of the slice: x: 4 (x_hi: 2, x_lo: 2; x = x_hi * 2 + x_lo), y: 4, z: 8, core: 2. Of those that a mesh axis runs over, the one named last changes fastest.
Arguments:
- conserved: float32 [5, 4, 4, 4, 64, 8192], P(None, None, None, None, 'layer', 'foot'), as said below
- register: float32 [5, 4, 4, 4, 64, 8192], P(None, None, None, None, 'layer', 'foot'), may hold values from -3 to 3
- neighbour: int32 [4, 8192], P(None, 'foot'), may hold values from 0 to 8191, as said below
- side_type: int32 [4, 8192], P(None, 'foot'), may hold values from 0 to 2, as said below
Outputs:
- advanced: float32 [5, 4, 4, 4, 64, 8192], P(None, None, None, None, 'layer', 'foot')
- new_register: float32 [5, 4, 4, 4, 64, 8192], P(None, None, None, None, 'layer', 'foot')
The draws below stay inside these ranges and needn't reach their ends.
Inputs may be any that keep to these rules, and one draw needn't show every extreme that they name: `conserved`: every density lies in 0.5 to 1.5, every pressure in 0.4 to 1.6, every velocity component within -0.8 to 0.8. `neighbour`: where side_type is 2 the entry names the column itself; elsewhere the named column's side s xor 1 names this column back, and the two elements share their face nodes index for index. The footprint is a grid of 8 x 4 square tiles of 16 x 16 columns; the columns of tile (a, b) are the 256 columns c with c // 256 = 4 * a + b, in any order. A side 0 or 1 of a column names a column of tile (a - 1, b) or (a + 1, b) or of its own tile, a side 2 or 3 one of tile (a, b - 1) or (a, b + 1) or of its own tile; sides on the district's outer edge have side_type 2. `side_type`: A side of type 1 faces a side of type 1.
All inputs are finite; a program needn't handle non-finite values.
Results may differ from the reference program's by a relative error of at most 0.0003.
Values sent between devices are 32-bit elements; how exact they have to be, the bound alone decides.
A program may use at most 128 MiB of HBM per device.

```python
import jax
import jax.numpy as jnp
import numpy as np
from jax import lax

TS = 16
COLS = 256
TILES_X = 8
NCOL = 8192
NZ = 64


def layout(key):
    layout_key = jax.random.fold_in(key, 7)
    devices = NCOL // COLS
    device_keys = jax.random.split(jax.random.fold_in(layout_key, 2), devices)
    cell_slot = jax.vmap(lambda subkey: jax.random.permutation(subkey, COLS))(device_keys)
    width_x = TILES_X * TS
    width_y = 4 * TS
    x_index = jnp.arange(width_x, dtype=jnp.int32)[:, None]
    y_index = jnp.arange(width_y, dtype=jnp.int32)[None, :]
    tile_number = x_index // TS * 4 + y_index // TS
    cell_number = x_index % TS * TS + y_index % TS
    device_of = tile_number
    column_id = device_of * COLS + cell_slot[device_of, cell_number]
    wall_x = jax.random.randint(jax.random.fold_in(layout_key, 3), (width_x + 1, width_y), 0, 100) < 15
    wall_y = jax.random.randint(jax.random.fold_in(layout_key, 4), (width_x, width_y + 1), 0, 100) < 15
    framed = jnp.pad(column_id, 1, constant_values=-1)
    across = jnp.stack([framed[:-2, 1:-1], framed[2:, 1:-1], framed[1:-1, :-2], framed[1:-1, 2:]])
    wall_faces = jnp.stack([wall_x[:-1], wall_x[1:], wall_y[:, :-1], wall_y[:, 1:]])
    inside = across >= 0
    face_types = jnp.where(inside, jnp.where(wall_faces, 1, 0), 2).astype(jnp.int32)
    named = jnp.where(inside, across, column_id[None]).astype(jnp.int32)
    flat_ids = column_id.reshape(-1)
    neighbour_out = jnp.zeros((4, NCOL), jnp.int32).at[:, flat_ids].set(named.reshape(4, -1))
    types_out = jnp.zeros((4, NCOL), jnp.int32).at[:, flat_ids].set(face_types.reshape(4, -1))
    return (neighbour_out, types_out)


def draw_neighbour(key, part):
    return layout(key)[0]


def draw_side_type(key, part):
    return layout(key)[1]


def draw_conserved(key, part):
    grid_shape = (4, 4, 4, NZ, NCOL)
    density_key = jax.random.fold_in(key, 11)
    velocity_key = jax.random.fold_in(key, 12)
    pressure_key = jax.random.fold_in(key, 13)
    density = jnp.clip(1.0 + 0.15 * jax.random.normal(density_key, grid_shape, jnp.float32), 0.6, 1.4)
    velocity = jnp.clip(0.3 * jax.random.normal(velocity_key, (3,) + grid_shape, jnp.float32), -0.8, 0.8)
    pressure = jnp.clip(0.9 * jnp.exp(0.2 * jax.random.normal(pressure_key, grid_shape, jnp.float32)), 0.45, 1.5)
    momentum = density * velocity
    energy = pressure / 0.4 + 0.5 * density * jnp.sum(velocity * velocity, axis=0)
    return jnp.concatenate([density[None], momentum, energy[None]], axis=0).astype(jnp.float32)


def block_levels(rng, shape, pieces, least, top_value):
    def one(dim, parts):
        draws = jax.random.uniform(jax.random.fold_in(jax.random.fold_in(rng, 6), dim), (parts,), jnp.float32, least / len(pieces), top_value / len(pieces))
        return jnp.repeat(jnp.exp(draws), shape[dim] // parts).reshape((-1,) + (1,) * (len(shape) - dim - 1))

    loudness = one(*pieces[0])
    for cut in pieces[1:]:
        loudness = loudness * one(*cut)
    return loudness


def scatter_about(key, shape, spread, reach, pieces=(), kind=jnp.bfloat16):
    values = jax.random.normal(key, shape, jnp.float32) * spread
    if len(pieces) > 0:
        values = block_levels(key, shape, pieces, -0.22, 0.18) * values
    return jnp.clip(values, min=-reach, max=reach).astype(kind)


def setup_inputs(seed: int = 0) -> dict:
    key_list = jax.random.split(jax.random.key(seed), 5)
    return {
        "conserved": draw_conserved(jax.random.fold_in(key_list[4], 71), 0),
        "register": scatter_about(key_list[1], (5, 4, 4, 4, NZ, NCOL), 0.5, 3.0, ((4, 8), (5, 32)), jnp.float32),
        "neighbour": draw_neighbour(jax.random.fold_in(key_list[4], 71), 0),
        "side_type": draw_side_type(jax.random.fold_in(key_list[4], 71), 0),
    }


ADIABATIC = 1.4
LIFT_FACTOR = 6.0
TIME_STEP = 0.02
SECTION_DECAY = -0.4178904745
SECTION_WEIGHT = 1.720146321549
FREE_STREAM = (1.0, 0.3, 0.1, 0.0, 1.0 / 0.56 + 0.05)

def derivative_table():
    nodes = np.array([-1.0, -1.0 / np.sqrt(5.0), 1.0 / np.sqrt(5.0), 1.0])
    products = np.array([np.prod([nodes[target_node] - nodes[another] for another in range(4) if another != target_node]) for target_node in range(4)])
    matrix = np.zeros((4, 4))
    for target_node in range(4):
        for source_node in range(4):
            if target_node != source_node:
                matrix[target_node, source_node] = products[target_node] / products[source_node] / (nodes[target_node] - nodes[source_node])
            else:
                matrix[target_node, target_node] = sum((1.0 / (nodes[target_node] - nodes[another]) for another in range(4) if another != target_node))
    return jnp.asarray(matrix, dtype=jnp.float32)

def primitives(conserved):
    density = conserved[0]
    velocity = conserved[1:4] / density
    pressure = (ADIABATIC - 1.0) * (conserved[4] - 0.5 * density * lax.optimization_barrier(jnp.sum(velocity * velocity, axis=0)))
    return (density, velocity, pressure)

def normal_flux(conserved, direction, velocity, pressure):
    normal_velocity = velocity[direction]
    entries = [conserved[1 + direction]]
    for component in range(3):
        entry_value = conserved[1 + component] * normal_velocity
        if component == direction:
            entry_value = entry_value + pressure
        entries.append(entry_value)
    entries.append((conserved[4] + pressure) * normal_velocity)
    return jnp.stack(entries)

def face_term(inside, outside, direction, orientation):
    density_in, velocity_in, pressure_in = primitives(inside)
    density_out, velocity_out, pressure_out = primitives(outside)
    flux_in = orientation * normal_flux(inside, direction, velocity_in, pressure_in)
    flux_out = orientation * normal_flux(outside, direction, velocity_out, pressure_out)
    speed_in = jnp.abs(velocity_in[direction]) + jnp.sqrt(ADIABATIC * pressure_in / density_in)
    speed_out = jnp.abs(velocity_out[direction]) + jnp.sqrt(ADIABATIC * pressure_out / density_out)
    wave_speed = jnp.maximum(speed_in, speed_out)
    common = 0.5 * (flux_in + flux_out) - 0.5 * wave_speed * (outside - inside)
    return -LIFT_FACTOR * (common - flux_in)

def mirrored(inside, direction):
    reflect = jnp.where(jnp.arange(5) == 1 + direction, -1.0, 1.0).astype(jnp.float32)
    return inside * reflect.reshape((5,) + (1,) * (inside.ndim - 1))

def far_state(inside):
    stream = jnp.asarray(FREE_STREAM, dtype=jnp.float32).reshape((5,) + (1,) * (inside.ndim - 1))
    return jnp.broadcast_to(stream, inside.shape)

def outer_state(inside, ghost_side, face_kind, direction):
    return jnp.where(face_kind == 0, ghost_side, jnp.where(face_kind == 1, mirrored(inside, direction), far_state(inside)))

def tendency(conserved, outsides):
    density, velocity, pressure = primitives(conserved)
    derivative = derivative_table()
    highest = lax.Precision.HIGHEST
    volume = jnp.einsum('pi,vijk...->vpjk...', derivative, normal_flux(conserved, 0, velocity, pressure), precision=highest)
    volume = volume + jnp.einsum('pj,vijk...->vipk...', derivative, normal_flux(conserved, 1, velocity, pressure), precision=highest)
    volume = volume + jnp.einsum('pk,vijk...->vijp...', derivative, normal_flux(conserved, 2, velocity, pressure), precision=highest)
    change = -volume
    change = change.at[:, 0].add(face_term(conserved[:, 0], outsides[0], 0, -1.0))
    change = change.at[:, 3].add(face_term(conserved[:, 3], outsides[1], 0, 1.0))
    change = change.at[:, :, 0].add(face_term(conserved[:, :, 0], outsides[2], 1, -1.0))
    change = change.at[:, :, 3].add(face_term(conserved[:, :, 3], outsides[3], 1, 1.0))
    change = change.at[:, :, :, 0].add(face_term(conserved[:, :, :, 0], outsides[4], 2, -1.0))
    change = change.at[:, :, :, 3].add(face_term(conserved[:, :, :, 3], outsides[5], 2, 1.0))
    return change

def reference(conserved, register, neighbour, side_type):
    layers = conserved.shape[4]
    bottoms = conserved[:, :, :, 0]
    tops = conserved[:, :, :, 3]

    def one_layer(height):
        current = lax.dynamic_index_in_dim(conserved, height, 4, keepdims=False)
        register_now = lax.dynamic_index_in_dim(register, height, 4, keepdims=False)
        below_top = lax.dynamic_index_in_dim(tops, jnp.maximum(height - 1, 0).astype(jnp.int32), 3, keepdims=False)
        above_bottom = lax.dynamic_index_in_dim(bottoms, jnp.minimum(height + 1, layers - 1).astype(jnp.int32), 3, keepdims=False)
        own_bottom = current[:, :, :, 0]
        own_top = current[:, :, :, 3]
        outside_low = jnp.where(height == 0, mirrored(own_bottom, 2), below_top)
        outside_high = jnp.where(height == layers - 1, far_state(own_top), above_bottom)
        lateral = [current[:, 0], current[:, 3], current[:, :, 0], current[:, :, 3]]
        outsides = []
        for facing in range(4):
            ghost_side = jnp.take(lateral[facing ^ 1], neighbour[facing], axis=-1)
            outsides.append(outer_state(lateral[facing], ghost_side, side_type[facing], facing // 2))
        outsides.append(outside_low)
        outsides.append(outside_high)
        change = tendency(current, outsides)
        register_next = SECTION_DECAY * register_now + TIME_STEP * change
        return (current + SECTION_WEIGHT * register_next, register_next)
    advanced, register_next = lax.map(one_layer, jnp.arange(layers, dtype=jnp.int32))
    return (jnp.moveaxis(advanced, 0, 4), jnp.moveaxis(register_next, 0, 4))
```

```python
import functools

import jax
import jax.numpy as jnp
import numpy as np
from jax import lax
from jax.experimental import pallas as pl
from jax.experimental.pallas import tpu as pltpu
from jax.sharding import PartitionSpec as P

TIME_STEP = 0.02
SECTION_DECAY = -0.4178904745
SECTION_WEIGHT = 1.720146321549
LIFT = 3.0 * TIME_STEP
FREE_STREAM = (1.0, 0.3, 0.1, 0.0, 1.0 / 0.56 + 0.05)
MESH = pl.DeviceIdType.MESH
SLOTS = 16
BF16 = jnp.bfloat16
F32 = jnp.float32
STEPS = (4, -4, 1, -1)


def derivative_entries():
    nodes = np.array([-1.0, -1.0 / np.sqrt(5.0), 1.0 / np.sqrt(5.0), 1.0])
    products = np.array(
        [np.prod([nodes[t] - nodes[a] for a in range(4) if a != t]) for t in range(4)]
    )
    matrix = np.zeros((4, 4))
    for t in range(4):
        for s in range(4):
            if t != s:
                matrix[t, s] = products[t] / products[s] / (nodes[t] - nodes[s])
            else:
                matrix[t, t] = sum(1.0 / (nodes[t] - nodes[a]) for a in range(4) if a != t)
    return matrix


ENTRIES = -TIME_STEP * derivative_entries()
ODD = [[0.5 * float(ENTRIES[p, i] - ENTRIES[p, 3 - i]) for i in (0, 1)] for p in (0, 1)]
EVEN = [0.5 * float(ENTRIES[p, 0] + ENTRIES[p, 3]) for p in (0, 1)]


def derived(f):
    s0, d0 = f[0] + f[3], f[0] - f[3]
    s1, d1 = f[1] + f[2], f[1] - f[2]
    t = s0 - s1
    a = ODD[0][0] * d0 + ODD[0][1] * d1
    b = EVEN[0] * t
    c = ODD[1][0] * d0 + ODD[1][1] * d1
    e = EVEN[1] * t
    return a + b, c + e, c - e, a - b


def inverse(x):
    r = pl.reciprocal(x, approx=True)
    return r * (2.0 - x * r)


def split(x):
    hi = x.astype(BF16)
    lo = (x - hi.astype(F32)).astype(BF16)
    return hi, lo


def dot(a, b):
    return jnp.dot(a, b, preferred_element_type=F32)


def dot_nt(a, b):
    return lax.dot_general(a, b, (((1,), (1,)), ((), ())), preferred_element_type=F32)


def trace_of(cv, side):
    face = (0, 3)[side % 2]
    block = cv[:, face] if side < 2 else cv[:, :, face]
    return block.reshape(640, 256)


def exchange_kernel(
    cons, reg, nb, cv, acc, ghost, vert,
    prim, stage, packed, arrived, sendv, recvv, load_sem, send_sem, recv_sem, vsend_sem, vrecv_sem,
):
    foot, layer = lax.axis_index("foot"), lax.axis_index("layer")
    feet, layers = lax.axis_size("foot"), lax.axis_size("layer")

    def at_foot(by):
        return (lax.rem(foot + by + feet, feet), layer)

    def at_layer(by):
        return (foot, lax.rem(layer + by + layers, layers))

    loads = [pltpu.make_async_copy(cons.at[v], cv.at[v], load_sem.at[v]) for v in range(5)]
    for copy in loads:
        copy.start()
    reg_load = pltpu.make_async_copy(reg, acc, load_sem.at[5])
    reg_load.start()

    barrier = pltpu.get_barrier_semaphore()
    partners = [at_foot(by) for by in STEPS] + [at_layer(by) for by in (1, -1)]
    for partner in partners:
        pl.semaphore_signal(barrier, inc=1, device_id=partner, device_id_type=MESH)

    here = nb[...] - foot * 256
    remote = jnp.logical_or(here < 0, here >= 256)
    mask = jnp.where(remote, 1.0, 0.0)
    mask8 = jnp.concatenate([mask, jnp.zeros_like(mask)], axis=0).astype(BF16)
    rows = lax.broadcasted_iota(jnp.int32, (256, 256), 0)
    cols = lax.broadcasted_iota(jnp.int32, (256, 256), 1)
    before = jnp.where(rows < cols, 1.0, 0.0).astype(BF16)
    rank = dot(mask8, before)
    rank = jnp.where(mask8.astype(F32) > 0.5, rank, -1.0).astype(jnp.int32)
    named = (lax.bitwise_and(nb[...], 255) + 1).astype(F32)
    named8 = jnp.concatenate([named, jnp.zeros_like(named)], axis=0).astype(BF16)
    slot = lax.bitwise_and(lax.broadcasted_iota(jnp.int32, (128, 256), 0), SLOTS - 1)
    lane_z = lax.broadcasted_iota(jnp.int32, (80, 128), 1) // SLOTS

    for copy in loads:
        copy.wait()
    pl.semaphore_wait(barrier, len(partners))

    vcopies = []
    for way in (0, 1):
        for h in (0, 1):
            lanes = pl.ds(h * 128, 128)
            stage[2 * way + h] = cv[:, :, :, pl.ds(24 * way, 8), lanes].reshape(640, 128)
            sendv[way, :, lanes] = stage[2 * way + h, pl.ds(7 * way, 80, stride=8), :]
        copy = pltpu.make_async_remote_copy(
            src_ref=sendv.at[way], dst_ref=recvv.at[way], send_sem=vsend_sem.at[way],
            recv_sem=vrecv_sem.at[way], device_id=at_layer((-1, 1)[way]), device_id_type=MESH,
        )
        copy.start()
        vcopies.append(copy)

    copies = []
    for side in range(4):
        q = side ^ 1
        hi, lo = split(trace_of(cv, q))
        pick = jnp.where(rank[q:q + 1] == slot, 1.0, 0.0).astype(BF16)
        stage[side] = dot_nt(hi, pick) + dot_nt(lo, pick)
        total = stage[side, pl.ds(0, 80, stride=8), :]
        for z in range(1, 8):
            total = jnp.where(lane_z == z, stage[side, pl.ds(z, 80, stride=8), :], total)
        packed[side, 0:80] = total
        packed[side, 80:88] = dot_nt(named8, pick)
        copy = pltpu.make_async_remote_copy(
            src_ref=packed.at[side], dst_ref=arrived.at[side], send_sem=send_sem.at[side],
            recv_sem=recv_sem.at[side], device_id=at_foot(STEPS[side]), device_id_type=MESH,
        )
        copy.start()
        copies.append(copy)
        select = jnp.where(here[side:side + 1] == rows, 1.0, 0.0).astype(BF16)
        ghost[side] = (dot(hi, select) + dot(lo, select)).reshape(5, 4, 32, 256)

    reg_load.wait()

    def z_lines(line, carry):
        i, j = line // 4, line % 4
        q = [[cv[v, i, j, pl.ds(8 * k, 8), :] for k in range(4)] for v in range(5)]
        flux = [[], [], [], [], []]
        for k in range(4):
            rho, mx, my, mz, energy = (q[v][k] for v in range(5))
            r = inverse(rho)
            kinetic = (mx * mx + my * my + mz * mz) * r
            pressure = 0.4 * energy - 0.2 * kinetic
            vz = mz * r
            rows_k = pl.ds(8 * k, 8)
            prim[0, i, j, rows_k, :] = mx * r
            prim[1, i, j, rows_k, :] = my * r
            prim[2, i, j, rows_k, :] = pressure
            flux[0].append(mz)
            flux[1].append(mx * vz)
            flux[2].append(my * vz)
            flux[3].append(mz * vz + pressure)
            flux[4].append((energy + pressure) * vz)
        for v in range(5):
            out = derived(flux[v])
            for k in range(4):
                rows_k = pl.ds(8 * k, 8)
                acc[v, i, j, rows_k, :] = SECTION_DECAY * acc[v, i, j, rows_k, :] + out[k]
        return carry

    lax.fori_loop(0, 16, z_lines, 0)

    def lines(direction, line, carry):
        a, k = line // 4, line % 4
        rows_k = pl.ds(pl.multiple_of(8 * k, 8), 8)

        def at(node):
            return (node, a, rows_k, slice(None)) if direction == 0 else (a, node, rows_k, slice(None))

        flux = [[], [], [], [], []]
        for node in range(4):
            vd = prim[(direction,) + at(node)]
            pressure = prim[(2,) + at(node)]
            m = [cv[(1 + c,) + at(node)] for c in range(3)]
            flux[0].append(m[direction])
            for c in range(3):
                entry = m[c] * vd
                if c == direction:
                    entry = entry + pressure
                flux[1 + c].append(entry)
            flux[4].append((cv[(4,) + at(node)] + pressure) * vd)
        for v in range(5):
            out = derived(flux[v])
            for node in range(4):
                acc[(v,) + at(node)] = acc[(v,) + at(node)] + out[node]
        return carry

    lax.fori_loop(0, 16, functools.partial(lines, 0), 0)
    lax.fori_loop(0, 16, functools.partial(lines, 1), 0)

    lane_z3 = lax.broadcasted_iota(jnp.int32, (80, 8, 128), 2) // SLOTS
    sub_z3 = lax.broadcasted_iota(jnp.int32, (80, 8, 128), 1)
    column = (lax.broadcasted_iota(jnp.int32, (256, 128), 0) + 1).astype(F32)
    for side in range(4):
        copies[side].wait()
        q = side ^ 1
        place = jnp.where(arrived[side, 80 + q:81 + q] == column, 1.0, 0.0).astype(BF16)
        spread = jnp.where(lane_z3 == sub_z3, arrived[side, 0:80][:, None, :], 0.0).reshape(640, 128)
        hi, lo = split(spread)
        both = jnp.concatenate([hi, lo], axis=1)
        twice = jnp.concatenate([place, place], axis=1)
        ghost[side] = ghost[side] + dot_nt(both, twice).reshape(5, 4, 32, 256)

    for copy in vcopies:
        copy.wait()
    lowest, highest = layer == 0, layer == layers - 1
    for v in range(5):
        part = pl.ds(16 * v, 16)
        own = sendv[0, part, :]
        vert[0, part, :] = jnp.where(lowest, -own if v == 3 else own, recvv[1, part, :])
        vert[1, part, :] = jnp.where(highest, jnp.full_like(own, FREE_STREAM[v]), recvv[0, part, :])


def state(q, direction, need_all=False):
    rho, energy = q[0], q[4]
    r = inverse(rho)
    kinetic = (q[1] * q[1] + q[2] * q[2] + q[3] * q[3]) * r
    pressure = 0.4 * energy - 0.2 * kinetic
    square = 1.4 * pressure * r
    sound = square * lax.rsqrt(square)
    return r, pressure, sound


def surface_kernel(cv, acc, ghost, vert, kinds, adv, new, adv_v, new_v, out_sem):
    sub = lax.broadcasted_iota(jnp.int32, (8, 128), 0)
    outs = []
    for i in range(4):

        def half(h, carry):
            lanes = pl.ds(pl.multiple_of(h * 128, 128), 128)
            kind = [jnp.broadcast_to(kinds[s:s + 1, lanes], (8, 128)) for s in range(4)]
            open_face = [kind[s] == 0 for s in range(4)]
            wall = [kind[s] == 1 for s in range(4)]
            for j in range(4):
                for k in range(4):
                    rows_k = pl.ds(8 * k, 8)
                    q = [cv[v, i, j, rows_k, lanes] for v in range(5)]
                    total = [acc[v, i, j, rows_k, lanes] for v in range(5)]
                    faces = []
                    if i in (0, 3):
                        faces.append((0, 0 if i == 0 else 1, (j, k)))
                    if j in (0, 3):
                        faces.append((1, 2 if j == 0 else 3, (i, k)))
                    if k in (0, 3):
                        faces.append((2, 4 if k == 0 else 5, (i, j)))
                    if faces:
                        r_in, p_in, c_in = state(q, 0)
                    for d, side, (a, b) in faces:
                        if side < 4:
                            outer = []
                            for v in range(5):
                                inner = -q[v] if v == 1 + d else q[v]
                                other = jnp.where(wall[side], inner, FREE_STREAM[v])
                                got = ghost[side, v, a, pl.ds(8 * b, 8), lanes]
                                outer.append(jnp.where(open_face[side], got, other))
                        else:
                            outer = []
                            for v in range(5):
                                m = v * 16 + a * 4 + b
                                if side == 4:
                                    near = cv[v, i, j, pl.ds(24, 8), lanes]
                                    near = pltpu.roll(near, 1, 0)
                                    edge = jnp.broadcast_to(vert[0, m:m + 1, lanes], (8, 128))
                                    outer.append(jnp.where(sub == 0, edge, near))
                                else:
                                    near = cv[v, i, j, pl.ds(0, 8), lanes]
                                    near = pltpu.roll(near, 7, 0)
                                    edge = jnp.broadcast_to(vert[1, m:m + 1, lanes], (8, 128))
                                    outer.append(jnp.where(sub == 7, edge, near))
                        sign = -1.0 if side % 2 == 0 else 1.0
                        r_out, p_out, c_out = state(outer, d)
                        v_in, v_out = q[1 + d] * r_in, outer[1 + d] * r_out
                        lam = LIFT * jnp.maximum(jnp.abs(v_in) + c_in, jnp.abs(v_out) + c_out)
                        s_in, s_out = (sign * LIFT) * v_in, (sign * LIFT) * v_out
                        w_in, w_out = lam - s_in, lam - s_out
                        for v in range(5):
                            total[v] = total[v] + (w_out * outer[v] - w_in * q[v])
                        total[1 + d] = total[1 + d] - (sign * LIFT) * (p_out - p_in)
                        total[4] = total[4] - (p_out * s_out - p_in * s_in)
                    for v in range(5):
                        new_v[v, i, j, rows_k, lanes] = total[v]
                        adv_v[v, i, j, rows_k, lanes] = q[v] + SECTION_WEIGHT * total[v]
            return carry

        lax.fori_loop(0, 2, half, 0)
        for n, (src, dst) in enumerate(((adv_v, adv), (new_v, new))):
            copy = pltpu.make_async_copy(src.at[:, i], dst.at[:, i], out_sem.at[n, i])
            copy.start()
            outs.append(copy)
    for copy in outs:
        copy.wait()


def per_device(conserved, register, neighbour, side_type):
    shape = (5, 4, 4, 32, 256)
    cons, reg = conserved.reshape(shape), register.reshape(shape)
    cv, acc, ghost, vert = pl.pallas_call(
        exchange_kernel,
        name="exchange",
        out_shape=(
            pltpu.VMEM(shape, F32),
            pltpu.VMEM(shape, F32),
            pltpu.VMEM((4, 5, 4, 32, 256), F32),
            pltpu.VMEM((2, 80, 256), F32),
        ),
        in_specs=[
            pl.BlockSpec(memory_space=pl.ANY),
            pl.BlockSpec(memory_space=pl.ANY),
            pl.BlockSpec(memory_space=pltpu.VMEM),
        ],
        out_specs=tuple([pl.BlockSpec(memory_space=pltpu.VMEM)] * 4),
        scratch_shapes=[
            pltpu.VMEM((3, 4, 4, 32, 256), F32),
            pltpu.VMEM((4, 640, 128), F32),
            pltpu.VMEM((4, 88, 128), F32),
            pltpu.VMEM((4, 88, 128), F32),
            pltpu.VMEM((2, 80, 256), F32),
            pltpu.VMEM((2, 80, 256), F32),
            pltpu.SemaphoreType.DMA((6,)),
            pltpu.SemaphoreType.DMA((4,)),
            pltpu.SemaphoreType.DMA((4,)),
            pltpu.SemaphoreType.DMA((2,)),
            pltpu.SemaphoreType.DMA((2,)),
        ],
        compiler_params=pltpu.CompilerParams(
            collective_id=0, has_side_effects=True, vmem_limit_bytes=40 * 1024 * 1024
        ),
    )(cons, reg, neighbour)
    cv, acc, ghost, vert = (
        pltpu.with_memory_space_constraint(x, pltpu.VMEM) for x in (cv, acc, ghost, vert)
    )
    adv, new = pl.pallas_call(
        surface_kernel,
        name="surface",
        out_shape=(jax.ShapeDtypeStruct(shape, F32), jax.ShapeDtypeStruct(shape, F32)),
        in_specs=[pl.BlockSpec(memory_space=pltpu.VMEM)] * 5,
        out_specs=(pl.BlockSpec(memory_space=pl.ANY), pl.BlockSpec(memory_space=pl.ANY)),
        scratch_shapes=[
            pltpu.VMEM(shape, F32),
            pltpu.VMEM(shape, F32),
            pltpu.SemaphoreType.DMA((2, 4)),
        ],
        compiler_params=pltpu.CompilerParams(vmem_limit_bytes=32 * 1024 * 1024),
    )(cv, acc, ghost, vert, side_type)
    full = (5, 4, 4, 4, 8, 256)
    return adv.reshape(full), new.reshape(full)


def solution(mesh):
    spec = P(None, None, None, None, "layer", "foot")
    return jax.shard_map(
        per_device,
        mesh=mesh,
        in_specs=(spec, spec, P(None, "foot"), P(None, "foot")),
        out_specs=(spec, spec),
        check_vma=False,
    )
```

```python
import functools

import jax
import jax.numpy as jnp
import numpy as np
from jax import lax
from jax.experimental import pallas as pl
from jax.experimental.pallas import tpu as pltpu
from jax.sharding import PartitionSpec as P

TIME_STEP = 0.02
SECTION_DECAY = -0.4178904745
SECTION_WEIGHT = 1.720146321549
LIFT = 3.0 * TIME_STEP
FREE_STREAM = (1.0, 0.3, 0.1, 0.0, 1.0 / 0.56 + 0.05)
MESH = pl.DeviceIdType.MESH
SLOTS = 16
BF16 = jnp.bfloat16
F32 = jnp.float32
STEPS = (4, -4, 1, -1)


def derivative_entries():
    nodes = np.array([-1.0, -1.0 / np.sqrt(5.0), 1.0 / np.sqrt(5.0), 1.0])
    products = np.array(
        [np.prod([nodes[t] - nodes[a] for a in range(4) if a != t]) for t in range(4)]
    )
    matrix = np.zeros((4, 4))
    for t in range(4):
        for s in range(4):
            if t != s:
                matrix[t, s] = products[t] / products[s] / (nodes[t] - nodes[s])
            else:
                matrix[t, t] = sum(1.0 / (nodes[t] - nodes[a]) for a in range(4) if a != t)
    return matrix


ENTRIES = -TIME_STEP * derivative_entries()
ODD = [[0.5 * float(ENTRIES[p, i] - ENTRIES[p, 3 - i]) for i in (0, 1)] for p in (0, 1)]
EVEN = [0.5 * float(ENTRIES[p, 0] + ENTRIES[p, 3]) for p in (0, 1)]


def derived(f):
    s0, d0 = f[0] + f[3], f[0] - f[3]
    s1, d1 = f[1] + f[2], f[1] - f[2]
    t = s0 - s1
    a = ODD[0][0] * d0 + ODD[0][1] * d1
    b = EVEN[0] * t
    c = ODD[1][0] * d0 + ODD[1][1] * d1
    e = EVEN[1] * t
    return a + b, c + e, c - e, a - b


def inverse(x):
    r = pl.reciprocal(x, approx=True)
    return r * (2.0 - x * r)


def split(x):
    hi = x.astype(BF16)
    lo = (x - hi.astype(F32)).astype(BF16)
    return hi, lo


def dot(a, b):
    return jnp.dot(a, b, preferred_element_type=F32)


def dot_nt(a, b):
    return lax.dot_general(a, b, (((1,), (1,)), ((), ())), preferred_element_type=F32)


def face_rows(side):
    face = (0, 3)[side % 2]
    return (slice(None), face) if side < 2 else (slice(None), slice(None), face)


def trace_of(cv, side):
    return cv[face_rows(side)].reshape(640, 256)


def primitive(q):
    r = inverse(q[0])
    kinetic = (q[1] * q[1] + q[2] * q[2] + q[3] * q[3]) * r
    pressure = 0.4 * q[4] - 0.2 * kinetic
    square = 1.4 * pressure * r
    return r, pressure, square * lax.rsqrt(square)


def face_change(inner, outer, direction, sign, inner_known=None):
    if inner_known is None:
        r_in, p_in, c_in = primitive(inner)
        v_in = inner[1 + direction] * r_in
    else:
        v_in, p_in, c_in = inner_known
    r_out, p_out, c_out = primitive(outer)
    v_out = outer[1 + direction] * r_out
    lam = LIFT * jnp.maximum(jnp.abs(v_in) + c_in, jnp.abs(v_out) + c_out)
    s_in, s_out = (sign * LIFT) * v_in, (sign * LIFT) * v_out
    w_in, w_out = lam - s_in, lam - s_out
    change = [w_out * outer[v] - w_in * inner[v] for v in range(5)]
    change[1 + direction] = change[1 + direction] - (sign * LIFT) * (p_out - p_in)
    change[4] = change[4] - (p_out * s_out - p_in * s_in)
    return change


def gather_slots(stage, side, lane_z):
    total = stage[side, pl.ds(0, 80, stride=8), :]
    for z in range(1, 8):
        total = jnp.where(lane_z == z, stage[side, pl.ds(z, 80, stride=8), :], total)
    return total


def exchange_kernel(
    cons, reg, nb_in, kinds_in, cv, acc, lateral, vertical, picks,
    nb, kinds, prim, ghost, stage, packed, own, arrived, sendv, recvv, load_sem, send_sem, recv_sem, vsend_sem, vrecv_sem,
):
    foot, layer = lax.axis_index("foot"), lax.axis_index("layer")
    feet, layers = lax.axis_size("foot"), lax.axis_size("layer")

    def at_foot(by):
        return (lax.rem(foot + by + feet, feet), layer)

    def at_layer(by):
        return (foot, lax.rem(layer + by + layers, layers))

    barrier = pltpu.get_barrier_semaphore()
    partners = [at_foot(by) for by in STEPS] + [at_layer(by) for by in (1, -1)]
    for partner in partners:
        pl.semaphore_signal(barrier, inc=1, device_id=partner, device_id_type=MESH)
    maps = [
        pltpu.make_async_copy(nb_in, nb, load_sem.at[6]),
        pltpu.make_async_copy(kinds_in, kinds, load_sem.at[7]),
    ]
    for copy in maps:
        copy.start()
    loads = [pltpu.make_async_copy(cons.at[v], cv.at[v], load_sem.at[v]) for v in range(5)]
    for copy in loads:
        copy.start()
    reg_load = pltpu.make_async_copy(reg, acc, load_sem.at[5])
    reg_load.start()

    slot = lax.bitwise_and(lax.broadcasted_iota(jnp.int32, (128, 256), 0), SLOTS - 1)
    lane_z = lax.broadcasted_iota(jnp.int32, (80, 128), 1) // SLOTS
    rows = lax.broadcasted_iota(jnp.int32, (256, 256), 0)
    cols = lax.broadcasted_iota(jnp.int32, (256, 256), 1)
    before = jnp.where(rows < cols, 1.0, 0.0).astype(BF16)
    for copy in maps:
        copy.wait()
    here = nb[...] - foot * 256
    mask = jnp.where(jnp.logical_or(here < 0, here >= 256), 1.0, 0.0)
    mask8 = jnp.concatenate([mask, jnp.zeros_like(mask)], axis=0).astype(BF16)
    rank = jnp.where(mask8.astype(F32) > 0.5, dot(mask8, before), -1.0).astype(jnp.int32)

    for copy in loads:
        copy.wait()

    for way in (0, 1):
        for h in (0, 1):
            lanes = pl.ds(h * 128, 128)
            stage[2 * way + h] = cv[:, :, :, pl.ds(24 * way, 8), lanes].reshape(640, 128)
            sendv[way, :, lanes] = stage[2 * way + h, pl.ds(7 * way, 80, stride=8), :]
    for side in range(4):
        hi, lo = split(trace_of(cv, side ^ 1))
        pick = jnp.where(rank[(side ^ 1):(side ^ 1) + 1] == slot, 1.0, 0.0).astype(BF16)
        stage[side] = dot_nt(hi, pick) + dot_nt(lo, pick)
        packed[side] = gather_slots(stage, side, lane_z)

    pl.semaphore_wait(barrier, len(partners))
    copies = []
    for side in range(4):
        copies.append(pltpu.make_async_remote_copy(
            src_ref=packed.at[side], dst_ref=arrived.at[side], send_sem=send_sem.at[side],
            recv_sem=recv_sem.at[side], device_id=at_foot(STEPS[side]), device_id_type=MESH,
        ))
    for way in (0, 1):
        copies.append(pltpu.make_async_remote_copy(
            src_ref=sendv.at[way], dst_ref=recvv.at[way], send_sem=vsend_sem.at[way],
            recv_sem=vrecv_sem.at[way], device_id=at_layer((-1, 1)[way]), device_id_type=MESH,
        ))
    for copy in copies:
        copy.start()

    reg_load.wait()

    def z_lines(line, carry):
        i, j = line // 4, line % 4
        q = [[cv[v, i, j, pl.ds(8 * k, 8), :] for k in range(4)] for v in range(5)]
        flux = [[], [], [], [], []]
        for k in range(4):
            rho, mx, my, mz, energy = (q[v][k] for v in range(5))
            r, pressure, sound = primitive([q[v][k] for v in range(5)])
            vz = mz * r
            rows_k = pl.ds(8 * k, 8)
            prim[0, i, j, rows_k, :] = mx * r
            prim[1, i, j, rows_k, :] = my * r
            prim[2, i, j, rows_k, :] = vz
            prim[3, i, j, rows_k, :] = pressure
            prim[4, i, j, rows_k, :] = sound
            flux[0].append(mz)
            flux[1].append(mx * vz)
            flux[2].append(my * vz)
            flux[3].append(mz * vz + pressure)
            flux[4].append((energy + pressure) * vz)
        for v in range(5):
            out = derived(flux[v])
            for k in range(4):
                rows_k = pl.ds(8 * k, 8)
                acc[v, i, j, rows_k, :] = SECTION_DECAY * acc[v, i, j, rows_k, :] + out[k]
        return carry

    lax.fori_loop(0, 16, z_lines, 0)

    def lines(direction, line, carry):
        a, k = line // 4, line % 4
        rows_k = pl.ds(pl.multiple_of(8 * k, 8), 8)

        def at(node):
            return (node, a, rows_k, slice(None)) if direction == 0 else (a, node, rows_k, slice(None))

        flux = [[], [], [], [], []]
        for node in range(4):
            vd = prim[(direction,) + at(node)]
            pressure = prim[(3,) + at(node)]
            m = [cv[(1 + c,) + at(node)] for c in range(3)]
            flux[0].append(m[direction])
            for c in range(3):
                entry = m[c] * vd
                if c == direction:
                    entry = entry + pressure
                flux[1 + c].append(entry)
            flux[4].append((cv[(4,) + at(node)] + pressure) * vd)
        for v in range(5):
            out = derived(flux[v])
            for node in range(4):
                acc[(v,) + at(node)] = acc[(v,) + at(node)] + out[node]
        return carry

    lax.fori_loop(0, 16, functools.partial(lines, 0), 0)
    lax.fori_loop(0, 16, functools.partial(lines, 1), 0)

    kind = kinds[...]
    open_face = kind == 0
    for side in range(4):
        hi, lo = split(trace_of(cv, side ^ 1))
        select = jnp.where(here[side:side + 1] == rows, 1.0, 0.0).astype(BF16)
        ghost[...] = (dot(hi, select) + dot(lo, select)).reshape(5, 4, 32, 256)
        local = jnp.broadcast_to(jnp.where(open_face, 1.0 - mask, 0.0)[side:side + 1], (8, 256)) > 0.5
        far = jnp.broadcast_to(kind[side:side + 1], (8, 256)) == 2
        flip = jnp.broadcast_to(jnp.where(kind == 1, -1.0, 1.0)[side:side + 1], (8, 256))
        d, face, sign = side // 2, (0, 3)[side % 2], (-1.0, 1.0)[side % 2]

        def lateral_nodes(node, carry):
            a, b = node // 4, node % 4
            rows_b = pl.ds(pl.multiple_of(8 * b, 8), 8)
            at = (face, a, rows_b, slice(None)) if d == 0 else (a, face, rows_b, slice(None))
            q = [cv[(v,) + at] for v in range(5)]
            outer = []
            for v in range(5):
                inner = q[v] * flip if v == 1 + d else q[v]
                outer.append(jnp.where(local, ghost[v, a, rows_b, :], jnp.where(far, FREE_STREAM[v], inner)))
            known = prim[(d,) + at], prim[(3,) + at], prim[(4,) + at]
            change = face_change(q, outer, d, sign, known)
            for v in range(5):
                acc[(v,) + at] = acc[(v,) + at] + change[v]
            return carry

        lax.fori_loop(0, 16, lateral_nodes, 0, unroll=2)

        named = lax.bitwise_and(nb[side:side + 1], 255)
        named = jnp.where(mask[side:side + 1] > 0.5, named, -1)
        onehot = jnp.where(rows == named, 1.0, 0.0).astype(BF16)
        hit = dot_nt(jnp.ones((8, 256), BF16), onehot).astype(BF16)
        order = dot(dot(hit, before).astype(BF16), onehot)
        order = jnp.where(jnp.logical_and(open_face, mask > 0.5)[side:side + 1], order[0:1], -1.0)
        pick = jnp.where(order.astype(jnp.int32) == slot, 1.0, 0.0).astype(BF16)
        picks[side] = pick
        hi, lo = split(trace_of(cv, side))
        stage[side] = dot_nt(hi, pick) + dot_nt(lo, pick)
        own[side, 0:80] = gather_slots(stage, side, lane_z)
        own[side, 80:88] = dot_nt(jnp.ones((8, 256), BF16), pick)

    sub = lax.broadcasted_iota(jnp.int32, (8, 256), 0)
    for way in (0, 1):
        rows_here, rows_there = (pl.ds(0, 8), pl.ds(24, 8)) if way == 0 else (pl.ds(24, 8), pl.ds(0, 8))
        shift, edge, sign = (1, 0, -1.0) if way == 0 else (7, 7, 1.0)

        def vertical_nodes(node, carry):
            at = (node // 4, node % 4, rows_here, slice(None))
            there = (node // 4, node % 4, rows_there, slice(None))
            q = [cv[(v,) + at] for v in range(5)]
            outer = [jnp.where(sub == edge, q[v], pltpu.roll(cv[(v,) + there], shift, 0)) for v in range(5)]
            known = prim[(2,) + at], prim[(3,) + at], prim[(4,) + at]
            change = face_change(q, outer, 2, sign, known)
            for v in range(5):
                acc[(v,) + at] = acc[(v,) + at] + change[v]
            return carry

        lax.fori_loop(0, 16, vertical_nodes, 0, unroll=2)

    for copy in copies:
        copy.wait()

    for side in range(4):
        valid = jnp.broadcast_to(own[side, 80:81] > 0.5, (16, 128))
        inner = [jnp.where(valid, own[side, 16 * v:16 * v + 16], FREE_STREAM[v]) for v in range(5)]
        outer = [jnp.where(valid, arrived[side, 16 * v:16 * v + 16], FREE_STREAM[v]) for v in range(5)]
        change = face_change(inner, outer, side // 2, (-1.0, 1.0)[side % 2])
        for v in range(5):
            lateral[side, 16 * v:16 * v + 16] = change[v]
    lowest, highest = layer == 0, layer == layers - 1
    for way in (0, 1):
        inner = [sendv[way, 16 * v:16 * v + 16] for v in range(5)]
        outer = []
        for v in range(5):
            got = recvv[1 - way, 16 * v:16 * v + 16]
            if way == 0:
                outer.append(jnp.where(lowest, -inner[v] if v == 3 else inner[v], got))
            else:
                outer.append(jnp.where(highest, jnp.full_like(got, FREE_STREAM[v]), got))
        change = face_change(inner, outer, 2, (-1.0, 1.0)[way])
        for v in range(5):
            vertical[way, 16 * v:16 * v + 16] = change[v]


def finish_kernel(cv, acc, lateral, vertical, picks, adv, new, adv_v, new_v, add, out_sem):
    lane_z = lax.broadcasted_iota(jnp.int32, (80, 8, 128), 2) // SLOTS
    sub_z = lax.broadcasted_iota(jnp.int32, (80, 8, 128), 1)
    sub = lax.broadcasted_iota(jnp.int32, (8, 256), 0)
    for side in (2, 3, 0, 1):
        spread = jnp.where(lane_z == sub_z, lateral[side][:, None, :], 0.0).reshape(640, 128)
        hi, lo = split(spread)
        both = jnp.concatenate([hi, lo], axis=1)
        twice = jnp.concatenate([picks[side], picks[side]], axis=0)
        add[side] = dot(both, twice).reshape(5, 4, 32, 256)
    outs = []
    for i in (1, 2, 0, 3):
        for v in range(5):
            for j in range(4):
                for k in range(4):
                    rows_k = pl.ds(8 * k, 8)
                    total = acc[v, i, j, rows_k, :]
                    if i in (0, 3):
                        total = total + add[0 if i == 0 else 1, v, j, rows_k, :]
                    if j in (0, 3):
                        total = total + add[2 if j == 0 else 3, v, i, rows_k, :]
                    m = v * 16 + i * 4 + j
                    if k == 0:
                        total = total + jnp.where(sub == 0, vertical[0, m:m + 1, :], 0.0)
                    if k == 3:
                        total = total + jnp.where(sub == 7, vertical[1, m:m + 1, :], 0.0)
                    new_v[v, i, j, rows_k, :] = total
                    adv_v[v, i, j, rows_k, :] = cv[v, i, j, rows_k, :] + SECTION_WEIGHT * total
        for n, (src, dst) in enumerate(((adv_v, adv), (new_v, new))):
            copy = pltpu.make_async_copy(src.at[:, i], dst.at[:, i], out_sem.at[n, i])
            copy.start()
            outs.append(copy)
    for copy in outs:
        copy.wait()


SHAPE = (5, 4, 4, 32, 256)


def per_device(conserved, register, neighbour, side_type):
    inputs = [
        pltpu.with_memory_space_constraint(x, pltpu.HBM)
        for x in (conserved.reshape(SHAPE), register.reshape(SHAPE), neighbour, side_type)
    ]
    handed = pl.pallas_call(
        exchange_kernel,
        name="exchange",
        out_shape=(
            pltpu.VMEM(SHAPE, F32),
            pltpu.VMEM(SHAPE, F32),
            pltpu.VMEM((4, 80, 128), F32),
            pltpu.VMEM((2, 80, 256), F32),
            pltpu.VMEM((4, 128, 256), BF16),
        ),
        in_specs=[pl.BlockSpec(memory_space=pltpu.HBM)] * 4,
        out_specs=tuple([pl.BlockSpec(memory_space=pltpu.VMEM)] * 5),
        scratch_shapes=[
            pltpu.VMEM((4, 256), jnp.int32),
            pltpu.VMEM((4, 256), jnp.int32),
            pltpu.VMEM(SHAPE, F32),
            pltpu.VMEM((5, 4, 32, 256), F32),
            pltpu.VMEM((4, 640, 128), F32),
            pltpu.VMEM((4, 80, 128), F32),
            pltpu.VMEM((4, 88, 128), F32),
            pltpu.VMEM((4, 80, 128), F32),
            pltpu.VMEM((2, 80, 256), F32),
            pltpu.VMEM((2, 80, 256), F32),
            pltpu.SemaphoreType.DMA((8,)),
            pltpu.SemaphoreType.DMA((4,)),
            pltpu.SemaphoreType.DMA((4,)),
            pltpu.SemaphoreType.DMA((2,)),
            pltpu.SemaphoreType.DMA((2,)),
        ],
        compiler_params=pltpu.CompilerParams(
            collective_id=0, has_side_effects=True, vmem_limit_bytes=40 * 1024 * 1024
        ),
    )(*inputs)
    handed = [pltpu.with_memory_space_constraint(x, pltpu.VMEM) for x in handed]
    adv, new = pl.pallas_call(
        finish_kernel,
        name="finish",
        out_shape=(jax.ShapeDtypeStruct(SHAPE, F32), jax.ShapeDtypeStruct(SHAPE, F32)),
        in_specs=[pl.BlockSpec(memory_space=pltpu.VMEM)] * 5,
        out_specs=(pl.BlockSpec(memory_space=pltpu.HBM), pl.BlockSpec(memory_space=pltpu.HBM)),
        scratch_shapes=[
            pltpu.VMEM(SHAPE, F32),
            pltpu.VMEM(SHAPE, F32),
            pltpu.VMEM((4, 5, 4, 32, 256), F32),
            pltpu.SemaphoreType.DMA((2, 4)),
        ],
        compiler_params=pltpu.CompilerParams(vmem_limit_bytes=32 * 1024 * 1024),
    )(*handed)
    full = (5, 4, 4, 4, 8, 256)
    return adv.reshape(full), new.reshape(full)


def solution(mesh):
    spec = P(None, None, None, None, "layer", "foot")
    return jax.shard_map(
        per_device,
        mesh=mesh,
        in_specs=(spec, spec, P(None, "foot"), P(None, "foot")),
        out_specs=(spec, spec),
        check_vma=False,
    )
```

```python
import functools

import jax
import jax.numpy as jnp
import numpy as np
from jax import lax
from jax.experimental import pallas as pl
from jax.experimental.pallas import tpu as pltpu
from jax.sharding import PartitionSpec as P

TIME_STEP = 0.02
SECTION_DECAY = -0.4178904745
SECTION_WEIGHT = 1.720146321549
LIFT = 3.0 * TIME_STEP
FREE_STREAM = (1.0, 0.3, 0.1, 0.0, 1.0 / 0.56 + 0.05)
MESH = pl.DeviceIdType.MESH
SLOTS = 16
BF16 = jnp.bfloat16
F32 = jnp.float32
STEPS = (4, -4, 1, -1)


def derivative_entries():
    nodes = np.array([-1.0, -1.0 / np.sqrt(5.0), 1.0 / np.sqrt(5.0), 1.0])
    products = np.array(
        [np.prod([nodes[t] - nodes[a] for a in range(4) if a != t]) for t in range(4)]
    )
    matrix = np.zeros((4, 4))
    for t in range(4):
        for s in range(4):
            if t != s:
                matrix[t, s] = products[t] / products[s] / (nodes[t] - nodes[s])
            else:
                matrix[t, t] = sum(1.0 / (nodes[t] - nodes[a]) for a in range(4) if a != t)
    return matrix


ENTRIES = -TIME_STEP * derivative_entries()
ODD = [[0.5 * float(ENTRIES[p, i] - ENTRIES[p, 3 - i]) for i in (0, 1)] for p in (0, 1)]
EVEN = [0.5 * float(ENTRIES[p, 0] + ENTRIES[p, 3]) for p in (0, 1)]


def derived(f):
    s0, d0 = f[0] + f[3], f[0] - f[3]
    s1, d1 = f[1] + f[2], f[1] - f[2]
    t = s0 - s1
    a = ODD[0][0] * d0 + ODD[0][1] * d1
    b = EVEN[0] * t
    c = ODD[1][0] * d0 + ODD[1][1] * d1
    e = EVEN[1] * t
    return a + b, c + e, c - e, a - b


def inverse(x):
    r = pl.reciprocal(x, approx=True)
    return r * (2.0 - x * r)


def split(x):
    hi = x.astype(BF16)
    lo = (x - hi.astype(F32)).astype(BF16)
    return hi, lo


def dot(a, b):
    return jnp.dot(a, b, preferred_element_type=F32)


def dot_nt(a, b):
    return lax.dot_general(a, b, (((1,), (1,)), ((), ())), preferred_element_type=F32)


def face_rows(side):
    face = (0, 3)[side % 2]
    return (slice(None), face) if side < 2 else (slice(None), slice(None), face)


def trace_of(cv, side):
    return cv[face_rows(side)].reshape(640, 256)


def primitive(q):
    r = inverse(q[0])
    kinetic = (q[1] * q[1] + q[2] * q[2] + q[3] * q[3]) * r
    pressure = 0.4 * q[4] - 0.2 * kinetic
    square = 1.4 * pressure * r
    return r, pressure, square * lax.rsqrt(square)


def face_change(inner, outer, direction, sign, inner_known=None):
    if inner_known is None:
        r_in, p_in, c_in = primitive(inner)
        v_in = inner[1 + direction] * r_in
    else:
        v_in, p_in, c_in = inner_known
    r_out, p_out, c_out = primitive(outer)
    v_out = outer[1 + direction] * r_out
    lam = LIFT * jnp.maximum(jnp.abs(v_in) + c_in, jnp.abs(v_out) + c_out)
    s_in, s_out = (sign * LIFT) * v_in, (sign * LIFT) * v_out
    w_in, w_out = lam - s_in, lam - s_out
    change = [w_out * outer[v] - w_in * inner[v] for v in range(5)]
    change[1 + direction] = change[1 + direction] - (sign * LIFT) * (p_out - p_in)
    change[4] = change[4] - (p_out * s_out - p_in * s_in)
    return change


def gather_slots(stage, side, lane_z):
    total = stage[side, pl.ds(0, 80, stride=8), :]
    for z in range(1, 8):
        total = jnp.where(lane_z == z, stage[side, pl.ds(z, 80, stride=8), :], total)
    return total


def exchange_kernel(
    cons, reg, nb_in, kinds_in, cv, acc, lateral, vertical, picks,
    nb, kinds, regv, prim, ghost, stage, packed, own, arrived, sendv, recvv, load_sem, send_sem, recv_sem, vsend_sem, vrecv_sem,
):
    foot, layer = lax.axis_index("foot"), lax.axis_index("layer")
    feet, layers = lax.axis_size("foot"), lax.axis_size("layer")

    def at_foot(by):
        return (lax.rem(foot + by + feet, feet), layer)

    def at_layer(by):
        return (foot, lax.rem(layer + by + layers, layers))

    barrier = pltpu.get_barrier_semaphore()
    partners = [at_foot(by) for by in STEPS] + [at_layer(by) for by in (1, -1)]
    for partner in partners:
        pl.semaphore_signal(barrier, inc=1, device_id=partner, device_id_type=MESH)
    maps = [
        pltpu.make_async_copy(nb_in, nb, load_sem.at[6]),
        pltpu.make_async_copy(kinds_in, kinds, load_sem.at[7]),
    ]
    for copy in maps:
        copy.start()
    loads = [pltpu.make_async_copy(cons.at[v], cv.at[v], load_sem.at[v]) for v in range(5)]
    for copy in loads:
        copy.start()
    reg_load = pltpu.make_async_copy(reg, regv, load_sem.at[5])
    reg_load.start()

    slot = lax.bitwise_and(lax.broadcasted_iota(jnp.int32, (128, 256), 0), SLOTS - 1)
    lane_z = lax.broadcasted_iota(jnp.int32, (80, 128), 1) // SLOTS
    rows = lax.broadcasted_iota(jnp.int32, (256, 256), 0)
    cols = lax.broadcasted_iota(jnp.int32, (256, 256), 1)
    before = jnp.where(rows < cols, 1.0, 0.0).astype(BF16)
    for copy in maps:
        copy.wait()
    here = nb[...] - foot * 256
    mask = jnp.where(jnp.logical_or(here < 0, here >= 256), 1.0, 0.0)
    mask8 = jnp.concatenate([mask, jnp.zeros_like(mask)], axis=0).astype(BF16)
    away = mask > 0.5
    rank = jnp.where(away, dot(mask8, before)[0:4], -1.0).astype(jnp.int32)
    names = jnp.where(away, lax.bitwise_and(nb[...], 255), 1000).astype(F32)
    names_down = jnp.transpose(jnp.concatenate([names, names], axis=0))
    kind = kinds[...]
    open_face = kind == 0
    orders = []
    for side in range(4):
        less = jnp.where(names_down[:, side:side + 1] < names[side:side + 1], 1.0, 0.0)
        order = jnp.sum(less, axis=0, keepdims=True)
        orders.append(jnp.where(jnp.logical_and(open_face, away)[side:side + 1], order, -1.0).astype(jnp.int32))

    for copy in loads:
        copy.wait()

    for way in (0, 1):
        for h in (0, 1):
            lanes = pl.ds(h * 128, 128)
            stage[2 * way + h] = cv[:, :, :, pl.ds(24 * way, 8), lanes].reshape(640, 128)
            sendv[way, :, lanes] = stage[2 * way + h, pl.ds(7 * way, 80, stride=8), :]
    for side in range(4):
        hi, lo = split(trace_of(cv, side))
        send = jnp.where(rank[side:side + 1] == slot, 1.0, 0.0).astype(BF16)
        pick = jnp.where(orders[side] == slot, 1.0, 0.0).astype(BF16)
        picks[side] = pick
        both = jnp.concatenate([send, pick], axis=0)
        rows_both = dot_nt(hi, both) + dot_nt(lo, both)
        stage[0] = rows_both[:, :128]
        stage[1] = rows_both[:, 128:]
        packed[side ^ 1] = gather_slots(stage, 0, lane_z)
        own[side, 0:80] = gather_slots(stage, 1, lane_z)
        own[side, 80:88] = dot_nt(jnp.ones((8, 256), BF16), pick)
    def z_lines(line, carry):
        i, j = line // 4, line % 4
        q = [[cv[v, i, j, pl.ds(8 * k, 8), :] for k in range(4)] for v in range(5)]
        flux = [[], [], [], [], []]
        for k in range(4):
            rho, mx, my, mz, energy = (q[v][k] for v in range(5))
            r, pressure, sound = primitive([q[v][k] for v in range(5)])
            vz = mz * r
            rows_k = pl.ds(8 * k, 8)
            prim[0, i, j, rows_k, :] = mx * r
            prim[1, i, j, rows_k, :] = my * r
            prim[2, i, j, rows_k, :] = vz
            prim[3, i, j, rows_k, :] = pressure
            prim[4, i, j, rows_k, :] = sound
            flux[0].append(mz)
            flux[1].append(mx * vz)
            flux[2].append(my * vz)
            flux[3].append(mz * vz + pressure)
            flux[4].append((energy + pressure) * vz)
        for v in range(5):
            out = derived(flux[v])
            for k in range(4):
                rows_k = pl.ds(8 * k, 8)
                acc[v, i, j, rows_k, :] = out[k]
        return carry

    lax.fori_loop(0, 16, z_lines, 0)


    pl.semaphore_wait(barrier, len(partners))
    copies = []
    for side in range(4):
        copies.append(pltpu.make_async_remote_copy(
            src_ref=packed.at[side], dst_ref=arrived.at[side], send_sem=send_sem.at[side],
            recv_sem=recv_sem.at[side], device_id=at_foot(STEPS[side]), device_id_type=MESH,
        ))
    for way in (0, 1):
        copies.append(pltpu.make_async_remote_copy(
            src_ref=sendv.at[way], dst_ref=recvv.at[way], send_sem=vsend_sem.at[way],
            recv_sem=vrecv_sem.at[way], device_id=at_layer((-1, 1)[way]), device_id_type=MESH,
        ))
    for copy in copies:
        copy.start()


    def lines(direction, line, carry):
        a, k = line // 4, line % 4
        rows_k = pl.ds(pl.multiple_of(8 * k, 8), 8)

        def at(node):
            return (node, a, rows_k, slice(None)) if direction == 0 else (a, node, rows_k, slice(None))

        flux = [[], [], [], [], []]
        for node in range(4):
            vd = prim[(direction,) + at(node)]
            pressure = prim[(3,) + at(node)]
            m = [cv[(1 + c,) + at(node)] for c in range(3)]
            flux[0].append(m[direction])
            for c in range(3):
                entry = m[c] * vd
                if c == direction:
                    entry = entry + pressure
                flux[1 + c].append(entry)
            flux[4].append((cv[(4,) + at(node)] + pressure) * vd)
        for v in range(5):
            out = derived(flux[v])
            for node in range(4):
                total = acc[(v,) + at(node)] + out[node]
                if direction == 1:
                    total = total + SECTION_DECAY * regv[(v,) + at(node)]
                acc[(v,) + at(node)] = total
        return carry

    lax.fori_loop(0, 16, functools.partial(lines, 0), 0)
    reg_load.wait()
    lax.fori_loop(0, 16, functools.partial(lines, 1), 0)
    for side in range(4):
        hi, lo = split(trace_of(cv, side ^ 1))
        select = jnp.where(here[side:side + 1] == rows, 1.0, 0.0).astype(BF16)
        ghost[...] = (dot(hi, select) + dot(lo, select)).reshape(5, 4, 32, 256)
        local = jnp.broadcast_to(jnp.where(open_face, 1.0 - mask, 0.0)[side:side + 1], (8, 256)) > 0.5
        far = jnp.broadcast_to(kind[side:side + 1], (8, 256)) == 2
        flip = jnp.broadcast_to(jnp.where(kind == 1, -1.0, 1.0)[side:side + 1], (8, 256))
        d, face, sign = side // 2, (0, 3)[side % 2], (-1.0, 1.0)[side % 2]

        def lateral_nodes(node, carry):
            a, b = node // 4, node % 4
            rows_b = pl.ds(pl.multiple_of(8 * b, 8), 8)
            at = (face, a, rows_b, slice(None)) if d == 0 else (a, face, rows_b, slice(None))
            q = [cv[(v,) + at] for v in range(5)]
            outer = []
            for v in range(5):
                inner = q[v] * flip if v == 1 + d else q[v]
                outer.append(jnp.where(local, ghost[v, a, rows_b, :], jnp.where(far, FREE_STREAM[v], inner)))
            known = prim[(d,) + at], prim[(3,) + at], prim[(4,) + at]
            change = face_change(q, outer, d, sign, known)
            for v in range(5):
                acc[(v,) + at] = acc[(v,) + at] + change[v]
            return carry

        lax.fori_loop(0, 16, lateral_nodes, 0, unroll=4)

    sub = lax.broadcasted_iota(jnp.int32, (8, 256), 0)
    for way in (0, 1):
        rows_here, rows_there = (pl.ds(0, 8), pl.ds(24, 8)) if way == 0 else (pl.ds(24, 8), pl.ds(0, 8))
        shift, edge, sign = (1, 0, -1.0) if way == 0 else (7, 7, 1.0)

        def vertical_nodes(node, carry):
            at = (node // 4, node % 4, rows_here, slice(None))
            there = (node // 4, node % 4, rows_there, slice(None))
            q = [cv[(v,) + at] for v in range(5)]
            outer = [jnp.where(sub == edge, q[v], pltpu.roll(cv[(v,) + there], shift, 0)) for v in range(5)]
            known = prim[(2,) + at], prim[(3,) + at], prim[(4,) + at]
            change = face_change(q, outer, 2, sign, known)
            for v in range(5):
                acc[(v,) + at] = acc[(v,) + at] + change[v]
            return carry

        lax.fori_loop(0, 16, vertical_nodes, 0, unroll=4)

    for copy in copies:
        copy.wait()

    for side in range(4):
        valid = jnp.broadcast_to(own[side, 80:81] > 0.5, (16, 128))
        inner = [jnp.where(valid, own[side, 16 * v:16 * v + 16], FREE_STREAM[v]) for v in range(5)]
        outer = [jnp.where(valid, arrived[side, 16 * v:16 * v + 16], FREE_STREAM[v]) for v in range(5)]
        change = face_change(inner, outer, side // 2, (-1.0, 1.0)[side % 2])
        for v in range(5):
            lateral[side, 16 * v:16 * v + 16] = change[v]
    lowest, highest = layer == 0, layer == layers - 1
    for way in (0, 1):
        inner = [sendv[way, 16 * v:16 * v + 16] for v in range(5)]
        outer = []
        for v in range(5):
            got = recvv[1 - way, 16 * v:16 * v + 16]
            if way == 0:
                outer.append(jnp.where(lowest, -inner[v] if v == 3 else inner[v], got))
            else:
                outer.append(jnp.where(highest, jnp.full_like(got, FREE_STREAM[v]), got))
        change = face_change(inner, outer, 2, (-1.0, 1.0)[way])
        for v in range(5):
            vertical[way, 16 * v:16 * v + 16] = change[v]
def finish_kernel(cv, acc, lateral, vertical, picks, adv, new, adv_v, new_v, add, out_sem):
    lane_z = lax.broadcasted_iota(jnp.int32, (80, 8, 128), 2) // SLOTS
    sub_z = lax.broadcasted_iota(jnp.int32, (80, 8, 128), 1)
    sub = lax.broadcasted_iota(jnp.int32, (8, 256), 0)
    def unpack(side):
        spread = jnp.where(lane_z == sub_z, lateral[side][:, None, :], 0.0).reshape(640, 128)
        hi, lo = split(spread)
        both = jnp.concatenate([hi, lo], axis=1)
        twice = jnp.concatenate([picks[side], picks[side]], axis=0)
        add[side] = dot(both, twice).reshape(5, 4, 32, 256)

    outs = []
    unpack(2)
    unpack(3)
    for i in (1, 2, 0, 3):
        if i in (0, 3):
            unpack(0 if i == 0 else 1)
        for v in range(5):
            for j in range(4):
                for k in range(4):
                    rows_k = pl.ds(8 * k, 8)
                    total = acc[v, i, j, rows_k, :]
                    if i in (0, 3):
                        total = total + add[0 if i == 0 else 1, v, j, rows_k, :]
                    if j in (0, 3):
                        total = total + add[2 if j == 0 else 3, v, i, rows_k, :]
                    m = v * 16 + i * 4 + j
                    if k == 0:
                        total = total + jnp.where(sub == 0, vertical[0, m:m + 1, :], 0.0)
                    if k == 3:
                        total = total + jnp.where(sub == 7, vertical[1, m:m + 1, :], 0.0)
                    new_v[v, i, j, rows_k, :] = total
                    adv_v[v, i, j, rows_k, :] = cv[v, i, j, rows_k, :] + SECTION_WEIGHT * total
        for n, (src, dst) in enumerate(((adv_v, adv), (new_v, new))):
            copy = pltpu.make_async_copy(src.at[:, i], dst.at[:, i], out_sem.at[n, i])
            copy.start()
            outs.append(copy)
    for copy in outs:
        copy.wait()


SHAPE = (5, 4, 4, 32, 256)


def per_device(conserved, register, neighbour, side_type):
    inputs = [
        pltpu.with_memory_space_constraint(x, pltpu.HBM)
        for x in (conserved.reshape(SHAPE), register.reshape(SHAPE), neighbour, side_type)
    ]
    handed = pl.pallas_call(
        exchange_kernel,
        name="exchange",
        out_shape=(
            pltpu.VMEM(SHAPE, F32),
            pltpu.VMEM(SHAPE, F32),
            pltpu.VMEM((4, 80, 128), F32),
            pltpu.VMEM((2, 80, 256), F32),
            pltpu.VMEM((4, 128, 256), BF16),
        ),
        in_specs=[pl.BlockSpec(memory_space=pltpu.HBM)] * 4,
        out_specs=tuple([pl.BlockSpec(memory_space=pltpu.VMEM)] * 5),
        scratch_shapes=[
            pltpu.VMEM((4, 256), jnp.int32),
            pltpu.VMEM((4, 256), jnp.int32),
            pltpu.VMEM(SHAPE, F32),
            pltpu.VMEM(SHAPE, F32),
            pltpu.VMEM((5, 4, 32, 256), F32),
            pltpu.VMEM((4, 640, 128), F32),
            pltpu.VMEM((4, 80, 128), F32),
            pltpu.VMEM((4, 88, 128), F32),
            pltpu.VMEM((4, 80, 128), F32),
            pltpu.VMEM((2, 80, 256), F32),
            pltpu.VMEM((2, 80, 256), F32),
            pltpu.SemaphoreType.DMA((8,)),
            pltpu.SemaphoreType.DMA((4,)),
            pltpu.SemaphoreType.DMA((4,)),
            pltpu.SemaphoreType.DMA((2,)),
            pltpu.SemaphoreType.DMA((2,)),
        ],
        compiler_params=pltpu.CompilerParams(
            collective_id=0, has_side_effects=True, vmem_limit_bytes=40 * 1024 * 1024
        ),
    )(*inputs)
    handed = [pltpu.with_memory_space_constraint(x, pltpu.VMEM) for x in handed]
    adv, new = pl.pallas_call(
        finish_kernel,
        name="finish",
        out_shape=(jax.ShapeDtypeStruct(SHAPE, F32), jax.ShapeDtypeStruct(SHAPE, F32)),
        in_specs=[pl.BlockSpec(memory_space=pltpu.VMEM)] * 5,
        out_specs=(pl.BlockSpec(memory_space=pltpu.HBM), pl.BlockSpec(memory_space=pltpu.HBM)),
        scratch_shapes=[
            pltpu.VMEM(SHAPE, F32),
            pltpu.VMEM(SHAPE, F32),
            pltpu.VMEM((4, 5, 4, 32, 256), F32),
            pltpu.SemaphoreType.DMA((2, 4)),
        ],
        compiler_params=pltpu.CompilerParams(vmem_limit_bytes=32 * 1024 * 1024),
    )(*handed)
    full = (5, 4, 4, 4, 8, 256)
    return adv.reshape(full), new.reshape(full)


def solution(mesh):
    spec = P(None, None, None, None, "layer", "foot")
    return jax.shard_map(
        per_device,
        mesh=mesh,
        in_specs=(spec, spec, P(None, "foot"), P(None, "foot")),
        out_specs=(spec, spec),
        check_vma=False,
    )
```

```python
import functools

import jax
import jax.numpy as jnp
import numpy as np
from jax import lax
from jax.experimental import pallas as pl
from jax.experimental.pallas import tpu as pltpu
from jax.sharding import PartitionSpec as P

TIME_STEP = 0.02
SECTION_DECAY = -0.4178904745
SECTION_WEIGHT = 1.720146321549
LIFT = 3.0 * TIME_STEP
FREE_STREAM = (1.0, 0.3, 0.1, 0.0, 1.0 / 0.56 + 0.05)
MESH = pl.DeviceIdType.MESH
SLOTS = 16
BF16 = jnp.bfloat16
F32 = jnp.float32
TILES_Y = 4


def derivative_entries():
    nodes = np.array([-1.0, -1.0 / np.sqrt(5.0), 1.0 / np.sqrt(5.0), 1.0])
    products = np.array(
        [np.prod([nodes[t] - nodes[a] for a in range(4) if a != t]) for t in range(4)]
    )
    matrix = np.zeros((4, 4))
    for t in range(4):
        for s in range(4):
            if t != s:
                matrix[t, s] = products[t] / products[s] / (nodes[t] - nodes[s])
            else:
                matrix[t, t] = sum(1.0 / (nodes[t] - nodes[a]) for a in range(4) if a != t)
    return matrix


ENTRIES = -TIME_STEP * derivative_entries()
ODD = [[0.5 * float(ENTRIES[p, i] - ENTRIES[p, 3 - i]) for i in (0, 1)] for p in (0, 1)]
EVEN = [0.5 * float(ENTRIES[p, 0] + ENTRIES[p, 3]) for p in (0, 1)]


def derived(f):
    s0, d0 = f[0] + f[3], f[0] - f[3]
    s1, d1 = f[1] + f[2], f[1] - f[2]
    t = s0 - s1
    a = ODD[0][0] * d0 + ODD[0][1] * d1
    b = EVEN[0] * t
    c = ODD[1][0] * d0 + ODD[1][1] * d1
    e = EVEN[1] * t
    return a + b, c + e, c - e, a - b


def inverse(x):
    r = pl.reciprocal(x, approx=True)
    return r * (2.0 - x * r)


def split(x):
    hi = x.astype(BF16)
    lo = (x - hi.astype(F32)).astype(BF16)
    return hi, lo


def dot(a, b):
    return jnp.dot(a, b, preferred_element_type=F32)


def dot_nt(a, b):
    return lax.dot_general(a, b, (((1,), (1,)), ((), ())), preferred_element_type=F32)


def face_rows(side):
    face = (0, 3)[side % 2]
    return (slice(None), face) if side < 2 else (slice(None), slice(None), face)


def trace_of(cv, side):
    return cv[face_rows(side)].reshape(640, 256)


def primitive(q):
    r = inverse(q[0])
    kinetic = (q[1] * q[1] + q[2] * q[2] + q[3] * q[3]) * r
    pressure = 0.4 * q[4] - 0.2 * kinetic
    square = 1.4 * pressure * r
    return r, pressure, square * lax.rsqrt(square)


def gather_slots(stage, side, lane_z):
    total = stage[side, pl.ds(0, 80, stride=8), :]
    for z in range(1, 8):
        total = jnp.where(lane_z == z, stage[side, pl.ds(z, 80, stride=8), :], total)
    return total


def exchange_kernel(
    cons, reg, nb_in, cv, acc, ghost, vert,
    nb, regv, prim, halves, picks, stage, packed, arrived, sendv, recvv,
    load_sem, send_sem, recv_sem, vsend_sem, vrecv_sem,
):
    foot, layer = lax.axis_index("foot"), lax.axis_index("layer")
    layers = lax.axis_size("layer")
    along, across = foot // TILES_Y, lax.rem(foot, TILES_Y)
    tiles = lax.axis_size("foot") // TILES_Y

    lower, upper = along > 0, along < tiles - 1
    left, right = across > 0, across < TILES_Y - 1
    below, above = layer > 0, layer < layers - 1
    sends = [
        ((foot + TILES_Y, layer), upper, lower),
        ((foot - TILES_Y, layer), lower, upper),
        ((foot + 1, layer), right, left),
        ((foot - 1, layer), left, right),
        ((foot, layer - 1), below, above),
        ((foot, layer + 1), above, below),
    ]

    barrier = pltpu.get_barrier_semaphore()
    partners = jnp.int32(0)
    for partner, there, _ in sends:
        partners = partners + there.astype(jnp.int32)

        @pl.when(there)
        def _():
            pl.semaphore_signal(barrier, inc=1, device_id=partner, device_id_type=MESH)

    nb_load = pltpu.make_async_copy(nb_in, nb, load_sem.at[6])
    nb_load.start()
    loads = [pltpu.make_async_copy(cons.at[v], cv.at[v], load_sem.at[v]) for v in range(5)]
    for copy in loads:
        copy.start()
    reg_load = pltpu.make_async_copy(reg, regv, load_sem.at[5])
    reg_load.start()

    slot = lax.bitwise_and(lax.broadcasted_iota(jnp.int32, (128, 256), 0), SLOTS - 1)
    lane_z = lax.broadcasted_iota(jnp.int32, (80, 128), 1) // SLOTS
    rows = lax.broadcasted_iota(jnp.int32, (256, 256), 0)
    cols = lax.broadcasted_iota(jnp.int32, (256, 256), 1)
    before = jnp.where(rows < cols, 1.0, 0.0).astype(BF16)
    nb_load.wait()
    here = nb[...] - foot * 256
    away = jnp.logical_or(here < 0, here >= 256)
    mask = jnp.where(away, 1.0, 0.0)
    mask8 = jnp.concatenate([mask, jnp.zeros_like(mask)], axis=0).astype(BF16)
    rank = jnp.where(away, dot(mask8, before)[0:4], -1.0).astype(jnp.int32)

    for copy in loads:
        copy.wait()

    for way in (0, 1):
        for h in (0, 1):
            lanes = pl.ds(h * 128, 128)
            stage[2 * way + h] = cv[:, :, :, pl.ds(24 * way, 8), lanes].reshape(640, 128)
            sendv[way, :, lanes] = stage[2 * way + h, pl.ds(7 * way, 80, stride=8), :]
    for side in range(4):
        hi, lo = split(trace_of(cv, side))
        halves[side, :, 0:256] = hi
        halves[side, :, 256:512] = lo
        send = jnp.where(rank[side:side + 1] == slot, 1.0, 0.0).astype(BF16)
        stage[side] = dot_nt(hi, send) + dot_nt(lo, send)
        packed[side ^ 1] = gather_slots(stage, side, lane_z)

    pl.semaphore_wait(barrier, partners)
    copies = []
    for side in range(4):
        copies.append(pltpu.make_async_remote_copy(
            src_ref=packed.at[side], dst_ref=arrived.at[side], send_sem=send_sem.at[side],
            recv_sem=recv_sem.at[side], device_id=sends[side][0], device_id_type=MESH,
        ))
    for way in (0, 1):
        copies.append(pltpu.make_async_remote_copy(
            src_ref=sendv.at[way], dst_ref=recvv.at[way], send_sem=vsend_sem.at[way],
            recv_sem=vrecv_sem.at[way], device_id=sends[4 + way][0], device_id_type=MESH,
        ))
    for copy, (_, there, _) in zip(copies, sends):

        @pl.when(there)
        def _():
            copy.start()

    def z_lines(line, carry):
        i, j = line // 4, line % 4
        q = [[cv[v, i, j, pl.ds(8 * k, 8), :] for k in range(4)] for v in range(5)]
        flux = [[], [], [], [], []]
        for k in range(4):
            rho, mx, my, mz, energy = (q[v][k] for v in range(5))
            r = inverse(rho)
            pressure = 0.4 * energy - 0.2 * ((mx * mx + my * my + mz * mz) * r)
            vz = mz * r
            rows_k = pl.ds(8 * k, 8)
            prim[0, i, j, rows_k, :] = mx * r
            prim[1, i, j, rows_k, :] = my * r
            prim[2, i, j, rows_k, :] = pressure
            flux[0].append(mz)
            flux[1].append(mx * vz)
            flux[2].append(my * vz)
            flux[3].append(mz * vz + pressure)
            flux[4].append((energy + pressure) * vz)
        for v in range(5):
            out = derived(flux[v])
            for k in range(4):
                rows_k = pl.ds(8 * k, 8)
                acc[v, i, j, rows_k, :] = out[k]
        return carry

    lax.fori_loop(0, 16, z_lines, 0)


    def lines(direction, line, carry):
        a, k = line // 4, line % 4
        rows_k = pl.ds(pl.multiple_of(8 * k, 8), 8)

        def at(node):
            return (node, a, rows_k, slice(None)) if direction == 0 else (a, node, rows_k, slice(None))

        flux = [[], [], [], [], []]
        for node in range(4):
            vd = prim[(direction,) + at(node)]
            pressure = prim[(2,) + at(node)]
            m = [cv[(1 + c,) + at(node)] for c in range(3)]
            flux[0].append(m[direction])
            for c in range(3):
                entry = m[c] * vd
                if c == direction:
                    entry = entry + pressure
                flux[1 + c].append(entry)
            flux[4].append((cv[(4,) + at(node)] + pressure) * vd)
        for v in range(5):
            out = derived(flux[v])
            for node in range(4):
                total = acc[(v,) + at(node)] + out[node]
                if direction == 1:
                    total = total + SECTION_DECAY * regv[(v,) + at(node)]
                acc[(v,) + at(node)] = total
        return carry

    lax.fori_loop(0, 16, functools.partial(lines, 0), 0)
    reg_load.wait()
    lax.fori_loop(0, 16, functools.partial(lines, 1), 0)

    names = jnp.where(away, lax.bitwise_and(nb[...], 255), 1000).astype(F32)
    names_down = jnp.transpose(jnp.concatenate([names, names], axis=0))
    for side in range(4):
        less = jnp.where(names_down[:, side:side + 1] < names[side:side + 1], 1.0, 0.0)
        order = jnp.sum(less, axis=0, keepdims=True)
        order = jnp.where(away[side:side + 1], order, -1.0).astype(jnp.int32)
        picks[side] = jnp.where(order == slot, 1.0, 0.0).astype(BF16)

    lane_z3 = lax.broadcasted_iota(jnp.int32, (80, 8, 128), 2) // SLOTS
    sub_z3 = lax.broadcasted_iota(jnp.int32, (80, 8, 128), 1)
    for side in range(4):
        _, there, comes = sends[side]

        @pl.when(there)
        def _():
            copies[side].wait_send()

        @pl.when(comes)
        def _():
            copies[side].wait_recv()

        @pl.when(jnp.logical_not(comes))
        def _():
            arrived[side] = jnp.zeros((80, 128), F32)

        spread = jnp.where(lane_z3 == sub_z3, arrived[side][:, None, :], 0.0).reshape(640, 128)
        far_hi, far_lo = split(spread)
        select = jnp.where(here[side:side + 1] == rows, 1.0, 0.0).astype(BF16)
        left_side = jnp.concatenate([halves[side ^ 1], far_hi, far_lo], axis=1)
        right_side = jnp.concatenate([select, select, picks[side], picks[side]], axis=0)
        ghost[side] = dot(left_side, right_side).reshape(5, 4, 32, 256)

    for way in (0, 1):
        _, there, comes = sends[4 + way]

        @pl.when(there)
        def _():
            copies[4 + way].wait_send()

        @pl.when(comes)
        def _():
            copies[4 + way].wait_recv()

        @pl.when(jnp.logical_not(comes))
        def _():
            recvv[way] = jnp.zeros((80, 256), F32)

    for v in range(5):
        part = pl.ds(16 * v, 16)
        own = sendv[0, part, :]
        vert[0, part, :] = jnp.where(below, recvv[1, part, :], -own if v == 3 else own)
        vert[1, part, :] = jnp.where(above, recvv[0, part, :], jnp.full_like(own, FREE_STREAM[v]))


def surface_kernel(cv, acc, ghost, vert, kinds, adv, new, adv_v, new_v, out_sem):
    sub = lax.broadcasted_iota(jnp.int32, (8, 128), 0)
    outs = []
    for i in range(4):

        def half(h, carry):
            lanes = pl.ds(pl.multiple_of(h * 128, 128), 128)
            kind = [jnp.broadcast_to(kinds[s:s + 1, lanes], (8, 128)) for s in range(4)]
            open_face = [kind[s] == 0 for s in range(4)]
            wall = [kind[s] == 1 for s in range(4)]
            for j in range(4):
                for k in range(4):
                    rows_k = pl.ds(8 * k, 8)
                    q = [cv[v, i, j, rows_k, lanes] for v in range(5)]
                    total = [acc[v, i, j, rows_k, lanes] for v in range(5)]
                    faces = []
                    if i in (0, 3):
                        faces.append((0, 0 if i == 0 else 1, (j, k)))
                    if j in (0, 3):
                        faces.append((1, 2 if j == 0 else 3, (i, k)))
                    if k in (0, 3):
                        faces.append((2, 4 if k == 0 else 5, (i, j)))
                    if faces:
                        r_in, p_in, c_in = primitive(q)
                    for d, side, (a, b) in faces:
                        if side < 4:
                            outer = []
                            for v in range(5):
                                inner = -q[v] if v == 1 + d else q[v]
                                other = jnp.where(wall[side], inner, FREE_STREAM[v])
                                got = ghost[side, v, a, pl.ds(8 * b, 8), lanes]
                                outer.append(jnp.where(open_face[side], got, other))
                        else:
                            outer = []
                            for v in range(5):
                                m = v * 16 + a * 4 + b
                                if side == 4:
                                    near = cv[v, i, j, pl.ds(24, 8), lanes]
                                    near = pltpu.roll(near, 1, 0)
                                    edge = jnp.broadcast_to(vert[0, m:m + 1, lanes], (8, 128))
                                    outer.append(jnp.where(sub == 0, edge, near))
                                else:
                                    near = cv[v, i, j, pl.ds(0, 8), lanes]
                                    near = pltpu.roll(near, 7, 0)
                                    edge = jnp.broadcast_to(vert[1, m:m + 1, lanes], (8, 128))
                                    outer.append(jnp.where(sub == 7, edge, near))
                        sign = -1.0 if side % 2 == 0 else 1.0
                        r_out, p_out, c_out = primitive(outer)
                        v_in, v_out = q[1 + d] * r_in, outer[1 + d] * r_out
                        lam = LIFT * jnp.maximum(jnp.abs(v_in) + c_in, jnp.abs(v_out) + c_out)
                        s_in, s_out = (sign * LIFT) * v_in, (sign * LIFT) * v_out
                        w_in, w_out = lam - s_in, lam - s_out
                        for v in range(5):
                            total[v] = total[v] + (w_out * outer[v] - w_in * q[v])
                        total[1 + d] = total[1 + d] - (sign * LIFT) * (p_out - p_in)
                        total[4] = total[4] - (p_out * s_out - p_in * s_in)
                    for v in range(5):
                        new_v[v, i, j, rows_k, lanes] = total[v]
                        adv_v[v, i, j, rows_k, lanes] = q[v] + SECTION_WEIGHT * total[v]
            return carry

        lax.fori_loop(0, 2, half, 0)
        for n, (src, dst) in enumerate(((adv_v, adv), (new_v, new))):
            copy = pltpu.make_async_copy(src.at[:, i], dst.at[:, i], out_sem.at[n, i])
            copy.start()
            outs.append(copy)
    for copy in outs:
        copy.wait()


SHAPE = (5, 4, 4, 32, 256)


def per_device(conserved, register, neighbour, side_type):
    inputs = [
        pltpu.with_memory_space_constraint(x, pltpu.HBM)
        for x in (conserved.reshape(SHAPE), register.reshape(SHAPE), neighbour)
    ]
    handed = pl.pallas_call(
        exchange_kernel,
        name="exchange",
        out_shape=(
            pltpu.VMEM(SHAPE, F32),
            pltpu.VMEM(SHAPE, F32),
            pltpu.VMEM((4, 5, 4, 32, 256), F32),
            pltpu.VMEM((2, 80, 256), F32),
        ),
        in_specs=[pl.BlockSpec(memory_space=pltpu.HBM)] * 3,
        out_specs=tuple([pl.BlockSpec(memory_space=pltpu.VMEM)] * 4),
        scratch_shapes=[
            pltpu.VMEM((4, 256), jnp.int32),
            pltpu.VMEM(SHAPE, F32),
            pltpu.VMEM((3, 4, 4, 32, 256), F32),
            pltpu.VMEM((4, 640, 512), BF16),
            pltpu.VMEM((4, 128, 256), BF16),
            pltpu.VMEM((4, 640, 128), F32),
            pltpu.VMEM((4, 80, 128), F32),
            pltpu.VMEM((4, 80, 128), F32),
            pltpu.VMEM((2, 80, 256), F32),
            pltpu.VMEM((2, 80, 256), F32),
            pltpu.SemaphoreType.DMA((7,)),
            pltpu.SemaphoreType.DMA((4,)),
            pltpu.SemaphoreType.DMA((4,)),
            pltpu.SemaphoreType.DMA((2,)),
            pltpu.SemaphoreType.DMA((2,)),
        ],
        compiler_params=pltpu.CompilerParams(
            collective_id=0, has_side_effects=True, vmem_limit_bytes=40 * 1024 * 1024
        ),
    )(*inputs)
    handed = [pltpu.with_memory_space_constraint(x, pltpu.VMEM) for x in handed]
    adv, new = pl.pallas_call(
        surface_kernel,
        name="surface",
        out_shape=(jax.ShapeDtypeStruct(SHAPE, F32), jax.ShapeDtypeStruct(SHAPE, F32)),
        in_specs=[pl.BlockSpec(memory_space=pltpu.VMEM)] * 5,
        out_specs=(pl.BlockSpec(memory_space=pltpu.HBM), pl.BlockSpec(memory_space=pltpu.HBM)),
        scratch_shapes=[
            pltpu.VMEM(SHAPE, F32),
            pltpu.VMEM(SHAPE, F32),
            pltpu.SemaphoreType.DMA((2, 4)),
        ],
        compiler_params=pltpu.CompilerParams(vmem_limit_bytes=32 * 1024 * 1024),
    )(*handed, side_type)
    full = (5, 4, 4, 4, 8, 256)
    return adv.reshape(full), new.reshape(full)


def solution(mesh):
    spec = P(None, None, None, None, "layer", "foot")
    return jax.shard_map(
        per_device,
        mesh=mesh,
        in_specs=(spec, spec, P(None, "foot"), P(None, "foot")),
        out_specs=(spec, spec),
        check_vma=False,
    )
```

```python
import functools

import jax
import jax.numpy as jnp
import numpy as np
from jax import lax
from jax.experimental import pallas as pl
from jax.experimental.pallas import tpu as pltpu
from jax.sharding import PartitionSpec as P

TIME_STEP = 0.02
SECTION_DECAY = -0.4178904745
SECTION_WEIGHT = 1.720146321549
LIFT = 3.0 * TIME_STEP
FREE_STREAM = (1.0, 0.3, 0.1, 0.0, 1.0 / 0.56 + 0.05)
MESH = pl.DeviceIdType.MESH
SLOTS = 16
BF16 = jnp.bfloat16
F32 = jnp.float32
TILES_Y = 4


def derivative_entries():
    nodes = np.array([-1.0, -1.0 / np.sqrt(5.0), 1.0 / np.sqrt(5.0), 1.0])
    products = np.array(
        [np.prod([nodes[t] - nodes[a] for a in range(4) if a != t]) for t in range(4)]
    )
    matrix = np.zeros((4, 4))
    for t in range(4):
        for s in range(4):
            if t != s:
                matrix[t, s] = products[t] / products[s] / (nodes[t] - nodes[s])
            else:
                matrix[t, t] = sum(1.0 / (nodes[t] - nodes[a]) for a in range(4) if a != t)
    return matrix


ENTRIES = -TIME_STEP * derivative_entries()
ODD = [[0.5 * float(ENTRIES[p, i] - ENTRIES[p, 3 - i]) for i in (0, 1)] for p in (0, 1)]
EVEN = [0.5 * float(ENTRIES[p, 0] + ENTRIES[p, 3]) for p in (0, 1)]


def derived(f):
    s0, d0 = f[0] + f[3], f[0] - f[3]
    s1, d1 = f[1] + f[2], f[1] - f[2]
    t = s0 - s1
    a = ODD[0][0] * d0 + ODD[0][1] * d1
    b = EVEN[0] * t
    c = ODD[1][0] * d0 + ODD[1][1] * d1
    e = EVEN[1] * t
    return a + b, c + e, c - e, a - b


def inverse(x):
    r = pl.reciprocal(x, approx=True)
    return r * (2.0 - x * r)


def split(x):
    hi = x.astype(BF16)
    lo = (x - hi.astype(F32)).astype(BF16)
    return hi, lo


def dot(a, b):
    return jnp.dot(a, b, preferred_element_type=F32)


def dot_nt(a, b):
    return lax.dot_general(a, b, (((1,), (1,)), ((), ())), preferred_element_type=F32)


def face_rows(side):
    face = (0, 3)[side % 2]
    return (slice(None), face) if side < 2 else (slice(None), slice(None), face)


def trace_of(cv, side):
    return cv[face_rows(side)].reshape(640, 256)


def primitive(q):
    r = inverse(q[0])
    kinetic = (q[1] * q[1] + q[2] * q[2] + q[3] * q[3]) * r
    pressure = 0.4 * q[4] - 0.2 * kinetic
    square = 1.4 * pressure * r
    return r, pressure, square * lax.rsqrt(square)


def gather_slots(stage, side, lane_z):
    total = stage[side, pl.ds(0, 80, stride=8), :]
    for z in range(1, 8):
        total = jnp.where(lane_z == z, stage[side, pl.ds(z, 80, stride=8), :], total)
    return total


def exchange_kernel(
    cons, reg, nb_in, cv, acc, ghost, vert, prim,
    nb, regv, picks, stage, packed, arrived, sendv, recvv,
    load_sem, send_sem, recv_sem, vsend_sem, vrecv_sem,
):
    foot, layer = lax.axis_index("foot"), lax.axis_index("layer")
    layers = lax.axis_size("layer")
    along, across = foot // TILES_Y, lax.rem(foot, TILES_Y)
    tiles = lax.axis_size("foot") // TILES_Y

    lower, upper = along > 0, along < tiles - 1
    left, right = across > 0, across < TILES_Y - 1
    below, above = layer > 0, layer < layers - 1
    sends = [
        ((foot + TILES_Y, layer), upper, lower),
        ((foot - TILES_Y, layer), lower, upper),
        ((foot + 1, layer), right, left),
        ((foot - 1, layer), left, right),
        ((foot, layer - 1), below, above),
        ((foot, layer + 1), above, below),
    ]

    barrier = pltpu.get_barrier_semaphore()
    partners = jnp.int32(0)
    for partner, there, _ in sends:
        partners = partners + there.astype(jnp.int32)

        @pl.when(there)
        def _():
            pl.semaphore_signal(barrier, inc=1, device_id=partner, device_id_type=MESH)

    nb_load = pltpu.make_async_copy(nb_in, nb, load_sem.at[6])
    nb_load.start()
    loads = [pltpu.make_async_copy(cons.at[v], cv.at[v], load_sem.at[v]) for v in range(5)]
    for copy in loads:
        copy.start()
    reg_load = pltpu.make_async_copy(reg, regv, load_sem.at[5])

    slot = lax.bitwise_and(lax.broadcasted_iota(jnp.int32, (128, 256), 0), SLOTS - 1)
    lane_z = lax.broadcasted_iota(jnp.int32, (80, 128), 1) // SLOTS
    rows = lax.broadcasted_iota(jnp.int32, (256, 256), 0)
    cols = lax.broadcasted_iota(jnp.int32, (256, 256), 1)
    before = jnp.where(rows < cols, 1.0, 0.0).astype(BF16)
    nb_load.wait()
    here = nb[...] - foot * 256
    away = jnp.logical_or(here < 0, here >= 256)
    mask = jnp.where(away, 1.0, 0.0)
    mask8 = jnp.concatenate([mask, jnp.zeros_like(mask)], axis=0).astype(BF16)
    rank = jnp.where(away, dot(mask8, before)[0:4], -1.0).astype(jnp.int32)

    for copy in loads:
        copy.wait()
    reg_load.start()

    for way in (0, 1):
        for h in (0, 1):
            lanes = pl.ds(h * 128, 128)
            stage[2 * way + h] = cv[:, :, :, pl.ds(24 * way, 8), lanes].reshape(640, 128)
            sendv[way, :, lanes] = stage[2 * way + h, pl.ds(7 * way, 80, stride=8), :]
    for side in range(4):
        hi, lo = split(trace_of(cv, side))
        send = jnp.where(rank[side:side + 1] == slot, 1.0, 0.0).astype(BF16)
        stage[side] = dot_nt(hi, send) + dot_nt(lo, send)
        packed[side ^ 1] = gather_slots(stage, side, lane_z)

    pl.semaphore_wait(barrier, partners)
    copies = []
    for side in range(4):
        copies.append(pltpu.make_async_remote_copy(
            src_ref=packed.at[side], dst_ref=arrived.at[side], send_sem=send_sem.at[side],
            recv_sem=recv_sem.at[side], device_id=sends[side][0], device_id_type=MESH,
        ))
    for way in (0, 1):
        copies.append(pltpu.make_async_remote_copy(
            src_ref=sendv.at[way], dst_ref=recvv.at[way], send_sem=vsend_sem.at[way],
            recv_sem=vrecv_sem.at[way], device_id=sends[4 + way][0], device_id_type=MESH,
        ))
    for copy, (_, there, _) in zip(copies, sends):

        @pl.when(there)
        def _():
            copy.start()

    def z_lines(line, carry):
        i, j = line // 4, line % 4
        q = [[cv[v, i, j, pl.ds(8 * k, 8), :] for k in range(4)] for v in range(5)]
        flux = [[], [], [], [], []]
        for k in range(4):
            rho, mx, my, mz, energy = (q[v][k] for v in range(5))
            r, pressure, sound = primitive([q[v][k] for v in range(5)])
            vz = mz * r
            rows_k = pl.ds(8 * k, 8)
            prim[0, i, j, rows_k, :] = mx * r
            prim[1, i, j, rows_k, :] = my * r
            prim[2, i, j, rows_k, :] = vz
            prim[3, i, j, rows_k, :] = pressure
            prim[4, i, j, rows_k, :] = sound
            flux[0].append(mz)
            flux[1].append(mx * vz)
            flux[2].append(my * vz)
            flux[3].append(mz * vz + pressure)
            flux[4].append((energy + pressure) * vz)
        for v in range(5):
            out = derived(flux[v])
            for k in range(4):
                rows_k = pl.ds(8 * k, 8)
                acc[v, i, j, rows_k, :] = out[k]
        return carry

    lax.fori_loop(0, 16, z_lines, 0)


    def lines(direction, line, carry):
        a, k = line // 4, line % 4
        rows_k = pl.ds(pl.multiple_of(8 * k, 8), 8)

        def at(node):
            return (node, a, rows_k, slice(None)) if direction == 0 else (a, node, rows_k, slice(None))

        flux = [[], [], [], [], []]
        for node in range(4):
            vd = prim[(direction,) + at(node)]
            pressure = prim[(3,) + at(node)]
            m = [cv[(1 + c,) + at(node)] for c in range(3)]
            flux[0].append(m[direction])
            for c in range(3):
                entry = m[c] * vd
                if c == direction:
                    entry = entry + pressure
                flux[1 + c].append(entry)
            flux[4].append((cv[(4,) + at(node)] + pressure) * vd)
        for v in range(5):
            out = derived(flux[v])
            for node in range(4):
                total = acc[(v,) + at(node)] + out[node]
                if direction == 1:
                    total = total + SECTION_DECAY * regv[(v,) + at(node)]
                acc[(v,) + at(node)] = total
        return carry

    lax.fori_loop(0, 16, functools.partial(lines, 0), 0)
    reg_load.wait()
    lax.fori_loop(0, 16, functools.partial(lines, 1), 0)

    names = jnp.where(away, lax.bitwise_and(nb[...], 255), 1000).astype(F32)
    names_down = jnp.transpose(jnp.concatenate([names, names], axis=0))
    for side in range(4):
        less = jnp.where(names_down[:, side:side + 1] < names[side:side + 1], 1.0, 0.0)
        order = jnp.sum(less, axis=0, keepdims=True)
        order = jnp.where(away[side:side + 1], order, -1.0).astype(jnp.int32)
        picks[side] = jnp.where(order == slot, 1.0, 0.0).astype(BF16)

    lane_z3 = lax.broadcasted_iota(jnp.int32, (80, 8, 128), 2) // SLOTS
    sub_z3 = lax.broadcasted_iota(jnp.int32, (80, 8, 128), 1)
    for side in range(4):
        select = jnp.where(here[side:side + 1] == rows, 1.0, 0.0).astype(BF16)
        hi, lo = split(trace_of(cv, side ^ 1))
        got = dot(hi, select) + dot(lo, select)
        ghost[side] = got.reshape(5, 4, 32, 256)

    for side in range(4):
        _, there, comes = sends[side]

        @pl.when(there)
        def _():
            copies[side].wait_send()

        @pl.when(comes)
        def _():
            copies[side].wait_recv()

        @pl.when(jnp.logical_not(comes))
        def _():
            arrived[side] = jnp.zeros((80, 128), F32)

        spread = jnp.where(lane_z3 == sub_z3, arrived[side][:, None, :], 0.0).reshape(640, 128)
        far_hi, far_lo = split(spread)
        both = jnp.concatenate([far_hi, far_lo], axis=1)
        twice = jnp.concatenate([picks[side], picks[side]], axis=0)
        ghost[side] = ghost[side] + dot(both, twice).reshape(5, 4, 32, 256)

    for way in (0, 1):
        _, there, comes = sends[4 + way]

        @pl.when(there)
        def _():
            copies[4 + way].wait_send()

        @pl.when(comes)
        def _():
            copies[4 + way].wait_recv()

        @pl.when(jnp.logical_not(comes))
        def _():
            recvv[way] = jnp.zeros((80, 256), F32)

    for v in range(5):
        part = pl.ds(16 * v, 16)
        own = sendv[0, part, :]
        vert[0, part, :] = jnp.where(below, recvv[1, part, :], -own if v == 3 else own)
        vert[1, part, :] = jnp.where(above, recvv[0, part, :], jnp.full_like(own, FREE_STREAM[v]))


def surface_kernel(cv, acc, ghost, vert, prim, kinds, adv, new, adv_v, new_v, out_sem):
    sub = lax.broadcasted_iota(jnp.int32, (8, 128), 0)
    outs = []
    for i in range(4):

        def half(js, h, carry):
            lanes = pl.ds(pl.multiple_of(h * 128, 128), 128)
            kind = [jnp.broadcast_to(kinds[s:s + 1, lanes], (8, 128)) for s in range(4)]
            open_face = [kind[s] == 0 for s in range(4)]
            wall = [kind[s] == 1 for s in range(4)]
            for j in js:
                for k in range(4):
                    rows_k = pl.ds(8 * k, 8)
                    q = [cv[v, i, j, rows_k, lanes] for v in range(5)]
                    total = [acc[v, i, j, rows_k, lanes] for v in range(5)]
                    faces = []
                    if i in (0, 3):
                        faces.append((0, 0 if i == 0 else 1, (j, k)))
                    if j in (0, 3):
                        faces.append((1, 2 if j == 0 else 3, (i, k)))
                    if k in (0, 3):
                        faces.append((2, 4 if k == 0 else 5, (i, j)))
                    if faces:
                        p_in, c_in = (prim[v, i, j, rows_k, lanes] for v in (3, 4))
                    for d, side, (a, b) in faces:
                        if side < 4:
                            outer = []
                            for v in range(5):
                                inner = -q[v] if v == 1 + d else q[v]
                                other = jnp.where(wall[side], inner, FREE_STREAM[v])
                                got = ghost[side, v, a, pl.ds(8 * b, 8), lanes]
                                outer.append(jnp.where(open_face[side], got, other))
                        else:
                            outer = []
                            for v in range(5):
                                m = v * 16 + a * 4 + b
                                if side == 4:
                                    near = cv[v, i, j, pl.ds(24, 8), lanes]
                                    near = pltpu.roll(near, 1, 0)
                                    edge = jnp.broadcast_to(vert[0, m:m + 1, lanes], (8, 128))
                                    outer.append(jnp.where(sub == 0, edge, near))
                                else:
                                    near = cv[v, i, j, pl.ds(0, 8), lanes]
                                    near = pltpu.roll(near, 7, 0)
                                    edge = jnp.broadcast_to(vert[1, m:m + 1, lanes], (8, 128))
                                    outer.append(jnp.where(sub == 7, edge, near))
                        sign = -1.0 if side % 2 == 0 else 1.0
                        r_out, p_out, c_out = primitive(outer)
                        v_in, v_out = prim[d, i, j, rows_k, lanes], outer[1 + d] * r_out
                        lam = LIFT * jnp.maximum(jnp.abs(v_in) + c_in, jnp.abs(v_out) + c_out)
                        s_in, s_out = (sign * LIFT) * v_in, (sign * LIFT) * v_out
                        w_in, w_out = lam - s_in, lam - s_out
                        for v in range(5):
                            total[v] = total[v] + (w_out * outer[v] - w_in * q[v])
                        total[1 + d] = total[1 + d] - (sign * LIFT) * (p_out - p_in)
                        total[4] = total[4] - (p_out * s_out - p_in * s_in)
                    for v in range(5):
                        new_v[v, i, j, rows_k, lanes] = total[v]
                        adv_v[v, i, j, rows_k, lanes] = q[v] + SECTION_WEIGHT * total[v]
            return carry

        for part in range(2):
            js = (2 * part, 2 * part + 1)
            lax.fori_loop(0, 2, functools.partial(half, js), 0)
            for n, (src, dst) in enumerate(((adv_v, adv), (new_v, new))):
                js_here = pl.ds(2 * part, 2)
                copy = pltpu.make_async_copy(src.at[:, i, js_here], dst.at[:, i, js_here], out_sem.at[n, 2 * i + part])
                copy.start()
                outs.append(copy)
    for copy in outs:
        copy.wait()


SHAPE = (5, 4, 4, 32, 256)


def per_device(conserved, register, neighbour, side_type):
    inputs = [
        pltpu.with_memory_space_constraint(x, pltpu.HBM)
        for x in (conserved.reshape(SHAPE), register.reshape(SHAPE), neighbour)
    ]
    handed = pl.pallas_call(
        exchange_kernel,
        name="exchange",
        out_shape=(
            pltpu.VMEM(SHAPE, F32),
            pltpu.VMEM(SHAPE, F32),
            pltpu.VMEM((4, 5, 4, 32, 256), F32),
            pltpu.VMEM((2, 80, 256), F32),
            pltpu.VMEM(SHAPE, F32),
        ),
        in_specs=[pl.BlockSpec(memory_space=pltpu.HBM)] * 3,
        out_specs=tuple([pl.BlockSpec(memory_space=pltpu.VMEM)] * 5),
        scratch_shapes=[
            pltpu.VMEM((4, 256), jnp.int32),
            pltpu.VMEM(SHAPE, F32),
            pltpu.VMEM((4, 128, 256), BF16),
            pltpu.VMEM((4, 640, 128), F32),
            pltpu.VMEM((4, 80, 128), F32),
            pltpu.VMEM((4, 80, 128), F32),
            pltpu.VMEM((2, 80, 256), F32),
            pltpu.VMEM((2, 80, 256), F32),
            pltpu.SemaphoreType.DMA((7,)),
            pltpu.SemaphoreType.DMA((4,)),
            pltpu.SemaphoreType.DMA((4,)),
            pltpu.SemaphoreType.DMA((2,)),
            pltpu.SemaphoreType.DMA((2,)),
        ],
        compiler_params=pltpu.CompilerParams(
            collective_id=0, has_side_effects=True, vmem_limit_bytes=40 * 1024 * 1024
        ),
    )(*inputs)
    handed = [pltpu.with_memory_space_constraint(x, pltpu.VMEM) for x in handed]
    adv, new = pl.pallas_call(
        surface_kernel,
        name="surface",
        out_shape=(jax.ShapeDtypeStruct(SHAPE, F32), jax.ShapeDtypeStruct(SHAPE, F32)),
        in_specs=[pl.BlockSpec(memory_space=pltpu.VMEM)] * 6,
        out_specs=(pl.BlockSpec(memory_space=pltpu.HBM), pl.BlockSpec(memory_space=pltpu.HBM)),
        scratch_shapes=[
            pltpu.VMEM(SHAPE, F32),
            pltpu.VMEM(SHAPE, F32),
            pltpu.SemaphoreType.DMA((2, 8)),
        ],
        compiler_params=pltpu.CompilerParams(vmem_limit_bytes=32 * 1024 * 1024),
    )(*handed, side_type)
    full = (5, 4, 4, 4, 8, 256)
    return adv.reshape(full), new.reshape(full)


def solution(mesh):
    spec = P(None, None, None, None, "layer", "foot")
    return jax.shard_map(
        per_device,
        mesh=mesh,
        in_specs=(spec, spec, P(None, "foot"), P(None, "foot")),
        out_specs=(spec, spec),
        check_vma=False,
    )
```

```python
import functools

import jax
import jax.numpy as jnp
import numpy as np
from jax import lax
from jax.experimental import pallas as pl
from jax.experimental.pallas import tpu as pltpu
from jax.sharding import PartitionSpec as P

TIME_STEP = 0.02
SECTION_DECAY = -0.4178904745
SECTION_WEIGHT = 1.720146321549
LIFT = 3.0 * TIME_STEP
FREE_STREAM = (1.0, 0.3, 0.1, 0.0, 1.0 / 0.56 + 0.05)
MESH = pl.DeviceIdType.MESH
SLOTS = 16
BF16 = jnp.bfloat16
F32 = jnp.float32
TILES_Y = 4


def derivative_entries():
    nodes = np.array([-1.0, -1.0 / np.sqrt(5.0), 1.0 / np.sqrt(5.0), 1.0])
    products = np.array(
        [np.prod([nodes[t] - nodes[a] for a in range(4) if a != t]) for t in range(4)]
    )
    matrix = np.zeros((4, 4))
    for t in range(4):
        for s in range(4):
            if t != s:
                matrix[t, s] = products[t] / products[s] / (nodes[t] - nodes[s])
            else:
                matrix[t, t] = sum(1.0 / (nodes[t] - nodes[a]) for a in range(4) if a != t)
    return matrix


ENTRIES = -TIME_STEP * derivative_entries()
ODD = [[0.5 * float(ENTRIES[p, i] - ENTRIES[p, 3 - i]) for i in (0, 1)] for p in (0, 1)]
EVEN = [0.5 * float(ENTRIES[p, 0] + ENTRIES[p, 3]) for p in (0, 1)]


def derived(f):
    s0, d0 = f[0] + f[3], f[0] - f[3]
    s1, d1 = f[1] + f[2], f[1] - f[2]
    t = s0 - s1
    a = ODD[0][0] * d0 + ODD[0][1] * d1
    b = EVEN[0] * t
    c = ODD[1][0] * d0 + ODD[1][1] * d1
    e = EVEN[1] * t
    return a + b, c + e, c - e, a - b


def inverse(x):
    r = pl.reciprocal(x, approx=True)
    return r * (2.0 - x * r)


def split(x):
    hi = x.astype(BF16)
    lo = (x - hi.astype(F32)).astype(BF16)
    return hi, lo


def dot(a, b):
    return jnp.dot(a, b, preferred_element_type=F32)


def dot_nt(a, b):
    return lax.dot_general(a, b, (((1,), (1,)), ((), ())), preferred_element_type=F32)


def face_rows(side):
    face = (0, 3)[side % 2]
    return (slice(None), face) if side < 2 else (slice(None), slice(None), face)


def trace_of(cv, side):
    return cv[face_rows(side)].reshape(640, 256)


def primitive(q):
    r = inverse(q[0])
    kinetic = (q[1] * q[1] + q[2] * q[2] + q[3] * q[3]) * r
    pressure = 0.4 * q[4] - 0.2 * kinetic
    square = 1.4 * pressure * r
    return r, pressure, square * lax.rsqrt(square)


def gather_slots(stage, side, lane_z):
    total = stage[side, pl.ds(0, 80, stride=8), :]
    for z in range(1, 8):
        total = jnp.where(lane_z == z, stage[side, pl.ds(z, 80, stride=8), :], total)
    return total


def exchange_kernel(
    cons, reg, nb_in, cv, acc, ghost, vert, prim,
    nb, regv, picks, send_picks, selects, stage, packed, arrived, sendv, recvv,
    load_sem, send_sem, recv_sem, vsend_sem, vrecv_sem,
):
    foot, layer = lax.axis_index("foot"), lax.axis_index("layer")
    layers = lax.axis_size("layer")
    along, across = foot // TILES_Y, lax.rem(foot, TILES_Y)
    tiles = lax.axis_size("foot") // TILES_Y

    lower, upper = along > 0, along < tiles - 1
    left, right = across > 0, across < TILES_Y - 1
    below, above = layer > 0, layer < layers - 1
    sends = [
        ((foot + TILES_Y, layer), upper, lower),
        ((foot - TILES_Y, layer), lower, upper),
        ((foot + 1, layer), right, left),
        ((foot - 1, layer), left, right),
        ((foot, layer - 1), below, above),
        ((foot, layer + 1), above, below),
    ]

    barrier = pltpu.get_barrier_semaphore()
    partners = jnp.int32(0)
    for partner, there, _ in sends:
        partners = partners + there.astype(jnp.int32)

        @pl.when(there)
        def _():
            pl.semaphore_signal(barrier, inc=1, device_id=partner, device_id_type=MESH)

    nb_load = pltpu.make_async_copy(nb_in, nb, load_sem.at[6])
    nb_load.start()
    loads = [pltpu.make_async_copy(cons.at[v], cv.at[v], load_sem.at[v]) for v in range(5)]
    for copy in loads:
        copy.start()
    reg_load = pltpu.make_async_copy(reg, regv, load_sem.at[5])

    slot = lax.bitwise_and(lax.broadcasted_iota(jnp.int32, (128, 256), 0), SLOTS - 1)
    lane_z = lax.broadcasted_iota(jnp.int32, (80, 128), 1) // SLOTS
    rows = lax.broadcasted_iota(jnp.int32, (256, 256), 0)
    cols = lax.broadcasted_iota(jnp.int32, (256, 256), 1)
    before = jnp.where(rows < cols, 1.0, 0.0).astype(BF16)
    nb_load.wait()
    here = nb[...] - foot * 256
    away = jnp.logical_or(here < 0, here >= 256)
    mask = jnp.where(away, 1.0, 0.0)
    mask8 = jnp.concatenate([mask, jnp.zeros_like(mask)], axis=0).astype(BF16)
    rank = jnp.where(away, dot(mask8, before)[0:4], -1.0).astype(jnp.int32)

    names = jnp.where(away, lax.bitwise_and(nb[...], 255), 1000).astype(F32)
    names_down = jnp.transpose(jnp.concatenate([names, names], axis=0))
    for side in range(4):
        less = jnp.where(names_down[:, side:side + 1] < names[side:side + 1], 1.0, 0.0)
        order = jnp.sum(less, axis=0, keepdims=True)
        order = jnp.where(away[side:side + 1], order, -1.0).astype(jnp.int32)
        picks[side] = jnp.where(order == slot, 1.0, 0.0).astype(BF16)

    for copy in loads:
        copy.wait()
    reg_load.start()

    for way in (0, 1):
        for h in (0, 1):
            lanes = pl.ds(h * 128, 128)
            stage[2 * way + h] = cv[:, :, :, pl.ds(24 * way, 8), lanes].reshape(640, 128)
            sendv[way, :, lanes] = stage[2 * way + h, pl.ds(7 * way, 80, stride=8), :]

    pl.semaphore_wait(barrier, partners)
    copies = []
    for side in range(4):
        copies.append(pltpu.make_async_remote_copy(
            src_ref=packed.at[side], dst_ref=arrived.at[side], send_sem=send_sem.at[side],
            recv_sem=recv_sem.at[side], device_id=sends[side][0], device_id_type=MESH,
        ))
    for way in (0, 1):
        copies.append(pltpu.make_async_remote_copy(
            src_ref=sendv.at[way], dst_ref=recvv.at[way], send_sem=vsend_sem.at[way],
            recv_sem=vrecv_sem.at[way], device_id=sends[4 + way][0], device_id_type=MESH,
        ))
    def launch(which):
        for copy, (_, there, _) in list(zip(copies, sends))[which]:

            @pl.when(there)
            def _():
                copy.start()

    launch(slice(4, 6))

    for side in range(4):
        hi, lo = split(trace_of(cv, side))
        send = jnp.where(rank[side:side + 1] == slot, 1.0, 0.0).astype(BF16)
        stage[side] = dot_nt(hi, send) + dot_nt(lo, send)
        packed[side ^ 1] = gather_slots(stage, side, lane_z)

    launch(slice(0, 4))

    def z_lines(line, carry):
        i, j = line // 4, line % 4
        q = [[cv[v, i, j, pl.ds(8 * k, 8), :] for k in range(4)] for v in range(5)]
        flux = [[], [], [], [], []]
        for k in range(4):
            rho, mx, my, mz, energy = (q[v][k] for v in range(5))
            r, pressure, sound = primitive([q[v][k] for v in range(5)])
            vz = mz * r
            rows_k = pl.ds(8 * k, 8)
            prim[0, i, j, rows_k, :] = mx * r
            prim[1, i, j, rows_k, :] = my * r
            prim[2, i, j, rows_k, :] = vz
            prim[3, i, j, rows_k, :] = pressure
            prim[4, i, j, rows_k, :] = sound
            flux[0].append(mz)
            flux[1].append(mx * vz)
            flux[2].append(my * vz)
            flux[3].append(mz * vz + pressure)
            flux[4].append((energy + pressure) * vz)
        for v in range(5):
            out = derived(flux[v])
            for k in range(4):
                rows_k = pl.ds(8 * k, 8)
                acc[v, i, j, rows_k, :] = out[k]
        return carry

    lax.fori_loop(0, 16, z_lines, 0, unroll=4)


    def lines(direction, line, carry):
        a, k = line // 4, line % 4
        rows_k = pl.ds(pl.multiple_of(8 * k, 8), 8)

        def at(node):
            return (node, a, rows_k, slice(None)) if direction == 0 else (a, node, rows_k, slice(None))

        flux = [[], [], [], [], []]
        for node in range(4):
            vd = prim[(direction,) + at(node)]
            pressure = prim[(3,) + at(node)]
            m = [cv[(1 + c,) + at(node)] for c in range(3)]
            flux[0].append(m[direction])
            for c in range(3):
                entry = m[c] * vd
                if c == direction:
                    entry = entry + pressure
                flux[1 + c].append(entry)
            flux[4].append((cv[(4,) + at(node)] + pressure) * vd)
        for v in range(5):
            out = derived(flux[v])
            for node in range(4):
                total = acc[(v,) + at(node)] + out[node]
                if direction == 1:
                    total = total + SECTION_DECAY * regv[(v,) + at(node)]
                acc[(v,) + at(node)] = total
        return carry

    lax.fori_loop(0, 16, functools.partial(lines, 0), 0, unroll=4)
    reg_load.wait()
    lax.fori_loop(0, 16, functools.partial(lines, 1), 0, unroll=4)

    for side in range(4):
        hi, lo = split(trace_of(cv, side))
        select = jnp.where(here[(side ^ 1):(side ^ 1) + 1] == rows, 1.0, 0.0).astype(BF16)
        got = dot(jnp.concatenate([hi, lo], axis=0), select)
        got = got[:640] + got[640:]
        ghost[side ^ 1] = got.reshape(5, 4, 32, 256)

    lane_z3 = lax.broadcasted_iota(jnp.int32, (80, 8, 128), 2) // SLOTS
    sub_z3 = lax.broadcasted_iota(jnp.int32, (80, 8, 128), 1)
    for side in range(4):
        _, there, comes = sends[side]

        @pl.when(there)
        def _():
            copies[side].wait_send()

        @pl.when(comes)
        def _():
            copies[side].wait_recv()

        @pl.when(jnp.logical_not(comes))
        def _():
            arrived[side] = jnp.zeros((80, 128), F32)

        spread = jnp.where(lane_z3 == sub_z3, arrived[side][:, None, :], 0.0).reshape(640, 128)
        far_hi, far_lo = split(spread)
        both = jnp.concatenate([far_hi, far_lo], axis=1)
        twice = jnp.concatenate([picks[side], picks[side]], axis=0)
        ghost[side] = ghost[side] + dot(both, twice).reshape(5, 4, 32, 256)

    for way in (0, 1):
        _, there, comes = sends[4 + way]

        @pl.when(there)
        def _():
            copies[4 + way].wait_send()

        @pl.when(comes)
        def _():
            copies[4 + way].wait_recv()

        @pl.when(jnp.logical_not(comes))
        def _():
            recvv[way] = jnp.zeros((80, 256), F32)

    for v in range(5):
        part = pl.ds(16 * v, 16)
        own = sendv[0, part, :]
        vert[0, part, :] = jnp.where(below, recvv[1, part, :], -own if v == 3 else own)
        vert[1, part, :] = jnp.where(above, recvv[0, part, :], jnp.full_like(own, FREE_STREAM[v]))


def surface_kernel(cv, acc, ghost, vert, prim, kinds, adv, new, adv_v, new_v, out_sem):
    sub = lax.broadcasted_iota(jnp.int32, (8, 128), 0)
    outs = []
    for i in range(4):

        def half(js, h, carry):
            lanes = pl.ds(pl.multiple_of(h * 128, 128), 128)
            kind = [jnp.broadcast_to(kinds[s:s + 1, lanes], (8, 128)) for s in range(4)]
            open_face = [kind[s] == 0 for s in range(4)]
            wall = [kind[s] == 1 for s in range(4)]
            for j in js:
                for k in range(4):
                    rows_k = pl.ds(8 * k, 8)
                    q = [cv[v, i, j, rows_k, lanes] for v in range(5)]
                    total = [acc[v, i, j, rows_k, lanes] for v in range(5)]
                    faces = []
                    if i in (0, 3):
                        faces.append((0, 0 if i == 0 else 1, (j, k)))
                    if j in (0, 3):
                        faces.append((1, 2 if j == 0 else 3, (i, k)))
                    if k in (0, 3):
                        faces.append((2, 4 if k == 0 else 5, (i, j)))
                    if faces:
                        p_in, c_in = (prim[v, i, j, rows_k, lanes] for v in (3, 4))
                    for d, side, (a, b) in faces:
                        if side < 4:
                            outer = []
                            for v in range(5):
                                inner = -q[v] if v == 1 + d else q[v]
                                other = jnp.where(wall[side], inner, FREE_STREAM[v])
                                got = ghost[side, v, a, pl.ds(8 * b, 8), lanes]
                                outer.append(jnp.where(open_face[side], got, other))
                        else:
                            outer = []
                            for v in range(5):
                                m = v * 16 + a * 4 + b
                                if side == 4:
                                    near = cv[v, i, j, pl.ds(24, 8), lanes]
                                    near = pltpu.roll(near, 1, 0)
                                    edge = jnp.broadcast_to(vert[0, m:m + 1, lanes], (8, 128))
                                    outer.append(jnp.where(sub == 0, edge, near))
                                else:
                                    near = cv[v, i, j, pl.ds(0, 8), lanes]
                                    near = pltpu.roll(near, 7, 0)
                                    edge = jnp.broadcast_to(vert[1, m:m + 1, lanes], (8, 128))
                                    outer.append(jnp.where(sub == 7, edge, near))
                        sign = -1.0 if side % 2 == 0 else 1.0
                        r_out, p_out, c_out = primitive(outer)
                        v_in, v_out = prim[d, i, j, rows_k, lanes], outer[1 + d] * r_out
                        lam = LIFT * jnp.maximum(jnp.abs(v_in) + c_in, jnp.abs(v_out) + c_out)
                        s_in, s_out = (sign * LIFT) * v_in, (sign * LIFT) * v_out
                        w_in, w_out = lam - s_in, lam - s_out
                        for v in range(5):
                            total[v] = total[v] + (w_out * outer[v] - w_in * q[v])
                        total[1 + d] = total[1 + d] - (sign * LIFT) * (p_out - p_in)
                        total[4] = total[4] - (p_out * s_out - p_in * s_in)
                    for v in range(5):
                        new_v[v, i, j, rows_k, lanes] = total[v]
                        adv_v[v, i, j, rows_k, lanes] = q[v] + SECTION_WEIGHT * total[v]
            return carry

        for part in range(2):
            js = (2 * part, 2 * part + 1)
            lax.fori_loop(0, 2, functools.partial(half, js), 0)
            for n, (src, dst) in enumerate(((adv_v, adv), (new_v, new))):
                js_here = pl.ds(2 * part, 2)
                copy = pltpu.make_async_copy(src.at[:, i, js_here], dst.at[:, i, js_here], out_sem.at[n, 2 * i + part])
                copy.start()
                outs.append(copy)
    for copy in outs:
        copy.wait()


SHAPE = (5, 4, 4, 32, 256)


def per_device(conserved, register, neighbour, side_type):
    inputs = [
        pltpu.with_memory_space_constraint(x, pltpu.HBM)
        for x in (conserved.reshape(SHAPE), register.reshape(SHAPE), neighbour)
    ]
    handed = pl.pallas_call(
        exchange_kernel,
        name="exchange",
        out_shape=(
            pltpu.VMEM(SHAPE, F32),
            pltpu.VMEM(SHAPE, F32),
            pltpu.VMEM((4, 5, 4, 32, 256), F32),
            pltpu.VMEM((2, 80, 256), F32),
            pltpu.VMEM(SHAPE, F32),
        ),
        in_specs=[pl.BlockSpec(memory_space=pltpu.HBM)] * 3,
        out_specs=tuple([pl.BlockSpec(memory_space=pltpu.VMEM)] * 5),
        scratch_shapes=[
            pltpu.VMEM((4, 256), jnp.int32),
            pltpu.VMEM(SHAPE, F32),
            pltpu.VMEM((4, 128, 256), BF16),
            pltpu.VMEM((4, 128, 256), BF16),
            pltpu.VMEM((4, 256, 256), BF16),
            pltpu.VMEM((4, 640, 128), F32),
            pltpu.VMEM((4, 80, 128), F32),
            pltpu.VMEM((4, 80, 128), F32),
            pltpu.VMEM((2, 80, 256), F32),
            pltpu.VMEM((2, 80, 256), F32),
            pltpu.SemaphoreType.DMA((7,)),
            pltpu.SemaphoreType.DMA((4,)),
            pltpu.SemaphoreType.DMA((4,)),
            pltpu.SemaphoreType.DMA((2,)),
            pltpu.SemaphoreType.DMA((2,)),
        ],
        compiler_params=pltpu.CompilerParams(
            collective_id=0, has_side_effects=True, vmem_limit_bytes=40 * 1024 * 1024
        ),
    )(*inputs)
    handed = [pltpu.with_memory_space_constraint(x, pltpu.VMEM) for x in handed]
    adv, new = pl.pallas_call(
        surface_kernel,
        name="surface",
        out_shape=(jax.ShapeDtypeStruct(SHAPE, F32), jax.ShapeDtypeStruct(SHAPE, F32)),
        in_specs=[pl.BlockSpec(memory_space=pltpu.VMEM)] * 6,
        out_specs=(pl.BlockSpec(memory_space=pltpu.HBM), pl.BlockSpec(memory_space=pltpu.HBM)),
        scratch_shapes=[
            pltpu.VMEM(SHAPE, F32),
            pltpu.VMEM(SHAPE, F32),
            pltpu.SemaphoreType.DMA((2, 8)),
        ],
        compiler_params=pltpu.CompilerParams(vmem_limit_bytes=32 * 1024 * 1024),
    )(*handed, side_type)
    full = (5, 4, 4, 4, 8, 256)
    return adv.reshape(full), new.reshape(full)


def solution(mesh):
    spec = P(None, None, None, None, "layer", "foot")
    return jax.shard_map(
        per_device,
        mesh=mesh,
        in_specs=(spec, spec, P(None, "foot"), P(None, "foot")),
        out_specs=(spec, spec),
        check_vma=False,
    )
```

```python
import functools

import jax
import jax.numpy as jnp
import numpy as np
from jax import lax
from jax.experimental import pallas as pl
from jax.experimental.pallas import tpu as pltpu
from jax.sharding import PartitionSpec as P

TIME_STEP = 0.02
SECTION_DECAY = -0.4178904745
SECTION_WEIGHT = 1.720146321549
LIFT = 3.0 * TIME_STEP
FREE_STREAM = (1.0, 0.3, 0.1, 0.0, 1.0 / 0.56 + 0.05)
MESH = pl.DeviceIdType.MESH
SLOTS = 16
BF16 = jnp.bfloat16
F32 = jnp.float32
TILES_Y = 4


def derivative_entries():
    nodes = np.array([-1.0, -1.0 / np.sqrt(5.0), 1.0 / np.sqrt(5.0), 1.0])
    products = np.array(
        [np.prod([nodes[t] - nodes[a] for a in range(4) if a != t]) for t in range(4)]
    )
    matrix = np.zeros((4, 4))
    for t in range(4):
        for s in range(4):
            if t != s:
                matrix[t, s] = products[t] / products[s] / (nodes[t] - nodes[s])
            else:
                matrix[t, t] = sum(1.0 / (nodes[t] - nodes[a]) for a in range(4) if a != t)
    return matrix


ENTRIES = -TIME_STEP * derivative_entries()
ODD = [[0.5 * float(ENTRIES[p, i] - ENTRIES[p, 3 - i]) for i in (0, 1)] for p in (0, 1)]
EVEN = [0.5 * float(ENTRIES[p, 0] + ENTRIES[p, 3]) for p in (0, 1)]


def derived(f):
    s0, d0 = f[0] + f[3], f[0] - f[3]
    s1, d1 = f[1] + f[2], f[1] - f[2]
    t = s0 - s1
    a = ODD[0][0] * d0 + ODD[0][1] * d1
    b = EVEN[0] * t
    c = ODD[1][0] * d0 + ODD[1][1] * d1
    e = EVEN[1] * t
    return a + b, c + e, c - e, a - b


def inverse(x):
    r = pl.reciprocal(x, approx=True)
    return r * (2.0 - x * r)


def split(x):
    hi = x.astype(BF16)
    lo = (x - hi.astype(F32)).astype(BF16)
    return hi, lo


def dot(a, b):
    return jnp.dot(a, b, preferred_element_type=F32)


def dot_nt(a, b):
    return lax.dot_general(a, b, (((1,), (1,)), ((), ())), preferred_element_type=F32)


def face_rows(side):
    face = (0, 3)[side % 2]
    return (slice(None), face) if side < 2 else (slice(None), slice(None), face)


def trace_of(cv, side):
    return cv[face_rows(side)].reshape(640, 256)


def primitive(q):
    r = inverse(q[0])
    kinetic = (q[1] * q[1] + q[2] * q[2] + q[3] * q[3]) * r
    pressure = 0.4 * q[4] - 0.2 * kinetic
    square = 1.4 * pressure * r
    return r, pressure, square * lax.rsqrt(square)


def gather_slots(stage, side, lane_z):
    total = stage[side, pl.ds(0, 80, stride=8), :]
    for z in range(1, 8):
        total = jnp.where(lane_z == z, stage[side, pl.ds(z, 80, stride=8), :], total)
    return total


def exchange_kernel(
    cons, reg, nb_in, cv, acc, ghost, vert, prim,
    nb, regv, picks, send_picks, selects, stage, packed, arrived, sendv, recvv,
    load_sem, send_sem, recv_sem, vsend_sem, vrecv_sem,
):
    foot, layer = lax.axis_index("foot"), lax.axis_index("layer")
    layers = lax.axis_size("layer")
    along, across = foot // TILES_Y, lax.rem(foot, TILES_Y)
    tiles = lax.axis_size("foot") // TILES_Y

    lower, upper = along > 0, along < tiles - 1
    left, right = across > 0, across < TILES_Y - 1
    below, above = layer > 0, layer < layers - 1
    sends = [
        ((foot + TILES_Y, layer), upper, lower),
        ((foot - TILES_Y, layer), lower, upper),
        ((foot + 1, layer), right, left),
        ((foot - 1, layer), left, right),
        ((foot, layer - 1), below, above),
        ((foot, layer + 1), above, below),
    ]

    barrier = pltpu.get_barrier_semaphore()
    partners = jnp.int32(0)
    for partner, there, _ in sends:
        partners = partners + there.astype(jnp.int32)

        @pl.when(there)
        def _():
            pl.semaphore_signal(barrier, inc=1, device_id=partner, device_id_type=MESH)

    nb_load = pltpu.make_async_copy(nb_in, nb, load_sem.at[6])
    nb_load.start()
    loads = [
        pltpu.make_async_copy(cons.at[:, :, :, part], cv.at[:, :, :, part], load_sem.at[n])
        for n, part in enumerate((pl.ds(0, 8), pl.ds(24, 8), pl.ds(8, 16)))
    ]
    for copy in loads:
        copy.start()
    reg_load = pltpu.make_async_copy(reg, regv, load_sem.at[5])

    slot = lax.bitwise_and(lax.broadcasted_iota(jnp.int32, (128, 256), 0), SLOTS - 1)
    lane_z = lax.broadcasted_iota(jnp.int32, (80, 128), 1) // SLOTS
    rows = lax.broadcasted_iota(jnp.int32, (256, 256), 0)
    cols = lax.broadcasted_iota(jnp.int32, (256, 256), 1)
    before = jnp.where(rows < cols, 1.0, 0.0).astype(BF16)
    nb_load.wait()
    here = nb[...] - foot * 256
    away = jnp.logical_or(here < 0, here >= 256)
    mask = jnp.where(away, 1.0, 0.0)
    mask8 = jnp.concatenate([mask, jnp.zeros_like(mask)], axis=0).astype(BF16)
    rank = jnp.where(away, dot(mask8, before)[0:4], -1.0).astype(jnp.int32)

    for way in (0, 1):
        loads[way].wait()
        for h in (0, 1):
            lanes = pl.ds(h * 128, 128)
            stage[2 * way + h] = cv[:, :, :, pl.ds(24 * way, 8), lanes].reshape(640, 128)
            sendv[way, :, lanes] = stage[2 * way + h, pl.ds(7 * way, 80, stride=8), :]

    pl.semaphore_wait(barrier, partners)
    copies = []
    for side in range(4):
        copies.append(pltpu.make_async_remote_copy(
            src_ref=packed.at[side], dst_ref=arrived.at[side], send_sem=send_sem.at[side],
            recv_sem=recv_sem.at[side], device_id=sends[side][0], device_id_type=MESH,
        ))
    for way in (0, 1):
        copies.append(pltpu.make_async_remote_copy(
            src_ref=sendv.at[way], dst_ref=recvv.at[way], send_sem=vsend_sem.at[way],
            recv_sem=vrecv_sem.at[way], device_id=sends[4 + way][0], device_id_type=MESH,
        ))
    def launch(which):
        for copy, (_, there, _) in list(zip(copies, sends))[which]:

            @pl.when(there)
            def _():
                copy.start()

    launch(slice(4, 6))

    names = jnp.where(away, lax.bitwise_and(nb[...], 255), 1000).astype(F32)
    names_down = jnp.transpose(jnp.concatenate([names, names], axis=0))
    for side in range(4):
        less = jnp.where(names_down[:, side:side + 1] < names[side:side + 1], 1.0, 0.0)
        order = jnp.sum(less, axis=0, keepdims=True)
        order = jnp.where(away[side:side + 1], order, -1.0).astype(jnp.int32)
        picks[side] = jnp.where(order == slot, 1.0, 0.0).astype(BF16)

    loads[2].wait()
    reg_load.start()

    for side in range(4):
        hi, lo = split(trace_of(cv, side))
        send = jnp.where(rank[side:side + 1] == slot, 1.0, 0.0).astype(BF16)
        stage[side] = dot_nt(hi, send) + dot_nt(lo, send)
        packed[side ^ 1] = gather_slots(stage, side, lane_z)

    launch(slice(0, 4))

    def z_lines(line, carry):
        i, j = line // 4, line % 4
        q = [[cv[v, i, j, pl.ds(8 * k, 8), :] for k in range(4)] for v in range(5)]
        flux = [[], [], [], [], []]
        for k in range(4):
            rho, mx, my, mz, energy = (q[v][k] for v in range(5))
            r, pressure, sound = primitive([q[v][k] for v in range(5)])
            vz = mz * r
            rows_k = pl.ds(8 * k, 8)
            prim[0, i, j, rows_k, :] = mx * r
            prim[1, i, j, rows_k, :] = my * r
            prim[2, i, j, rows_k, :] = vz
            prim[3, i, j, rows_k, :] = pressure
            prim[4, i, j, rows_k, :] = sound
            flux[0].append(mz)
            flux[1].append(mx * vz)
            flux[2].append(my * vz)
            flux[3].append(mz * vz + pressure)
            flux[4].append((energy + pressure) * vz)
        for v in range(5):
            out = derived(flux[v])
            for k in range(4):
                rows_k = pl.ds(8 * k, 8)
                acc[v, i, j, rows_k, :] = out[k]
        return carry

    lax.fori_loop(0, 16, z_lines, 0, unroll=4)


    def lines(direction, line, carry):
        a, k = line // 4, line % 4
        rows_k = pl.ds(pl.multiple_of(8 * k, 8), 8)

        def at(node):
            return (node, a, rows_k, slice(None)) if direction == 0 else (a, node, rows_k, slice(None))

        flux = [[], [], [], [], []]
        for node in range(4):
            vd = prim[(direction,) + at(node)]
            pressure = prim[(3,) + at(node)]
            m = [cv[(1 + c,) + at(node)] for c in range(3)]
            flux[0].append(m[direction])
            for c in range(3):
                entry = m[c] * vd
                if c == direction:
                    entry = entry + pressure
                flux[1 + c].append(entry)
            flux[4].append((cv[(4,) + at(node)] + pressure) * vd)
        for v in range(5):
            out = derived(flux[v])
            for node in range(4):
                total = acc[(v,) + at(node)] + out[node]
                if direction == 1:
                    total = total + SECTION_DECAY * regv[(v,) + at(node)]
                acc[(v,) + at(node)] = total
        return carry

    lax.fori_loop(0, 16, functools.partial(lines, 0), 0, unroll=4)
    reg_load.wait()
    lax.fori_loop(0, 16, functools.partial(lines, 1), 0, unroll=4)

    for side in range(4):
        hi, lo = split(trace_of(cv, side))
        select = jnp.where(here[(side ^ 1):(side ^ 1) + 1] == rows, 1.0, 0.0).astype(BF16)
        got = dot(jnp.concatenate([hi, lo], axis=0), select)
        got = got[:640] + got[640:]
        ghost[side ^ 1] = got.reshape(5, 4, 32, 256)

    lane_z3 = lax.broadcasted_iota(jnp.int32, (80, 8, 128), 2) // SLOTS
    sub_z3 = lax.broadcasted_iota(jnp.int32, (80, 8, 128), 1)
    for side in range(4):
        _, there, comes = sends[side]

        @pl.when(there)
        def _():
            copies[side].wait_send()

        @pl.when(comes)
        def _():
            copies[side].wait_recv()

        @pl.when(jnp.logical_not(comes))
        def _():
            arrived[side] = jnp.zeros((80, 128), F32)

        spread = jnp.where(lane_z3 == sub_z3, arrived[side][:, None, :], 0.0).reshape(640, 128)
        far_hi, far_lo = split(spread)
        both = jnp.concatenate([far_hi, far_lo], axis=1)
        twice = jnp.concatenate([picks[side], picks[side]], axis=0)
        ghost[side] = ghost[side] + dot(both, twice).reshape(5, 4, 32, 256)

    for way in (0, 1):
        _, there, comes = sends[4 + way]

        @pl.when(there)
        def _():
            copies[4 + way].wait_send()

        @pl.when(comes)
        def _():
            copies[4 + way].wait_recv()

        @pl.when(jnp.logical_not(comes))
        def _():
            recvv[way] = jnp.zeros((80, 256), F32)

    for v in range(5):
        part = pl.ds(16 * v, 16)
        own = sendv[0, part, :]
        vert[0, part, :] = jnp.where(below, recvv[1, part, :], -own if v == 3 else own)
        vert[1, part, :] = jnp.where(above, recvv[0, part, :], jnp.full_like(own, FREE_STREAM[v]))


def surface_kernel(cv, acc, ghost, vert, prim, kinds, adv, new, adv_v, new_v, out_sem):
    sub = lax.broadcasted_iota(jnp.int32, (8, 128), 0)
    outs = []
    for i in range(4):

        def half(js, h, carry):
            lanes = pl.ds(pl.multiple_of(h * 128, 128), 128)
            kind = [jnp.broadcast_to(kinds[s:s + 1, lanes], (8, 128)) for s in range(4)]
            open_face = [kind[s] == 0 for s in range(4)]
            wall = [kind[s] == 1 for s in range(4)]
            for j in js:
                for k in range(4):
                    rows_k = pl.ds(8 * k, 8)
                    q = [cv[v, i, j, rows_k, lanes] for v in range(5)]
                    total = [acc[v, i, j, rows_k, lanes] for v in range(5)]
                    faces = []
                    if i in (0, 3):
                        faces.append((0, 0 if i == 0 else 1, (j, k)))
                    if j in (0, 3):
                        faces.append((1, 2 if j == 0 else 3, (i, k)))
                    if k in (0, 3):
                        faces.append((2, 4 if k == 0 else 5, (i, j)))
                    if faces:
                        p_in, c_in = (prim[v, i, j, rows_k, lanes] for v in (3, 4))
                    for d, side, (a, b) in faces:
                        if side < 4:
                            outer = []
                            for v in range(5):
                                inner = -q[v] if v == 1 + d else q[v]
                                other = jnp.where(wall[side], inner, FREE_STREAM[v])
                                got = ghost[side, v, a, pl.ds(8 * b, 8), lanes]
                                outer.append(jnp.where(open_face[side], got, other))
                        else:
                            outer = []
                            for v in range(5):
                                m = v * 16 + a * 4 + b
                                if side == 4:
                                    near = cv[v, i, j, pl.ds(24, 8), lanes]
                                    near = pltpu.roll(near, 1, 0)
                                    edge = jnp.broadcast_to(vert[0, m:m + 1, lanes], (8, 128))
                                    outer.append(jnp.where(sub == 0, edge, near))
                                else:
                                    near = cv[v, i, j, pl.ds(0, 8), lanes]
                                    near = pltpu.roll(near, 7, 0)
                                    edge = jnp.broadcast_to(vert[1, m:m + 1, lanes], (8, 128))
                                    outer.append(jnp.where(sub == 7, edge, near))
                        sign = -1.0 if side % 2 == 0 else 1.0
                        r_out, p_out, c_out = primitive(outer)
                        v_in, v_out = prim[d, i, j, rows_k, lanes], outer[1 + d] * r_out
                        lam = LIFT * jnp.maximum(jnp.abs(v_in) + c_in, jnp.abs(v_out) + c_out)
                        s_in, s_out = (sign * LIFT) * v_in, (sign * LIFT) * v_out
                        w_in, w_out = lam - s_in, lam - s_out
                        for v in range(5):
                            total[v] = total[v] + (w_out * outer[v] - w_in * q[v])
                        total[1 + d] = total[1 + d] - (sign * LIFT) * (p_out - p_in)
                        total[4] = total[4] - (p_out * s_out - p_in * s_in)
                    for v in range(5):
                        new_v[v, i, j, rows_k, lanes] = total[v]
                        adv_v[v, i, j, rows_k, lanes] = q[v] + SECTION_WEIGHT * total[v]
            return carry

        for part in range(2):
            js = (2 * part, 2 * part + 1)
            lax.fori_loop(0, 2, functools.partial(half, js), 0)
            for n, (src, dst) in enumerate(((adv_v, adv), (new_v, new))):
                js_here = pl.ds(2 * part, 2)
                copy = pltpu.make_async_copy(src.at[:, i, js_here], dst.at[:, i, js_here], out_sem.at[n, 2 * i + part])
                copy.start()
                outs.append(copy)
    for copy in outs:
        copy.wait()


SHAPE = (5, 4, 4, 32, 256)


def per_device(conserved, register, neighbour, side_type):
    inputs = [
        pltpu.with_memory_space_constraint(x, pltpu.HBM)
        for x in (conserved.reshape(SHAPE), register.reshape(SHAPE), neighbour)
    ]
    handed = pl.pallas_call(
        exchange_kernel,
        name="exchange",
        out_shape=(
            pltpu.VMEM(SHAPE, F32),
            pltpu.VMEM(SHAPE, F32),
            pltpu.VMEM((4, 5, 4, 32, 256), F32),
            pltpu.VMEM((2, 80, 256), F32),
            pltpu.VMEM(SHAPE, F32),
        ),
        in_specs=[pl.BlockSpec(memory_space=pltpu.HBM)] * 3,
        out_specs=tuple([pl.BlockSpec(memory_space=pltpu.VMEM)] * 5),
        scratch_shapes=[
            pltpu.VMEM((4, 256), jnp.int32),
            pltpu.VMEM(SHAPE, F32),
            pltpu.VMEM((4, 128, 256), BF16),
            pltpu.VMEM((4, 128, 256), BF16),
            pltpu.VMEM((4, 256, 256), BF16),
            pltpu.VMEM((4, 640, 128), F32),
            pltpu.VMEM((4, 80, 128), F32),
            pltpu.VMEM((4, 80, 128), F32),
            pltpu.VMEM((2, 80, 256), F32),
            pltpu.VMEM((2, 80, 256), F32),
            pltpu.SemaphoreType.DMA((7,)),
            pltpu.SemaphoreType.DMA((4,)),
            pltpu.SemaphoreType.DMA((4,)),
            pltpu.SemaphoreType.DMA((2,)),
            pltpu.SemaphoreType.DMA((2,)),
        ],
        compiler_params=pltpu.CompilerParams(
            collective_id=0, has_side_effects=True, vmem_limit_bytes=40 * 1024 * 1024
        ),
    )(*inputs)
    handed = [pltpu.with_memory_space_constraint(x, pltpu.VMEM) for x in handed]
    adv, new = pl.pallas_call(
        surface_kernel,
        name="surface",
        out_shape=(jax.ShapeDtypeStruct(SHAPE, F32), jax.ShapeDtypeStruct(SHAPE, F32)),
        in_specs=[pl.BlockSpec(memory_space=pltpu.VMEM)] * 6,
        out_specs=(pl.BlockSpec(memory_space=pltpu.HBM), pl.BlockSpec(memory_space=pltpu.HBM)),
        scratch_shapes=[
            pltpu.VMEM(SHAPE, F32),
            pltpu.VMEM(SHAPE, F32),
            pltpu.SemaphoreType.DMA((2, 8)),
        ],
        compiler_params=pltpu.CompilerParams(vmem_limit_bytes=32 * 1024 * 1024),
    )(*handed, side_type)
    full = (5, 4, 4, 4, 8, 256)
    return adv.reshape(full), new.reshape(full)


def solution(mesh):
    spec = P(None, None, None, None, "layer", "foot")
    return jax.shard_map(
        per_device,
        mesh=mesh,
        in_specs=(spec, spec, P(None, "foot"), P(None, "foot")),
        out_specs=(spec, spec),
        check_vma=False,
    )
```

```python
import functools

import jax
import jax.numpy as jnp
import numpy as np
from jax import lax
from jax.experimental import pallas as pl
from jax.experimental.pallas import tpu as pltpu
from jax.sharding import PartitionSpec as P

TIME_STEP = 0.02
SECTION_DECAY = -0.4178904745
SECTION_WEIGHT = 1.720146321549
LIFT = 3.0 * TIME_STEP
FREE_STREAM = (1.0, 0.3, 0.1, 0.0, 1.0 / 0.56 + 0.05)
MESH = pl.DeviceIdType.MESH
SLOTS = 16
BF16 = jnp.bfloat16
F32 = jnp.float32
TILES_Y = 4


def derivative_entries():
    nodes = np.array([-1.0, -1.0 / np.sqrt(5.0), 1.0 / np.sqrt(5.0), 1.0])
    products = np.array(
        [np.prod([nodes[t] - nodes[a] for a in range(4) if a != t]) for t in range(4)]
    )
    matrix = np.zeros((4, 4))
    for t in range(4):
        for s in range(4):
            if t != s:
                matrix[t, s] = products[t] / products[s] / (nodes[t] - nodes[s])
            else:
                matrix[t, t] = sum(1.0 / (nodes[t] - nodes[a]) for a in range(4) if a != t)
    return matrix


ENTRIES = -TIME_STEP * derivative_entries()
ODD = [[0.5 * float(ENTRIES[p, i] - ENTRIES[p, 3 - i]) for i in (0, 1)] for p in (0, 1)]
EVEN = [0.5 * float(ENTRIES[p, 0] + ENTRIES[p, 3]) for p in (0, 1)]


def derived(f):
    s0, d0 = f[0] + f[3], f[0] - f[3]
    s1, d1 = f[1] + f[2], f[1] - f[2]
    t = s0 - s1
    a = ODD[0][0] * d0 + ODD[0][1] * d1
    b = EVEN[0] * t
    c = ODD[1][0] * d0 + ODD[1][1] * d1
    e = EVEN[1] * t
    return a + b, c + e, c - e, a - b


def inverse(x):
    r = pl.reciprocal(x, approx=True)
    return r * (2.0 - x * r)


def split(x):
    hi = x.astype(BF16)
    lo = (x - hi.astype(F32)).astype(BF16)
    return hi, lo


def dot(a, b):
    return jnp.dot(a, b, preferred_element_type=F32)


def dot_nt(a, b):
    return lax.dot_general(a, b, (((1,), (1,)), ((), ())), preferred_element_type=F32)


def face_rows(side):
    face = (0, 3)[side % 2]
    return (slice(None), face) if side < 2 else (slice(None), slice(None), face)


def trace_of(cv, side):
    return cv[face_rows(side)].reshape(640, 256)


def primitive(q):
    r = inverse(q[0])
    kinetic = (q[1] * q[1] + q[2] * q[2] + q[3] * q[3]) * r
    pressure = 0.4 * q[4] - 0.2 * kinetic
    square = 1.4 * pressure * r
    return r, pressure, square * lax.rsqrt(square)


def gather_slots(stage, side, lane_z):
    total = stage[side, pl.ds(0, 80, stride=8), :]
    for z in range(1, 8):
        total = jnp.where(lane_z == z, stage[side, pl.ds(z, 80, stride=8), :], total)
    return total


def exchange_kernel(
    cons, reg, nb_in, cv, acc, ghost, vert, prim,
    nb, regv, picks, send_picks, selects, stage, packed, arrived, sendv, recvv,
    load_sem, send_sem, recv_sem, vsend_sem, vrecv_sem,
):
    foot, layer = lax.axis_index("foot"), lax.axis_index("layer")
    layers = lax.axis_size("layer")
    along, across = foot // TILES_Y, lax.rem(foot, TILES_Y)
    tiles = lax.axis_size("foot") // TILES_Y

    lower, upper = along > 0, along < tiles - 1
    left, right = across > 0, across < TILES_Y - 1
    below, above = layer > 0, layer < layers - 1
    sends = [
        ((foot + TILES_Y, layer), upper, lower),
        ((foot - TILES_Y, layer), lower, upper),
        ((foot + 1, layer), right, left),
        ((foot - 1, layer), left, right),
        ((foot, layer - 1), below, above),
        ((foot, layer + 1), above, below),
    ]

    barrier = pltpu.get_barrier_semaphore()
    partners = jnp.int32(0)
    for partner, there, _ in sends:
        partners = partners + there.astype(jnp.int32)

        @pl.when(there)
        def _():
            pl.semaphore_signal(barrier, inc=1, device_id=partner, device_id_type=MESH)

    nb_load = pltpu.make_async_copy(nb_in, nb, load_sem.at[6])
    nb_load.start()
    loads = [
        pltpu.make_async_copy(cons.at[:, :, :, part], cv.at[:, :, :, part], load_sem.at[n])
        for n, part in enumerate((pl.ds(0, 8), pl.ds(24, 8), pl.ds(8, 16)))
    ]
    for copy in loads:
        copy.start()
    reg_load = pltpu.make_async_copy(reg, regv, load_sem.at[5])

    slot = lax.bitwise_and(lax.broadcasted_iota(jnp.int32, (128, 256), 0), SLOTS - 1)
    lane_z = lax.broadcasted_iota(jnp.int32, (80, 128), 1) // SLOTS
    rows = lax.broadcasted_iota(jnp.int32, (256, 256), 0)
    cols = lax.broadcasted_iota(jnp.int32, (256, 256), 1)
    before = jnp.where(rows < cols, 1.0, 0.0).astype(BF16)
    nb_load.wait()
    here = nb[...] - foot * 256
    away = jnp.logical_or(here < 0, here >= 256)
    mask = jnp.where(away, 1.0, 0.0)
    mask8 = jnp.concatenate([mask, jnp.zeros_like(mask)], axis=0).astype(BF16)
    rank = jnp.where(away, dot(mask8, before)[0:4], -1.0).astype(jnp.int32)

    for way in (0, 1):
        loads[way].wait()
        for h in (0, 1):
            lanes = pl.ds(h * 128, 128)
            stage[2 * way + h] = cv[:, :, :, pl.ds(24 * way, 8), lanes].reshape(640, 128)
            sendv[way, :, lanes] = stage[2 * way + h, pl.ds(7 * way, 80, stride=8), :]

    copies = []
    for side in range(4):
        copies.append(pltpu.make_async_remote_copy(
            src_ref=packed.at[side], dst_ref=arrived.at[side], send_sem=send_sem.at[side],
            recv_sem=recv_sem.at[side], device_id=sends[side][0], device_id_type=MESH,
        ))
    for way in (0, 1):
        copies.append(pltpu.make_async_remote_copy(
            src_ref=sendv.at[way], dst_ref=recvv.at[way], send_sem=vsend_sem.at[way],
            recv_sem=vrecv_sem.at[way], device_id=sends[4 + way][0], device_id_type=MESH,
        ))
    def launch(which):
        for copy, (_, there, _) in list(zip(copies, sends))[which]:

            @pl.when(there)
            def _():
                copy.start()


    names = jnp.where(away, lax.bitwise_and(nb[...], 255), 1000).astype(F32)
    names_down = jnp.transpose(jnp.concatenate([names, names], axis=0))
    for side in range(4):
        less = jnp.where(names_down[:, side:side + 1] < names[side:side + 1], 1.0, 0.0)
        order = jnp.sum(less, axis=0, keepdims=True)
        order = jnp.where(away[side:side + 1], order, -1.0).astype(jnp.int32)
        picks[side] = jnp.where(order == slot, 1.0, 0.0).astype(BF16)

    loads[2].wait()
    reg_load.start()

    def open_vertical():
        pl.semaphore_wait(barrier, partners)
        launch(slice(4, 6))

    first = layer == layers // 2 - 1
    pl.when(first)(open_vertical)

    for side in range(4):
        hi, lo = split(trace_of(cv, side))
        send = jnp.where(rank[side:side + 1] == slot, 1.0, 0.0).astype(BF16)
        stage[side] = dot_nt(hi, send) + dot_nt(lo, send)
        packed[side ^ 1] = gather_slots(stage, side, lane_z)

    pl.when(jnp.logical_not(first))(open_vertical)
    launch(slice(0, 4))

    def z_lines(line, carry):
        i, j = line // 4, line % 4
        q = [[cv[v, i, j, pl.ds(8 * k, 8), :] for k in range(4)] for v in range(5)]
        flux = [[], [], [], [], []]
        for k in range(4):
            rho, mx, my, mz, energy = (q[v][k] for v in range(5))
            r, pressure, sound = primitive([q[v][k] for v in range(5)])
            vz = mz * r
            rows_k = pl.ds(8 * k, 8)
            prim[0, i, j, rows_k, :] = mx * r
            prim[1, i, j, rows_k, :] = my * r
            prim[2, i, j, rows_k, :] = vz
            prim[3, i, j, rows_k, :] = pressure
            prim[4, i, j, rows_k, :] = sound
            flux[0].append(mz)
            flux[1].append(mx * vz)
            flux[2].append(my * vz)
            flux[3].append(mz * vz + pressure)
            flux[4].append((energy + pressure) * vz)
        for v in range(5):
            out = derived(flux[v])
            for k in range(4):
                rows_k = pl.ds(8 * k, 8)
                acc[v, i, j, rows_k, :] = out[k]
        return carry

    lax.fori_loop(0, 16, z_lines, 0, unroll=4)


    def lines(direction, line, carry):
        a, k = line // 4, line % 4
        rows_k = pl.ds(pl.multiple_of(8 * k, 8), 8)

        def at(node):
            return (node, a, rows_k, slice(None)) if direction == 0 else (a, node, rows_k, slice(None))

        flux = [[], [], [], [], []]
        for node in range(4):
            vd = prim[(direction,) + at(node)]
            pressure = prim[(3,) + at(node)]
            m = [cv[(1 + c,) + at(node)] for c in range(3)]
            flux[0].append(m[direction])
            for c in range(3):
                entry = m[c] * vd
                if c == direction:
                    entry = entry + pressure
                flux[1 + c].append(entry)
            flux[4].append((cv[(4,) + at(node)] + pressure) * vd)
        for v in range(5):
            out = derived(flux[v])
            for node in range(4):
                total = acc[(v,) + at(node)] + out[node]
                if direction == 1:
                    total = total + SECTION_DECAY * regv[(v,) + at(node)]
                acc[(v,) + at(node)] = total
        return carry

    lax.fori_loop(0, 16, functools.partial(lines, 0), 0, unroll=4)
    reg_load.wait()
    lax.fori_loop(0, 16, functools.partial(lines, 1), 0, unroll=4)

    for side in range(4):
        hi, lo = split(trace_of(cv, side))
        select = jnp.where(here[(side ^ 1):(side ^ 1) + 1] == rows, 1.0, 0.0).astype(BF16)
        got = dot(jnp.concatenate([hi, lo], axis=0), select)
        got = got[:640] + got[640:]
        ghost[side ^ 1] = got.reshape(5, 4, 32, 256)

    lane_z3 = lax.broadcasted_iota(jnp.int32, (80, 8, 128), 2) // SLOTS
    sub_z3 = lax.broadcasted_iota(jnp.int32, (80, 8, 128), 1)
    for side in range(4):
        _, there, comes = sends[side]

        @pl.when(there)
        def _():
            copies[side].wait_send()

        @pl.when(comes)
        def _():
            copies[side].wait_recv()

        @pl.when(jnp.logical_not(comes))
        def _():
            arrived[side] = jnp.zeros((80, 128), F32)

        spread = jnp.where(lane_z3 == sub_z3, arrived[side][:, None, :], 0.0).reshape(640, 128)
        far_hi, far_lo = split(spread)
        both = jnp.concatenate([far_hi, far_lo], axis=1)
        twice = jnp.concatenate([picks[side], picks[side]], axis=0)
        ghost[side] = ghost[side] + dot(both, twice).reshape(5, 4, 32, 256)

    for way in (0, 1):
        _, there, comes = sends[4 + way]

        @pl.when(there)
        def _():
            copies[4 + way].wait_send()

        @pl.when(comes)
        def _():
            copies[4 + way].wait_recv()

        @pl.when(jnp.logical_not(comes))
        def _():
            recvv[way] = jnp.zeros((80, 256), F32)

    for v in range(5):
        part = pl.ds(16 * v, 16)
        own = sendv[0, part, :]
        vert[0, part, :] = jnp.where(below, recvv[1, part, :], -own if v == 3 else own)
        vert[1, part, :] = jnp.where(above, recvv[0, part, :], jnp.full_like(own, FREE_STREAM[v]))


def surface_kernel(cv, acc, ghost, vert, prim, kinds, adv, new, adv_v, new_v, out_sem):
    sub = lax.broadcasted_iota(jnp.int32, (8, 128), 0)
    outs = []
    for i in range(4):

        def half(js, h, carry):
            lanes = pl.ds(pl.multiple_of(h * 128, 128), 128)
            kind = [jnp.broadcast_to(kinds[s:s + 1, lanes], (8, 128)) for s in range(4)]
            open_face = [kind[s] == 0 for s in range(4)]
            wall = [kind[s] == 1 for s in range(4)]
            for j in js:
                for k in range(4):
                    rows_k = pl.ds(8 * k, 8)
                    q = [cv[v, i, j, rows_k, lanes] for v in range(5)]
                    total = [acc[v, i, j, rows_k, lanes] for v in range(5)]
                    faces = []
                    if i in (0, 3):
                        faces.append((0, 0 if i == 0 else 1, (j, k)))
                    if j in (0, 3):
                        faces.append((1, 2 if j == 0 else 3, (i, k)))
                    if k in (0, 3):
                        faces.append((2, 4 if k == 0 else 5, (i, j)))
                    if faces:
                        p_in, c_in = (prim[v, i, j, rows_k, lanes] for v in (3, 4))
                    for d, side, (a, b) in faces:
                        if side < 4:
                            outer = []
                            for v in range(5):
                                inner = -q[v] if v == 1 + d else q[v]
                                other = jnp.where(wall[side], inner, FREE_STREAM[v])
                                got = ghost[side, v, a, pl.ds(8 * b, 8), lanes]
                                outer.append(jnp.where(open_face[side], got, other))
                        else:
                            outer = []
                            for v in range(5):
                                m = v * 16 + a * 4 + b
                                if side == 4:
                                    near = cv[v, i, j, pl.ds(24, 8), lanes]
                                    near = pltpu.roll(near, 1, 0)
                                    edge = jnp.broadcast_to(vert[0, m:m + 1, lanes], (8, 128))
                                    outer.append(jnp.where(sub == 0, edge, near))
                                else:
                                    near = cv[v, i, j, pl.ds(0, 8), lanes]
                                    near = pltpu.roll(near, 7, 0)
                                    edge = jnp.broadcast_to(vert[1, m:m + 1, lanes], (8, 128))
                                    outer.append(jnp.where(sub == 7, edge, near))
                        sign = -1.0 if side % 2 == 0 else 1.0
                        r_out, p_out, c_out = primitive(outer)
                        v_in, v_out = prim[d, i, j, rows_k, lanes], outer[1 + d] * r_out
                        lam = LIFT * jnp.maximum(jnp.abs(v_in) + c_in, jnp.abs(v_out) + c_out)
                        s_in, s_out = (sign * LIFT) * v_in, (sign * LIFT) * v_out
                        w_in, w_out = lam - s_in, lam - s_out
                        for v in range(5):
                            total[v] = total[v] + (w_out * outer[v] - w_in * q[v])
                        total[1 + d] = total[1 + d] - (sign * LIFT) * (p_out - p_in)
                        total[4] = total[4] - (p_out * s_out - p_in * s_in)
                    for v in range(5):
                        new_v[v, i, j, rows_k, lanes] = total[v]
                        adv_v[v, i, j, rows_k, lanes] = q[v] + SECTION_WEIGHT * total[v]
            return carry

        for part in range(2):
            js = (2 * part, 2 * part + 1)
            lax.fori_loop(0, 2, functools.partial(half, js), 0)
            for n, (src, dst) in enumerate(((adv_v, adv), (new_v, new))):
                js_here = pl.ds(2 * part, 2)
                copy = pltpu.make_async_copy(src.at[:, i, js_here], dst.at[:, i, js_here], out_sem.at[n, 2 * i + part])
                copy.start()
                outs.append(copy)
    for copy in outs:
        copy.wait()


SHAPE = (5, 4, 4, 32, 256)


def per_device(conserved, register, neighbour, side_type):
    inputs = [
        pltpu.with_memory_space_constraint(x, pltpu.HBM)
        for x in (conserved.reshape(SHAPE), register.reshape(SHAPE), neighbour)
    ]
    handed = pl.pallas_call(
        exchange_kernel,
        name="exchange",
        out_shape=(
            pltpu.VMEM(SHAPE, F32),
            pltpu.VMEM(SHAPE, F32),
            pltpu.VMEM((4, 5, 4, 32, 256), F32),
            pltpu.VMEM((2, 80, 256), F32),
            pltpu.VMEM(SHAPE, F32),
        ),
        in_specs=[pl.BlockSpec(memory_space=pltpu.HBM)] * 3,
        out_specs=tuple([pl.BlockSpec(memory_space=pltpu.VMEM)] * 5),
        scratch_shapes=[
            pltpu.VMEM((4, 256), jnp.int32),
            pltpu.VMEM(SHAPE, F32),
            pltpu.VMEM((4, 128, 256), BF16),
            pltpu.VMEM((4, 128, 256), BF16),
            pltpu.VMEM((4, 256, 256), BF16),
            pltpu.VMEM((4, 640, 128), F32),
            pltpu.VMEM((4, 80, 128), F32),
            pltpu.VMEM((4, 80, 128), F32),
            pltpu.VMEM((2, 80, 256), F32),
            pltpu.VMEM((2, 80, 256), F32),
            pltpu.SemaphoreType.DMA((7,)),
            pltpu.SemaphoreType.DMA((4,)),
            pltpu.SemaphoreType.DMA((4,)),
            pltpu.SemaphoreType.DMA((2,)),
            pltpu.SemaphoreType.DMA((2,)),
        ],
        compiler_params=pltpu.CompilerParams(
            collective_id=0, has_side_effects=True, vmem_limit_bytes=40 * 1024 * 1024
        ),
    )(*inputs)
    handed = [pltpu.with_memory_space_constraint(x, pltpu.VMEM) for x in handed]
    adv, new = pl.pallas_call(
        surface_kernel,
        name="surface",
        out_shape=(jax.ShapeDtypeStruct(SHAPE, F32), jax.ShapeDtypeStruct(SHAPE, F32)),
        in_specs=[pl.BlockSpec(memory_space=pltpu.VMEM)] * 6,
        out_specs=(pl.BlockSpec(memory_space=pltpu.HBM), pl.BlockSpec(memory_space=pltpu.HBM)),
        scratch_shapes=[
            pltpu.VMEM(SHAPE, F32),
            pltpu.VMEM(SHAPE, F32),
            pltpu.SemaphoreType.DMA((2, 8)),
        ],
        compiler_params=pltpu.CompilerParams(vmem_limit_bytes=32 * 1024 * 1024),
    )(*handed, side_type)
    full = (5, 4, 4, 4, 8, 256)
    return adv.reshape(full), new.reshape(full)


def solution(mesh):
    spec = P(None, None, None, None, "layer", "foot")
    return jax.shard_map(
        per_device,
        mesh=mesh,
        in_specs=(spec, spec, P(None, "foot"), P(None, "foot")),
        out_specs=(spec, spec),
        check_vma=False,
    )
```

```python
import functools

import jax
import jax.numpy as jnp
import numpy as np
from jax import lax
from jax.experimental import pallas as pl
from jax.experimental.pallas import tpu as pltpu
from jax.sharding import PartitionSpec as P

TIME_STEP = 0.02
SECTION_DECAY = -0.4178904745
SECTION_WEIGHT = 1.720146321549
LIFT = 3.0 * TIME_STEP
FREE_STREAM = (1.0, 0.3, 0.1, 0.0, 1.0 / 0.56 + 0.05)
MESH = pl.DeviceIdType.MESH
SLOTS = 16
BF16 = jnp.bfloat16
F32 = jnp.float32
TILES_Y = 4


def derivative_entries():
    nodes = np.array([-1.0, -1.0 / np.sqrt(5.0), 1.0 / np.sqrt(5.0), 1.0])
    products = np.array(
        [np.prod([nodes[t] - nodes[a] for a in range(4) if a != t]) for t in range(4)]
    )
    matrix = np.zeros((4, 4))
    for t in range(4):
        for s in range(4):
            if t != s:
                matrix[t, s] = products[t] / products[s] / (nodes[t] - nodes[s])
            else:
                matrix[t, t] = sum(1.0 / (nodes[t] - nodes[a]) for a in range(4) if a != t)
    return matrix


ENTRIES = -TIME_STEP * derivative_entries()
ODD = [[0.5 * float(ENTRIES[p, i] - ENTRIES[p, 3 - i]) for i in (0, 1)] for p in (0, 1)]
EVEN = [0.5 * float(ENTRIES[p, 0] + ENTRIES[p, 3]) for p in (0, 1)]


def derived(f):
    s0, d0 = f[0] + f[3], f[0] - f[3]
    s1, d1 = f[1] + f[2], f[1] - f[2]
    t = s0 - s1
    a = ODD[0][0] * d0 + ODD[0][1] * d1
    b = EVEN[0] * t
    c = ODD[1][0] * d0 + ODD[1][1] * d1
    e = EVEN[1] * t
    return a + b, c + e, c - e, a - b


def inverse(x):
    r = pl.reciprocal(x, approx=True)
    return r * (2.0 - x * r)


def split(x):
    hi = x.astype(BF16)
    lo = (x - hi.astype(F32)).astype(BF16)
    return hi, lo


def dot(a, b):
    return jnp.dot(a, b, preferred_element_type=F32)


def dot_nt(a, b):
    return lax.dot_general(a, b, (((1,), (1,)), ((), ())), preferred_element_type=F32)


def face_rows(side):
    face = (0, 3)[side % 2]
    return (slice(None), face) if side < 2 else (slice(None), slice(None), face)


def trace_of(cv, side):
    return cv[face_rows(side)].reshape(640, 256)


def primitive(q):
    r = inverse(q[0])
    kinetic = (q[1] * q[1] + q[2] * q[2] + q[3] * q[3]) * r
    pressure = 0.4 * q[4] - 0.2 * kinetic
    square = 1.4 * pressure * r
    return r, pressure, square * lax.rsqrt(square)


def gather_slots(stage, side, lane_z):
    total = stage[side, pl.ds(0, 80, stride=8), :]
    for z in range(1, 8):
        total = jnp.where(lane_z == z, stage[side, pl.ds(z, 80, stride=8), :], total)
    return total


def exchange_kernel(
    cons, reg, nb_in, kinds_in, cv, acc, ghost, vert, prim,
    nb, kinds, regv, picks, send_picks, selects, stage, packed, arrived, sendv, recvv,
    load_sem, send_sem, recv_sem, vsend_sem, vrecv_sem,
):
    foot, layer = lax.axis_index("foot"), lax.axis_index("layer")
    layers = lax.axis_size("layer")
    along, across = foot // TILES_Y, lax.rem(foot, TILES_Y)
    tiles = lax.axis_size("foot") // TILES_Y

    lower, upper = along > 0, along < tiles - 1
    left, right = across > 0, across < TILES_Y - 1
    below, above = layer > 0, layer < layers - 1
    sends = [
        ((foot + TILES_Y, layer), upper, lower),
        ((foot - TILES_Y, layer), lower, upper),
        ((foot + 1, layer), right, left),
        ((foot - 1, layer), left, right),
        ((foot, layer - 1), below, above),
        ((foot, layer + 1), above, below),
    ]

    barrier = pltpu.get_barrier_semaphore()
    partners = jnp.int32(0)
    for partner, there, _ in sends:
        partners = partners + there.astype(jnp.int32)

        @pl.when(there)
        def _():
            pl.semaphore_signal(barrier, inc=1, device_id=partner, device_id_type=MESH)

    nb_load = pltpu.make_async_copy(nb_in, nb, load_sem.at[6])
    nb_load.start()
    kinds_load = pltpu.make_async_copy(kinds_in, kinds, load_sem.at[7])
    kinds_load.start()
    loads = [
        pltpu.make_async_copy(cons.at[:, :, :, part], cv.at[:, :, :, part], load_sem.at[n])
        for n, part in enumerate((pl.ds(0, 8), pl.ds(24, 8), pl.ds(8, 16)))
    ]
    for copy in loads:
        copy.start()
    reg_load = pltpu.make_async_copy(reg, regv, load_sem.at[5])

    slot = lax.bitwise_and(lax.broadcasted_iota(jnp.int32, (128, 256), 0), SLOTS - 1)
    lane_z = lax.broadcasted_iota(jnp.int32, (80, 128), 1) // SLOTS
    rows = lax.broadcasted_iota(jnp.int32, (256, 256), 0)
    cols = lax.broadcasted_iota(jnp.int32, (256, 256), 1)
    before = jnp.where(rows < cols, 1.0, 0.0).astype(BF16)
    nb_load.wait()
    here = nb[...] - foot * 256
    away = jnp.logical_or(here < 0, here >= 256)
    mask = jnp.where(away, 1.0, 0.0)
    mask8 = jnp.concatenate([mask, jnp.zeros_like(mask)], axis=0).astype(BF16)
    rank = jnp.where(away, dot(mask8, before)[0:4], -1.0).astype(jnp.int32)

    for way in (0, 1):
        loads[way].wait()
        for h in (0, 1):
            lanes = pl.ds(h * 128, 128)
            stage[2 * way + h] = cv[:, :, :, pl.ds(24 * way, 8), lanes].reshape(640, 128)
            sendv[way, :, lanes] = stage[2 * way + h, pl.ds(7 * way, 80, stride=8), :]

    copies = []
    for side in range(4):
        copies.append(pltpu.make_async_remote_copy(
            src_ref=packed.at[side], dst_ref=arrived.at[side], send_sem=send_sem.at[side],
            recv_sem=recv_sem.at[side], device_id=sends[side][0], device_id_type=MESH,
        ))
    for way in (0, 1):
        copies.append(pltpu.make_async_remote_copy(
            src_ref=sendv.at[way], dst_ref=recvv.at[way], send_sem=vsend_sem.at[way],
            recv_sem=vrecv_sem.at[way], device_id=sends[4 + way][0], device_id_type=MESH,
        ))
    def launch(which):
        for copy, (_, there, _) in list(zip(copies, sends))[which]:

            @pl.when(there)
            def _():
                copy.start()


    names = jnp.where(away, lax.bitwise_and(nb[...], 255), 1000).astype(F32)
    names_down = jnp.transpose(jnp.concatenate([names, names], axis=0))
    for side in range(4):
        less = jnp.where(names_down[:, side:side + 1] < names[side:side + 1], 1.0, 0.0)
        order = jnp.sum(less, axis=0, keepdims=True)
        order = jnp.where(away[side:side + 1], order, -1.0).astype(jnp.int32)
        picks[side] = jnp.where(order == slot, 1.0, 0.0).astype(BF16)

    kinds_load.wait()
    loads[2].wait()
    reg_load.start()

    def open_vertical():
        pl.semaphore_wait(barrier, partners)
        launch(slice(4, 6))

    first = layer == layers // 2 - 1
    pl.when(first)(open_vertical)

    for side in range(4):
        hi, lo = split(trace_of(cv, side))
        send = jnp.where(rank[side:side + 1] == slot, 1.0, 0.0).astype(BF16)
        stage[side] = dot_nt(hi, send) + dot_nt(lo, send)
        packed[side ^ 1] = gather_slots(stage, side, lane_z)

    pl.when(jnp.logical_not(first))(open_vertical)
    launch(slice(0, 4))

    def z_lines(line, carry):
        i, j = line // 4, line % 4
        q = [[cv[v, i, j, pl.ds(8 * k, 8), :] for k in range(4)] for v in range(5)]
        flux = [[], [], [], [], []]
        for k in range(4):
            rho, mx, my, mz, energy = (q[v][k] for v in range(5))
            r, pressure, sound = primitive([q[v][k] for v in range(5)])
            vz = mz * r
            rows_k = pl.ds(8 * k, 8)
            prim[0, i, j, rows_k, :] = mx * r
            prim[1, i, j, rows_k, :] = my * r
            prim[2, i, j, rows_k, :] = vz
            prim[3, i, j, rows_k, :] = pressure
            prim[4, i, j, rows_k, :] = sound
            flux[0].append(mz)
            flux[1].append(mx * vz)
            flux[2].append(my * vz)
            flux[3].append(mz * vz + pressure)
            flux[4].append((energy + pressure) * vz)
        for v in range(5):
            out = derived(flux[v])
            for k in range(4):
                rows_k = pl.ds(8 * k, 8)
                acc[v, i, j, rows_k, :] = out[k]
        return carry

    lax.fori_loop(0, 16, z_lines, 0, unroll=4)


    def lines(direction, line, carry):
        a, k = line // 4, line % 4
        rows_k = pl.ds(pl.multiple_of(8 * k, 8), 8)

        def at(node):
            return (node, a, rows_k, slice(None)) if direction == 0 else (a, node, rows_k, slice(None))

        flux = [[], [], [], [], []]
        for node in range(4):
            vd = prim[(direction,) + at(node)]
            pressure = prim[(3,) + at(node)]
            m = [cv[(1 + c,) + at(node)] for c in range(3)]
            flux[0].append(m[direction])
            for c in range(3):
                entry = m[c] * vd
                if c == direction:
                    entry = entry + pressure
                flux[1 + c].append(entry)
            flux[4].append((cv[(4,) + at(node)] + pressure) * vd)
        for v in range(5):
            out = derived(flux[v])
            for node in range(4):
                total = acc[(v,) + at(node)] + out[node]
                if direction == 1:
                    total = total + SECTION_DECAY * regv[(v,) + at(node)]
                acc[(v,) + at(node)] = total
        return carry

    lax.fori_loop(0, 16, functools.partial(lines, 0), 0, unroll=4)
    reg_load.wait()
    lax.fori_loop(0, 16, functools.partial(lines, 1), 0, unroll=4)

    for side in range(4):
        hi, lo = split(trace_of(cv, side))
        select = jnp.where(here[(side ^ 1):(side ^ 1) + 1] == rows, 1.0, 0.0).astype(BF16)
        got = dot(jnp.concatenate([hi, lo], axis=0), select)
        got = got[:640] + got[640:]
        ghost[side ^ 1] = got.reshape(5, 4, 32, 256)

    lane_z3 = lax.broadcasted_iota(jnp.int32, (80, 8, 128), 2) // SLOTS
    sub_z3 = lax.broadcasted_iota(jnp.int32, (80, 8, 128), 1)
    for side in range(4):
        _, there, comes = sends[side]

        @pl.when(there)
        def _():
            copies[side].wait_send()

        @pl.when(comes)
        def _():
            copies[side].wait_recv()

        @pl.when(jnp.logical_not(comes))
        def _():
            arrived[side] = jnp.zeros((80, 128), F32)

        spread = jnp.where(lane_z3 == sub_z3, arrived[side][:, None, :], 0.0).reshape(640, 128)
        far_hi, far_lo = split(spread)
        both = jnp.concatenate([far_hi, far_lo], axis=1)
        twice = jnp.concatenate([picks[side], picks[side]], axis=0)
        got = ghost[side].reshape(640, 256) + dot(both, twice)
        own = trace_of(cv, side)
        kind = jnp.broadcast_to(kinds[side:side + 1], (128, 256))
        flip = jnp.where(kind == 1, -1.0, 1.0)
        for v in range(5):
            part = slice(128 * v, 128 * v + 128)
            inner = own[part] * flip if v == 1 + side // 2 else own[part]
            outer = jnp.where(kind == 0, got[part], jnp.where(kind == 2, FREE_STREAM[v], inner))
            ghost[side, v] = outer.reshape(4, 32, 256)

    for way in (0, 1):
        _, there, comes = sends[4 + way]

        @pl.when(there)
        def _():
            copies[4 + way].wait_send()

        @pl.when(comes)
        def _():
            copies[4 + way].wait_recv()

        @pl.when(jnp.logical_not(comes))
        def _():
            recvv[way] = jnp.zeros((80, 256), F32)

    for v in range(5):
        part = pl.ds(16 * v, 16)
        own = sendv[0, part, :]
        vert[0, part, :] = jnp.where(below, recvv[1, part, :], -own if v == 3 else own)
        vert[1, part, :] = jnp.where(above, recvv[0, part, :], jnp.full_like(own, FREE_STREAM[v]))


def surface_kernel(cv, acc, ghost, vert, prim, adv, new, adv_v, new_v, out_sem):
    sub = lax.broadcasted_iota(jnp.int32, (8, 128), 0)
    outs = []
    for i in range(4):

        def half(js, h, carry):
            lanes = pl.ds(pl.multiple_of(h * 128, 128), 128)
            for j in js:
                for k in range(4):
                    rows_k = pl.ds(8 * k, 8)
                    q = [cv[v, i, j, rows_k, lanes] for v in range(5)]
                    total = [acc[v, i, j, rows_k, lanes] for v in range(5)]
                    faces = []
                    if i in (0, 3):
                        faces.append((0, 0 if i == 0 else 1, (j, k)))
                    if j in (0, 3):
                        faces.append((1, 2 if j == 0 else 3, (i, k)))
                    if k in (0, 3):
                        faces.append((2, 4 if k == 0 else 5, (i, j)))
                    if faces:
                        p_in, c_in = (prim[v, i, j, rows_k, lanes] for v in (3, 4))
                    for d, side, (a, b) in faces:
                        if side < 4:
                            outer = [ghost[side, v, a, pl.ds(8 * b, 8), lanes] for v in range(5)]
                        else:
                            outer = []
                            for v in range(5):
                                m = v * 16 + a * 4 + b
                                if side == 4:
                                    near = cv[v, i, j, pl.ds(24, 8), lanes]
                                    near = pltpu.roll(near, 1, 0)
                                    edge = jnp.broadcast_to(vert[0, m:m + 1, lanes], (8, 128))
                                    outer.append(jnp.where(sub == 0, edge, near))
                                else:
                                    near = cv[v, i, j, pl.ds(0, 8), lanes]
                                    near = pltpu.roll(near, 7, 0)
                                    edge = jnp.broadcast_to(vert[1, m:m + 1, lanes], (8, 128))
                                    outer.append(jnp.where(sub == 7, edge, near))
                        sign = -1.0 if side % 2 == 0 else 1.0
                        r_out, p_out, c_out = primitive(outer)
                        v_in, v_out = prim[d, i, j, rows_k, lanes], outer[1 + d] * r_out
                        lam = LIFT * jnp.maximum(jnp.abs(v_in) + c_in, jnp.abs(v_out) + c_out)
                        s_in, s_out = (sign * LIFT) * v_in, (sign * LIFT) * v_out
                        w_in, w_out = lam - s_in, lam - s_out
                        for v in range(5):
                            total[v] = total[v] + (w_out * outer[v] - w_in * q[v])
                        total[1 + d] = total[1 + d] - (sign * LIFT) * (p_out - p_in)
                        total[4] = total[4] - (p_out * s_out - p_in * s_in)
                    for v in range(5):
                        new_v[v, i, j, rows_k, lanes] = total[v]
                        adv_v[v, i, j, rows_k, lanes] = q[v] + SECTION_WEIGHT * total[v]
            return carry

        for part in range(2):
            js = (2 * part, 2 * part + 1)
            lax.fori_loop(0, 2, functools.partial(half, js), 0)
            for n, (src, dst) in enumerate(((adv_v, adv), (new_v, new))):
                js_here = pl.ds(2 * part, 2)
                copy = pltpu.make_async_copy(src.at[:, i, js_here], dst.at[:, i, js_here], out_sem.at[n, 2 * i + part])
                copy.start()
                outs.append(copy)
    for copy in outs:
        copy.wait()


SHAPE = (5, 4, 4, 32, 256)


def per_device(conserved, register, neighbour, side_type):
    inputs = [
        pltpu.with_memory_space_constraint(x, pltpu.HBM)
        for x in (conserved.reshape(SHAPE), register.reshape(SHAPE), neighbour, side_type)
    ]
    handed = pl.pallas_call(
        exchange_kernel,
        name="exchange",
        out_shape=(
            pltpu.VMEM(SHAPE, F32),
            pltpu.VMEM(SHAPE, F32),
            pltpu.VMEM((4, 5, 4, 32, 256), F32),
            pltpu.VMEM((2, 80, 256), F32),
            pltpu.VMEM(SHAPE, F32),
        ),
        in_specs=[pl.BlockSpec(memory_space=pltpu.HBM)] * 4,
        out_specs=tuple([pl.BlockSpec(memory_space=pltpu.VMEM)] * 5),
        scratch_shapes=[
            pltpu.VMEM((4, 256), jnp.int32),
            pltpu.VMEM((4, 256), jnp.int32),
            pltpu.VMEM(SHAPE, F32),
            pltpu.VMEM((4, 128, 256), BF16),
            pltpu.VMEM((4, 128, 256), BF16),
            pltpu.VMEM((4, 256, 256), BF16),
            pltpu.VMEM((4, 640, 128), F32),
            pltpu.VMEM((4, 80, 128), F32),
            pltpu.VMEM((4, 80, 128), F32),
            pltpu.VMEM((2, 80, 256), F32),
            pltpu.VMEM((2, 80, 256), F32),
            pltpu.SemaphoreType.DMA((8,)),
            pltpu.SemaphoreType.DMA((4,)),
            pltpu.SemaphoreType.DMA((4,)),
            pltpu.SemaphoreType.DMA((2,)),
            pltpu.SemaphoreType.DMA((2,)),
        ],
        compiler_params=pltpu.CompilerParams(
            collective_id=0, has_side_effects=True, vmem_limit_bytes=40 * 1024 * 1024
        ),
    )(*inputs)
    handed = [pltpu.with_memory_space_constraint(x, pltpu.VMEM) for x in handed]
    adv, new = pl.pallas_call(
        surface_kernel,
        name="surface",
        out_shape=(jax.ShapeDtypeStruct(SHAPE, F32), jax.ShapeDtypeStruct(SHAPE, F32)),
        in_specs=[pl.BlockSpec(memory_space=pltpu.VMEM)] * 5,
        out_specs=(pl.BlockSpec(memory_space=pltpu.HBM), pl.BlockSpec(memory_space=pltpu.HBM)),
        scratch_shapes=[
            pltpu.VMEM(SHAPE, F32),
            pltpu.VMEM(SHAPE, F32),
            pltpu.SemaphoreType.DMA((2, 8)),
        ],
        compiler_params=pltpu.CompilerParams(vmem_limit_bytes=32 * 1024 * 1024),
    )(*handed)
    full = (5, 4, 4, 4, 8, 256)
    return adv.reshape(full), new.reshape(full)


def solution(mesh):
    spec = P(None, None, None, None, "layer", "foot")
    return jax.shard_map(
        per_device,
        mesh=mesh,
        in_specs=(spec, spec, P(None, "foot"), P(None, "foot")),
        out_specs=(spec, spec),
        check_vma=False,
    )
```

```python
import functools

import jax
import jax.numpy as jnp
import numpy as np
from jax import lax
from jax.experimental import pallas as pl
from jax.experimental.pallas import tpu as pltpu
from jax.sharding import PartitionSpec as P

TIME_STEP = 0.02
SECTION_DECAY = -0.4178904745
SECTION_WEIGHT = 1.720146321549
LIFT = 3.0 * TIME_STEP
FREE_STREAM = (1.0, 0.3, 0.1, 0.0, 1.0 / 0.56 + 0.05)
MESH = pl.DeviceIdType.MESH
SLOTS = 16
BF16 = jnp.bfloat16
F32 = jnp.float32
TILES_Y = 4


def derivative_entries():
    nodes = np.array([-1.0, -1.0 / np.sqrt(5.0), 1.0 / np.sqrt(5.0), 1.0])
    products = np.array(
        [np.prod([nodes[t] - nodes[a] for a in range(4) if a != t]) for t in range(4)]
    )
    matrix = np.zeros((4, 4))
    for t in range(4):
        for s in range(4):
            if t != s:
                matrix[t, s] = products[t] / products[s] / (nodes[t] - nodes[s])
            else:
                matrix[t, t] = sum(1.0 / (nodes[t] - nodes[a]) for a in range(4) if a != t)
    return matrix


ENTRIES = -TIME_STEP * derivative_entries()
ODD = [[0.5 * float(ENTRIES[p, i] - ENTRIES[p, 3 - i]) for i in (0, 1)] for p in (0, 1)]
EVEN = [0.5 * float(ENTRIES[p, 0] + ENTRIES[p, 3]) for p in (0, 1)]


def derived(f):
    s0, d0 = f[0] + f[3], f[0] - f[3]
    s1, d1 = f[1] + f[2], f[1] - f[2]
    t = s0 - s1
    a = ODD[0][0] * d0 + ODD[0][1] * d1
    b = EVEN[0] * t
    c = ODD[1][0] * d0 + ODD[1][1] * d1
    e = EVEN[1] * t
    return a + b, c + e, c - e, a - b


def inverse(x):
    r = pl.reciprocal(x, approx=True)
    return r * (2.0 - x * r)


def split(x):
    hi = x.astype(BF16)
    lo = (x - hi.astype(F32)).astype(BF16)
    return hi, lo


def dot(a, b):
    return jnp.dot(a, b, preferred_element_type=F32)


def dot_nt(a, b):
    return lax.dot_general(a, b, (((1,), (1,)), ((), ())), preferred_element_type=F32)


def face_rows(side):
    face = (0, 3)[side % 2]
    return (slice(None), face) if side < 2 else (slice(None), slice(None), face)


def trace_of(cv, side):
    return cv[face_rows(side)].reshape(640, 256)


def primitive(q):
    r = inverse(q[0])
    kinetic = (q[1] * q[1] + q[2] * q[2] + q[3] * q[3]) * r
    pressure = 0.4 * q[4] - 0.2 * kinetic
    square = 1.4 * pressure * r
    return r, pressure, square * lax.rsqrt(square)


def face_change(inner, outer, direction, sign, inner_known=None):
    if inner_known is None:
        r_in, p_in, c_in = primitive(inner)
        v_in = inner[1 + direction] * r_in
    else:
        v_in, p_in, c_in = inner_known
    r_out, p_out, c_out = primitive(outer)
    v_out = outer[1 + direction] * r_out
    lam = LIFT * jnp.maximum(jnp.abs(v_in) + c_in, jnp.abs(v_out) + c_out)
    s_in, s_out = (sign * LIFT) * v_in, (sign * LIFT) * v_out
    w_in, w_out = lam - s_in, lam - s_out
    change = [w_out * outer[v] - w_in * inner[v] for v in range(5)]
    change[1 + direction] = change[1 + direction] - (sign * LIFT) * (p_out - p_in)
    change[4] = change[4] - (p_out * s_out - p_in * s_in)
    return change


def gather_slots(stage, side, lane_z):
    total = stage[side, pl.ds(0, 80, stride=8), :]
    for z in range(1, 8):
        total = jnp.where(lane_z == z, stage[side, pl.ds(z, 80, stride=8), :], total)
    return total


def exchange_kernel(
    cons, reg, nb_in, kinds_in, cv, acc, ghost, vert, prim,
    nb, kinds, regv, picks, send_picks, selects, stage, packed, arrived, sendv, recvv,
    load_sem, send_sem, recv_sem, vsend_sem, vrecv_sem,
):
    foot, layer = lax.axis_index("foot"), lax.axis_index("layer")
    layers = lax.axis_size("layer")
    along, across = foot // TILES_Y, lax.rem(foot, TILES_Y)
    tiles = lax.axis_size("foot") // TILES_Y

    lower, upper = along > 0, along < tiles - 1
    left, right = across > 0, across < TILES_Y - 1
    below, above = layer > 0, layer < layers - 1
    sends = [
        ((foot + TILES_Y, layer), upper, lower),
        ((foot - TILES_Y, layer), lower, upper),
        ((foot + 1, layer), right, left),
        ((foot - 1, layer), left, right),
        ((foot, layer - 1), below, above),
        ((foot, layer + 1), above, below),
    ]

    barrier = pltpu.get_barrier_semaphore()
    partners = jnp.int32(0)
    for partner, there, _ in sends:
        partners = partners + there.astype(jnp.int32)

        @pl.when(there)
        def _():
            pl.semaphore_signal(barrier, inc=1, device_id=partner, device_id_type=MESH)

    nb_load = pltpu.make_async_copy(nb_in, nb, load_sem.at[6])
    nb_load.start()
    kinds_load = pltpu.make_async_copy(kinds_in, kinds, load_sem.at[7])
    kinds_load.start()
    loads = [
        pltpu.make_async_copy(cons.at[:, :, :, part], cv.at[:, :, :, part], load_sem.at[n])
        for n, part in enumerate((pl.ds(0, 8), pl.ds(24, 8), pl.ds(8, 16)))
    ]
    for copy in loads:
        copy.start()
    reg_load = pltpu.make_async_copy(reg, regv, load_sem.at[5])

    slot = lax.bitwise_and(lax.broadcasted_iota(jnp.int32, (128, 256), 0), SLOTS - 1)
    lane_z = lax.broadcasted_iota(jnp.int32, (80, 128), 1) // SLOTS
    rows = lax.broadcasted_iota(jnp.int32, (256, 256), 0)
    cols = lax.broadcasted_iota(jnp.int32, (256, 256), 1)
    before = jnp.where(rows < cols, 1.0, 0.0).astype(BF16)
    nb_load.wait()
    here = nb[...] - foot * 256
    away = jnp.logical_or(here < 0, here >= 256)
    mask = jnp.where(away, 1.0, 0.0)
    mask8 = jnp.concatenate([mask, jnp.zeros_like(mask)], axis=0).astype(BF16)
    rank = jnp.where(away, dot(mask8, before)[0:4], -1.0).astype(jnp.int32)

    for way in (0, 1):
        loads[way].wait()
        for h in (0, 1):
            lanes = pl.ds(h * 128, 128)
            stage[2 * way + h] = cv[:, :, :, pl.ds(24 * way, 8), lanes].reshape(640, 128)
            sendv[way, :, lanes] = stage[2 * way + h, pl.ds(7 * way, 80, stride=8), :]

    copies = []
    for side in range(4):
        copies.append(pltpu.make_async_remote_copy(
            src_ref=packed.at[side], dst_ref=arrived.at[side], send_sem=send_sem.at[side],
            recv_sem=recv_sem.at[side], device_id=sends[side][0], device_id_type=MESH,
        ))
    for way in (0, 1):
        copies.append(pltpu.make_async_remote_copy(
            src_ref=sendv.at[way], dst_ref=recvv.at[way], send_sem=vsend_sem.at[way],
            recv_sem=vrecv_sem.at[way], device_id=sends[4 + way][0], device_id_type=MESH,
        ))
    def launch(which):
        for copy, (_, there, _) in list(zip(copies, sends))[which]:

            @pl.when(there)
            def _():
                copy.start()


    names = jnp.where(away, lax.bitwise_and(nb[...], 255), 1000).astype(F32)
    names_down = jnp.transpose(jnp.concatenate([names, names], axis=0))
    for side in range(4):
        less = jnp.where(names_down[:, side:side + 1] < names[side:side + 1], 1.0, 0.0)
        order = jnp.sum(less, axis=0, keepdims=True)
        order = jnp.where(away[side:side + 1], order, -1.0).astype(jnp.int32)
        picks[side] = jnp.where(order == slot, 1.0, 0.0).astype(BF16)

    kinds_load.wait()
    loads[2].wait()
    reg_load.start()

    def open_vertical():
        pl.semaphore_wait(barrier, partners)
        launch(slice(4, 6))

    late = along == tiles // 2 - 1
    first = jnp.logical_and(layer == layers // 2 - 1, jnp.logical_not(late))
    second = jnp.logical_not(jnp.logical_or(first, late))
    pl.when(first)(open_vertical)

    for side in range(4):
        hi, lo = split(trace_of(cv, side))
        send = jnp.where(rank[side:side + 1] == slot, 1.0, 0.0).astype(BF16)
        stage[side] = dot_nt(hi, send) + dot_nt(lo, send)
        packed[side ^ 1] = gather_slots(stage, side, lane_z)

    pl.when(second)(open_vertical)

    @pl.when(jnp.logical_not(late))
    def _():
        launch(slice(0, 4))


    def z_lines(line, carry):
        i, j = line // 4, line % 4
        q = [[cv[v, i, j, pl.ds(8 * k, 8), :] for k in range(4)] for v in range(5)]
        flux = [[], [], [], [], []]
        for k in range(4):
            rho, mx, my, mz, energy = (q[v][k] for v in range(5))
            r, pressure, sound = primitive([q[v][k] for v in range(5)])
            vz = mz * r
            rows_k = pl.ds(8 * k, 8)
            prim[0, i, j, rows_k, :] = mx * r
            prim[1, i, j, rows_k, :] = my * r
            prim[2, i, j, rows_k, :] = vz
            prim[3, i, j, rows_k, :] = pressure
            prim[4, i, j, rows_k, :] = sound
            flux[0].append(mz)
            flux[1].append(mx * vz)
            flux[2].append(my * vz)
            flux[3].append(mz * vz + pressure)
            flux[4].append((energy + pressure) * vz)
        for v in range(5):
            out = derived(flux[v])
            for k in range(4):
                rows_k = pl.ds(8 * k, 8)
                acc[v, i, j, rows_k, :] = out[k]
        return carry

    lax.fori_loop(0, 16, z_lines, 0, unroll=4)

    @pl.when(late)
    def _():
        open_vertical()
        launch(slice(0, 4))


    def lines(direction, line, carry):
        a, k = line // 4, line % 4
        rows_k = pl.ds(pl.multiple_of(8 * k, 8), 8)

        def at(node):
            return (node, a, rows_k, slice(None)) if direction == 0 else (a, node, rows_k, slice(None))

        flux = [[], [], [], [], []]
        for node in range(4):
            vd = prim[(direction,) + at(node)]
            pressure = prim[(3,) + at(node)]
            m = [cv[(1 + c,) + at(node)] for c in range(3)]
            flux[0].append(m[direction])
            for c in range(3):
                entry = m[c] * vd
                if c == direction:
                    entry = entry + pressure
                flux[1 + c].append(entry)
            flux[4].append((cv[(4,) + at(node)] + pressure) * vd)
        for v in range(5):
            out = derived(flux[v])
            for node in range(4):
                total = acc[(v,) + at(node)] + out[node]
                if direction == 1:
                    total = total + SECTION_DECAY * regv[(v,) + at(node)]
                acc[(v,) + at(node)] = total
        return carry

    lax.fori_loop(0, 16, functools.partial(lines, 0), 0, unroll=4)
    reg_load.wait()
    lax.fori_loop(0, 16, functools.partial(lines, 1), 0, unroll=4)

    for side in range(4):
        hi, lo = split(trace_of(cv, side))
        select = jnp.where(here[(side ^ 1):(side ^ 1) + 1] == rows, 1.0, 0.0).astype(BF16)
        got = dot(jnp.concatenate([hi, lo], axis=0), select)
        got = got[:640] + got[640:]
        ghost[side ^ 1] = got.reshape(5, 4, 32, 256)

    lane_z3 = lax.broadcasted_iota(jnp.int32, (80, 8, 128), 2) // SLOTS
    sub_z3 = lax.broadcasted_iota(jnp.int32, (80, 8, 128), 1)
    for side in range(4):
        _, there, comes = sends[side]

        @pl.when(there)
        def _():
            copies[side].wait_send()

        @pl.when(comes)
        def _():
            copies[side].wait_recv()

        @pl.when(jnp.logical_not(comes))
        def _():
            arrived[side] = jnp.zeros((80, 128), F32)

        spread = jnp.where(lane_z3 == sub_z3, arrived[side][:, None, :], 0.0).reshape(640, 128)
        far_hi, far_lo = split(spread)
        both = jnp.concatenate([far_hi, far_lo], axis=1)
        twice = jnp.concatenate([picks[side], picks[side]], axis=0)
        got = ghost[side].reshape(640, 256) + dot(both, twice)
        own = trace_of(cv, side)
        kind = jnp.broadcast_to(kinds[side:side + 1], (128, 256))
        flip = jnp.where(kind == 1, -1.0, 1.0)
        for v in range(5):
            part = slice(128 * v, 128 * v + 128)
            inner = own[part] * flip if v == 1 + side // 2 else own[part]
            outer = jnp.where(kind == 0, got[part], jnp.where(kind == 2, FREE_STREAM[v], inner))
            ghost[side, v] = outer.reshape(4, 32, 256)

    for side in (0, 1):
        face, sign = 3 * side, 2.0 * side - 1.0

        def x_face(node, carry):
            a, b = node // 4, node % 4
            rows_b = pl.ds(pl.multiple_of(8 * b, 8), 8)
            at = (face, a, rows_b, slice(None))
            q = [cv[(v,) + at] for v in range(5)]
            outer = [ghost[side, v, a, rows_b, :] for v in range(5)]
            known = prim[(0,) + at], prim[(3,) + at], prim[(4,) + at]
            change = face_change(q, outer, 0, sign, known)
            for v in range(5):
                acc[(v,) + at] = acc[(v,) + at] + change[v]
            return carry

        lax.fori_loop(0, 16, x_face, 0, unroll=4)

    for way in (0, 1):
        _, there, comes = sends[4 + way]

        @pl.when(there)
        def _():
            copies[4 + way].wait_send()

        @pl.when(comes)
        def _():
            copies[4 + way].wait_recv()

        @pl.when(jnp.logical_not(comes))
        def _():
            recvv[way] = jnp.zeros((80, 256), F32)

    for v in range(5):
        part = pl.ds(16 * v, 16)
        own = sendv[0, part, :]
        vert[0, part, :] = jnp.where(below, recvv[1, part, :], -own if v == 3 else own)
        vert[1, part, :] = jnp.where(above, recvv[0, part, :], jnp.full_like(own, FREE_STREAM[v]))


def surface_kernel(cv, acc, ghost, vert, prim, adv, new, adv_v, new_v, out_sem):
    sub = lax.broadcasted_iota(jnp.int32, (8, 128), 0)
    outs = []
    for i in range(4):

        def half(js, h, carry):
            lanes = pl.ds(pl.multiple_of(h * 128, 128), 128)
            for j in js:
                for k in range(4):
                    rows_k = pl.ds(8 * k, 8)
                    q = [cv[v, i, j, rows_k, lanes] for v in range(5)]
                    total = [acc[v, i, j, rows_k, lanes] for v in range(5)]
                    faces = []
                    if j in (0, 3):
                        faces.append((1, 2 if j == 0 else 3, (i, k)))
                    if k in (0, 3):
                        faces.append((2, 4 if k == 0 else 5, (i, j)))
                    if faces:
                        p_in, c_in = (prim[v, i, j, rows_k, lanes] for v in (3, 4))
                    for d, side, (a, b) in faces:
                        if side < 4:
                            outer = [ghost[side, v, a, pl.ds(8 * b, 8), lanes] for v in range(5)]
                        else:
                            outer = []
                            for v in range(5):
                                m = v * 16 + a * 4 + b
                                if side == 4:
                                    near = cv[v, i, j, pl.ds(24, 8), lanes]
                                    near = pltpu.roll(near, 1, 0)
                                    edge = jnp.broadcast_to(vert[0, m:m + 1, lanes], (8, 128))
                                    outer.append(jnp.where(sub == 0, edge, near))
                                else:
                                    near = cv[v, i, j, pl.ds(0, 8), lanes]
                                    near = pltpu.roll(near, 7, 0)
                                    edge = jnp.broadcast_to(vert[1, m:m + 1, lanes], (8, 128))
                                    outer.append(jnp.where(sub == 7, edge, near))
                        sign = -1.0 if side % 2 == 0 else 1.0
                        r_out, p_out, c_out = primitive(outer)
                        v_in, v_out = prim[d, i, j, rows_k, lanes], outer[1 + d] * r_out
                        lam = LIFT * jnp.maximum(jnp.abs(v_in) + c_in, jnp.abs(v_out) + c_out)
                        s_in, s_out = (sign * LIFT) * v_in, (sign * LIFT) * v_out
                        w_in, w_out = lam - s_in, lam - s_out
                        for v in range(5):
                            total[v] = total[v] + (w_out * outer[v] - w_in * q[v])
                        total[1 + d] = total[1 + d] - (sign * LIFT) * (p_out - p_in)
                        total[4] = total[4] - (p_out * s_out - p_in * s_in)
                    for v in range(5):
                        new_v[v, i, j, rows_k, lanes] = total[v]
                        adv_v[v, i, j, rows_k, lanes] = q[v] + SECTION_WEIGHT * total[v]
            return carry

        for part in range(2):
            js = (2 * part, 2 * part + 1)
            lax.fori_loop(0, 2, functools.partial(half, js), 0)
            for n, (src, dst) in enumerate(((adv_v, adv), (new_v, new))):
                js_here = pl.ds(2 * part, 2)
                copy = pltpu.make_async_copy(src.at[:, i, js_here], dst.at[:, i, js_here], out_sem.at[n, 2 * i + part])
                copy.start()
                outs.append(copy)
    for copy in outs:
        copy.wait()


SHAPE = (5, 4, 4, 32, 256)


def per_device(conserved, register, neighbour, side_type):
    inputs = [
        pltpu.with_memory_space_constraint(x, pltpu.HBM)
        for x in (conserved.reshape(SHAPE), register.reshape(SHAPE), neighbour, side_type)
    ]
    handed = pl.pallas_call(
        exchange_kernel,
        name="exchange",
        out_shape=(
            pltpu.VMEM(SHAPE, F32),
            pltpu.VMEM(SHAPE, F32),
            pltpu.VMEM((4, 5, 4, 32, 256), F32),
            pltpu.VMEM((2, 80, 256), F32),
            pltpu.VMEM(SHAPE, F32),
        ),
        in_specs=[pl.BlockSpec(memory_space=pltpu.HBM)] * 4,
        out_specs=tuple([pl.BlockSpec(memory_space=pltpu.VMEM)] * 5),
        scratch_shapes=[
            pltpu.VMEM((4, 256), jnp.int32),
            pltpu.VMEM((4, 256), jnp.int32),
            pltpu.VMEM(SHAPE, F32),
            pltpu.VMEM((4, 128, 256), BF16),
            pltpu.VMEM((4, 128, 256), BF16),
            pltpu.VMEM((4, 256, 256), BF16),
            pltpu.VMEM((4, 640, 128), F32),
            pltpu.VMEM((4, 80, 128), F32),
            pltpu.VMEM((4, 80, 128), F32),
            pltpu.VMEM((2, 80, 256), F32),
            pltpu.VMEM((2, 80, 256), F32),
            pltpu.SemaphoreType.DMA((8,)),
            pltpu.SemaphoreType.DMA((4,)),
            pltpu.SemaphoreType.DMA((4,)),
            pltpu.SemaphoreType.DMA((2,)),
            pltpu.SemaphoreType.DMA((2,)),
        ],
        compiler_params=pltpu.CompilerParams(
            collective_id=0, has_side_effects=True, vmem_limit_bytes=40 * 1024 * 1024
        ),
    )(*inputs)
    handed = [pltpu.with_memory_space_constraint(x, pltpu.VMEM) for x in handed]
    adv, new = pl.pallas_call(
        surface_kernel,
        name="surface",
        out_shape=(jax.ShapeDtypeStruct(SHAPE, F32), jax.ShapeDtypeStruct(SHAPE, F32)),
        in_specs=[pl.BlockSpec(memory_space=pltpu.VMEM)] * 5,
        out_specs=(pl.BlockSpec(memory_space=pltpu.HBM), pl.BlockSpec(memory_space=pltpu.HBM)),
        scratch_shapes=[
            pltpu.VMEM(SHAPE, F32),
            pltpu.VMEM(SHAPE, F32),
            pltpu.SemaphoreType.DMA((2, 8)),
        ],
        compiler_params=pltpu.CompilerParams(vmem_limit_bytes=32 * 1024 * 1024),
    )(*handed)
    full = (5, 4, 4, 4, 8, 256)
    return adv.reshape(full), new.reshape(full)


def solution(mesh):
    spec = P(None, None, None, None, "layer", "foot")
    return jax.shard_map(
        per_device,
        mesh=mesh,
        in_specs=(spec, spec, P(None, "foot"), P(None, "foot")),
        out_specs=(spec, spec),
        check_vma=False,
    )
```

```python
import functools

import jax
import jax.numpy as jnp
import numpy as np
from jax import lax
from jax.experimental import pallas as pl
from jax.experimental.pallas import tpu as pltpu
from jax.sharding import PartitionSpec as P

TIME_STEP = 0.02
SECTION_DECAY = -0.4178904745
SECTION_WEIGHT = 1.720146321549
LIFT = 3.0 * TIME_STEP
FREE_STREAM = (1.0, 0.3, 0.1, 0.0, 1.0 / 0.56 + 0.05)
MESH = pl.DeviceIdType.MESH
SLOTS = 16
BF16 = jnp.bfloat16
F32 = jnp.float32
TILES_Y = 4


def derivative_entries():
    nodes = np.array([-1.0, -1.0 / np.sqrt(5.0), 1.0 / np.sqrt(5.0), 1.0])
    products = np.array(
        [np.prod([nodes[t] - nodes[a] for a in range(4) if a != t]) for t in range(4)]
    )
    matrix = np.zeros((4, 4))
    for t in range(4):
        for s in range(4):
            if t != s:
                matrix[t, s] = products[t] / products[s] / (nodes[t] - nodes[s])
            else:
                matrix[t, t] = sum(1.0 / (nodes[t] - nodes[a]) for a in range(4) if a != t)
    return matrix


ENTRIES = -TIME_STEP * derivative_entries()
ODD = [[0.5 * float(ENTRIES[p, i] - ENTRIES[p, 3 - i]) for i in (0, 1)] for p in (0, 1)]
EVEN = [0.5 * float(ENTRIES[p, 0] + ENTRIES[p, 3]) for p in (0, 1)]


def derived(f):
    s0, d0 = f[0] + f[3], f[0] - f[3]
    s1, d1 = f[1] + f[2], f[1] - f[2]
    t = s0 - s1
    a = ODD[0][0] * d0 + ODD[0][1] * d1
    b = EVEN[0] * t
    c = ODD[1][0] * d0 + ODD[1][1] * d1
    e = EVEN[1] * t
    return a + b, c + e, c - e, a - b


def inverse(x):
    r = pl.reciprocal(x, approx=True)
    return r * (2.0 - x * r)


def split(x):
    hi = x.astype(BF16)
    lo = (x - hi.astype(F32)).astype(BF16)
    return hi, lo


def dot(a, b):
    return jnp.dot(a, b, preferred_element_type=F32)


def dot_nt(a, b):
    return lax.dot_general(a, b, (((1,), (1,)), ((), ())), preferred_element_type=F32)


def face_rows(side):
    face = (0, 3)[side % 2]
    return (slice(None), face) if side < 2 else (slice(None), slice(None), face)


def trace_of(cv, side):
    return cv[face_rows(side)].reshape(640, 256)


def primitive(q):
    r = inverse(q[0])
    kinetic = (q[1] * q[1] + q[2] * q[2] + q[3] * q[3]) * r
    pressure = 0.4 * q[4] - 0.2 * kinetic
    square = 1.4 * pressure * r
    return r, pressure, square * lax.rsqrt(square)


def face_change(inner, outer, direction, sign, inner_known=None):
    if inner_known is None:
        r_in, p_in, c_in = primitive(inner)
        v_in = inner[1 + direction] * r_in
    else:
        v_in, p_in, c_in = inner_known
    r_out, p_out, c_out = primitive(outer)
    v_out = outer[1 + direction] * r_out
    lam = LIFT * jnp.maximum(jnp.abs(v_in) + c_in, jnp.abs(v_out) + c_out)
    s_in, s_out = (sign * LIFT) * v_in, (sign * LIFT) * v_out
    w_in, w_out = lam - s_in, lam - s_out
    change = [w_out * outer[v] - w_in * inner[v] for v in range(5)]
    change[1 + direction] = change[1 + direction] - (sign * LIFT) * (p_out - p_in)
    change[4] = change[4] - (p_out * s_out - p_in * s_in)
    return change


def gather_slots(stage, side, lane_z):
    total = stage[side, pl.ds(0, 80, stride=8), :]
    for z in range(1, 8):
        total = jnp.where(lane_z == z, stage[side, pl.ds(z, 80, stride=8), :], total)
    return total


def exchange_kernel(
    cons, reg, nb_in, kinds_in, cv, acc, ghost, vert, prim,
    nb, kinds, regv, picks, send_picks, selects, stage, packed, arrived, sendv, recvv,
    load_sem, send_sem, recv_sem, vsend_sem, vrecv_sem,
):
    foot, layer = lax.axis_index("foot"), lax.axis_index("layer")
    layers = lax.axis_size("layer")
    along, across = foot // TILES_Y, lax.rem(foot, TILES_Y)
    tiles = lax.axis_size("foot") // TILES_Y

    lower, upper = along > 0, along < tiles - 1
    left, right = across > 0, across < TILES_Y - 1
    below, above = layer > 0, layer < layers - 1
    sends = [
        ((foot + TILES_Y, layer), upper, lower),
        ((foot - TILES_Y, layer), lower, upper),
        ((foot + 1, layer), right, left),
        ((foot - 1, layer), left, right),
        ((foot, layer - 1), below, above),
        ((foot, layer + 1), above, below),
    ]

    barrier = pltpu.get_barrier_semaphore()
    partners = jnp.int32(0)
    for partner, there, _ in sends:
        partners = partners + there.astype(jnp.int32)

        @pl.when(there)
        def _():
            pl.semaphore_signal(barrier, inc=1, device_id=partner, device_id_type=MESH)

    nb_load = pltpu.make_async_copy(nb_in, nb, load_sem.at[6])
    nb_load.start()
    kinds_load = pltpu.make_async_copy(kinds_in, kinds, load_sem.at[7])
    kinds_load.start()
    loads = [
        pltpu.make_async_copy(cons.at[:, :, :, part], cv.at[:, :, :, part], load_sem.at[n])
        for n, part in enumerate((pl.ds(0, 8), pl.ds(24, 8), pl.ds(8, 16)))
    ]
    for copy in loads:
        copy.start()
    reg_load = pltpu.make_async_copy(reg, regv, load_sem.at[5])

    slot = lax.bitwise_and(lax.broadcasted_iota(jnp.int32, (128, 256), 0), SLOTS - 1)
    lane_z = lax.broadcasted_iota(jnp.int32, (80, 128), 1) // SLOTS
    rows = lax.broadcasted_iota(jnp.int32, (256, 256), 0)
    cols = lax.broadcasted_iota(jnp.int32, (256, 256), 1)
    before = jnp.where(rows < cols, 1.0, 0.0).astype(BF16)
    nb_load.wait()
    here = nb[...] - foot * 256
    away = jnp.logical_or(here < 0, here >= 256)
    mask = jnp.where(away, 1.0, 0.0)
    mask8 = jnp.concatenate([mask, jnp.zeros_like(mask)], axis=0).astype(BF16)
    rank = jnp.where(away, dot(mask8, before)[0:4], -1.0).astype(jnp.int32)

    for way in (0, 1):
        loads[way].wait()
        for h in (0, 1):
            lanes = pl.ds(h * 128, 128)
            stage[2 * way + h] = cv[:, :, :, pl.ds(24 * way, 8), lanes].reshape(640, 128)
            sendv[way, :, lanes] = stage[2 * way + h, pl.ds(7 * way, 80, stride=8), :]

    copies = []
    for side in range(4):
        copies.append(pltpu.make_async_remote_copy(
            src_ref=packed.at[side], dst_ref=arrived.at[side], send_sem=send_sem.at[side],
            recv_sem=recv_sem.at[side], device_id=sends[side][0], device_id_type=MESH,
        ))
    for way in (0, 1):
        copies.append(pltpu.make_async_remote_copy(
            src_ref=sendv.at[way], dst_ref=recvv.at[way], send_sem=vsend_sem.at[way],
            recv_sem=vrecv_sem.at[way], device_id=sends[4 + way][0], device_id_type=MESH,
        ))
    def launch(which):
        for copy, (_, there, _) in list(zip(copies, sends))[which]:

            @pl.when(there)
            def _():
                copy.start()


    names = jnp.where(away, lax.bitwise_and(nb[...], 255), 1000).astype(F32)
    names_down = jnp.transpose(jnp.concatenate([names, names], axis=0))
    for side in range(4):
        less = jnp.where(names_down[:, side:side + 1] < names[side:side + 1], 1.0, 0.0)
        order = jnp.sum(less, axis=0, keepdims=True)
        order = jnp.where(away[side:side + 1], order, -1.0).astype(jnp.int32)
        picks[side] = jnp.where(order == slot, 1.0, 0.0).astype(BF16)

    kinds_load.wait()
    loads[2].wait()
    reg_load.start()

    def open_vertical():
        pl.semaphore_wait(barrier, partners)
        launch(slice(4, 6))

    late = along == tiles // 2 - 1
    first = jnp.logical_and(layer == layers // 2 - 1, jnp.logical_not(late))
    pl.when(first)(open_vertical)

    for side in range(4):
        hi, lo = split(trace_of(cv, side))
        send = jnp.where(rank[side:side + 1] == slot, 1.0, 0.0).astype(BF16)
        stage[side] = dot_nt(hi, send) + dot_nt(lo, send)
        packed[side ^ 1] = gather_slots(stage, side, lane_z)

    pl.when(jnp.logical_not(first))(open_vertical)
    launch(slice(0, 4))


    def z_lines(line, carry):
        i, j = line // 4, line % 4
        q = [[cv[v, i, j, pl.ds(8 * k, 8), :] for k in range(4)] for v in range(5)]
        flux = [[], [], [], [], []]
        for k in range(4):
            rho, mx, my, mz, energy = (q[v][k] for v in range(5))
            r, pressure, sound = primitive([q[v][k] for v in range(5)])
            vz = mz * r
            rows_k = pl.ds(8 * k, 8)
            prim[0, i, j, rows_k, :] = mx * r
            prim[1, i, j, rows_k, :] = my * r
            prim[2, i, j, rows_k, :] = vz
            prim[3, i, j, rows_k, :] = pressure
            prim[4, i, j, rows_k, :] = sound
            flux[0].append(mz)
            flux[1].append(mx * vz)
            flux[2].append(my * vz)
            flux[3].append(mz * vz + pressure)
            flux[4].append((energy + pressure) * vz)
        for v in range(5):
            out = derived(flux[v])
            for k in range(4):
                rows_k = pl.ds(8 * k, 8)
                acc[v, i, j, rows_k, :] = out[k]
        return carry

    lax.fori_loop(0, 16, z_lines, 0, unroll=4)


    def lines(direction, line, carry):
        a, k = line // 4, line % 4
        rows_k = pl.ds(pl.multiple_of(8 * k, 8), 8)

        def at(node):
            return (node, a, rows_k, slice(None)) if direction == 0 else (a, node, rows_k, slice(None))

        flux = [[], [], [], [], []]
        for node in range(4):
            vd = prim[(direction,) + at(node)]
            pressure = prim[(3,) + at(node)]
            m = [cv[(1 + c,) + at(node)] for c in range(3)]
            flux[0].append(m[direction])
            for c in range(3):
                entry = m[c] * vd
                if c == direction:
                    entry = entry + pressure
                flux[1 + c].append(entry)
            flux[4].append((cv[(4,) + at(node)] + pressure) * vd)
        for v in range(5):
            out = derived(flux[v])
            for node in range(4):
                total = acc[(v,) + at(node)] + out[node]
                if direction == 1:
                    total = total + SECTION_DECAY * regv[(v,) + at(node)]
                acc[(v,) + at(node)] = total
        return carry

    lax.fori_loop(0, 16, functools.partial(lines, 0), 0, unroll=4)
    reg_load.wait()
    lax.fori_loop(0, 16, functools.partial(lines, 1), 0, unroll=4)

    for side in range(4):
        hi, lo = split(trace_of(cv, side))
        select = jnp.where(here[(side ^ 1):(side ^ 1) + 1] == rows, 1.0, 0.0).astype(BF16)
        got = dot(jnp.concatenate([hi, lo], axis=0), select)
        got = got[:640] + got[640:]
        ghost[side ^ 1] = got.reshape(5, 4, 32, 256)

    lane_z3 = lax.broadcasted_iota(jnp.int32, (80, 8, 128), 2) // SLOTS
    sub_z3 = lax.broadcasted_iota(jnp.int32, (80, 8, 128), 1)
    for side in range(4):
        _, there, comes = sends[side]

        @pl.when(there)
        def _():
            copies[side].wait_send()

        @pl.when(comes)
        def _():
            copies[side].wait_recv()

        @pl.when(jnp.logical_not(comes))
        def _():
            arrived[side] = jnp.zeros((80, 128), F32)

        spread = jnp.where(lane_z3 == sub_z3, arrived[side][:, None, :], 0.0).reshape(640, 128)
        far_hi, far_lo = split(spread)
        both = jnp.concatenate([far_hi, far_lo], axis=1)
        twice = jnp.concatenate([picks[side], picks[side]], axis=0)
        got = ghost[side].reshape(640, 256) + dot(both, twice)
        own = trace_of(cv, side)
        kind = jnp.broadcast_to(kinds[side:side + 1], (128, 256))
        flip = jnp.where(kind == 1, -1.0, 1.0)
        for v in range(5):
            part = slice(128 * v, 128 * v + 128)
            inner = own[part] * flip if v == 1 + side // 2 else own[part]
            outer = jnp.where(kind == 0, got[part], jnp.where(kind == 2, FREE_STREAM[v], inner))
            ghost[side, v] = outer.reshape(4, 32, 256)

    for side in (0, 1):
        face, sign = 3 * side, 2.0 * side - 1.0

        def x_face(node, carry):
            a, b = node // 4, node % 4
            rows_b = pl.ds(pl.multiple_of(8 * b, 8), 8)
            at = (face, a, rows_b, slice(None))
            q = [cv[(v,) + at] for v in range(5)]
            outer = [ghost[side, v, a, rows_b, :] for v in range(5)]
            known = prim[(0,) + at], prim[(3,) + at], prim[(4,) + at]
            change = face_change(q, outer, 0, sign, known)
            for v in range(5):
                acc[(v,) + at] = acc[(v,) + at] + change[v]
            return carry

        lax.fori_loop(0, 16, x_face, 0, unroll=4)

    for way in (0, 1):
        _, there, comes = sends[4 + way]

        @pl.when(there)
        def _():
            copies[4 + way].wait_send()

        @pl.when(comes)
        def _():
            copies[4 + way].wait_recv()

        @pl.when(jnp.logical_not(comes))
        def _():
            recvv[way] = jnp.zeros((80, 256), F32)

    for v in range(5):
        part = pl.ds(16 * v, 16)
        own = sendv[0, part, :]
        vert[0, part, :] = jnp.where(below, recvv[1, part, :], -own if v == 3 else own)
        vert[1, part, :] = jnp.where(above, recvv[0, part, :], jnp.full_like(own, FREE_STREAM[v]))


def surface_kernel(cv, acc, ghost, vert, prim, adv, new, adv_v, new_v, out_sem):
    sub = lax.broadcasted_iota(jnp.int32, (8, 128), 0)
    outs = []
    for i in range(4):

        def half(js, h, carry):
            lanes = pl.ds(pl.multiple_of(h * 128, 128), 128)
            for j in js:
                for k in range(4):
                    rows_k = pl.ds(8 * k, 8)
                    q = [cv[v, i, j, rows_k, lanes] for v in range(5)]
                    total = [acc[v, i, j, rows_k, lanes] for v in range(5)]
                    faces = []
                    if j in (0, 3):
                        faces.append((1, 2 if j == 0 else 3, (i, k)))
                    if k in (0, 3):
                        faces.append((2, 4 if k == 0 else 5, (i, j)))
                    if faces:
                        p_in, c_in = (prim[v, i, j, rows_k, lanes] for v in (3, 4))
                    for d, side, (a, b) in faces:
                        if side < 4:
                            outer = [ghost[side, v, a, pl.ds(8 * b, 8), lanes] for v in range(5)]
                        else:
                            outer = []
                            for v in range(5):
                                m = v * 16 + a * 4 + b
                                if side == 4:
                                    near = cv[v, i, j, pl.ds(24, 8), lanes]
                                    near = pltpu.roll(near, 1, 0)
                                    edge = jnp.broadcast_to(vert[0, m:m + 1, lanes], (8, 128))
                                    outer.append(jnp.where(sub == 0, edge, near))
                                else:
                                    near = cv[v, i, j, pl.ds(0, 8), lanes]
                                    near = pltpu.roll(near, 7, 0)
                                    edge = jnp.broadcast_to(vert[1, m:m + 1, lanes], (8, 128))
                                    outer.append(jnp.where(sub == 7, edge, near))
                        sign = -1.0 if side % 2 == 0 else 1.0
                        r_out, p_out, c_out = primitive(outer)
                        v_in, v_out = prim[d, i, j, rows_k, lanes], outer[1 + d] * r_out
                        lam = LIFT * jnp.maximum(jnp.abs(v_in) + c_in, jnp.abs(v_out) + c_out)
                        s_in, s_out = (sign * LIFT) * v_in, (sign * LIFT) * v_out
                        w_in, w_out = lam - s_in, lam - s_out
                        for v in range(5):
                            total[v] = total[v] + (w_out * outer[v] - w_in * q[v])
                        total[1 + d] = total[1 + d] - (sign * LIFT) * (p_out - p_in)
                        total[4] = total[4] - (p_out * s_out - p_in * s_in)
                    for v in range(5):
                        new_v[v, i, j, rows_k, lanes] = total[v]
                        adv_v[v, i, j, rows_k, lanes] = q[v] + SECTION_WEIGHT * total[v]
            return carry

        for part in range(2):
            js = (2 * part, 2 * part + 1)
            lax.fori_loop(0, 2, functools.partial(half, js), 0)
            for n, (src, dst) in enumerate(((adv_v, adv), (new_v, new))):
                js_here = pl.ds(2 * part, 2)
                copy = pltpu.make_async_copy(src.at[:, i, js_here], dst.at[:, i, js_here], out_sem.at[n, 2 * i + part])
                copy.start()
                outs.append(copy)
    for copy in outs:
        copy.wait()


SHAPE = (5, 4, 4, 32, 256)


def per_device(conserved, register, neighbour, side_type):
    inputs = [
        pltpu.with_memory_space_constraint(x, pltpu.HBM)
        for x in (conserved.reshape(SHAPE), register.reshape(SHAPE), neighbour, side_type)
    ]
    handed = pl.pallas_call(
        exchange_kernel,
        name="exchange",
        out_shape=(
            pltpu.VMEM(SHAPE, F32),
            pltpu.VMEM(SHAPE, F32),
            pltpu.VMEM((4, 5, 4, 32, 256), F32),
            pltpu.VMEM((2, 80, 256), F32),
            pltpu.VMEM(SHAPE, F32),
        ),
        in_specs=[pl.BlockSpec(memory_space=pltpu.HBM)] * 4,
        out_specs=tuple([pl.BlockSpec(memory_space=pltpu.VMEM)] * 5),
        scratch_shapes=[
            pltpu.VMEM((4, 256), jnp.int32),
            pltpu.VMEM((4, 256), jnp.int32),
            pltpu.VMEM(SHAPE, F32),
            pltpu.VMEM((4, 128, 256), BF16),
            pltpu.VMEM((4, 128, 256), BF16),
            pltpu.VMEM((4, 256, 256), BF16),
            pltpu.VMEM((4, 640, 128), F32),
            pltpu.VMEM((4, 80, 128), F32),
            pltpu.VMEM((4, 80, 128), F32),
            pltpu.VMEM((2, 80, 256), F32),
            pltpu.VMEM((2, 80, 256), F32),
            pltpu.SemaphoreType.DMA((8,)),
            pltpu.SemaphoreType.DMA((4,)),
            pltpu.SemaphoreType.DMA((4,)),
            pltpu.SemaphoreType.DMA((2,)),
            pltpu.SemaphoreType.DMA((2,)),
        ],
        compiler_params=pltpu.CompilerParams(
            collective_id=0, has_side_effects=True, vmem_limit_bytes=40 * 1024 * 1024
        ),
    )(*inputs)
    handed = [pltpu.with_memory_space_constraint(x, pltpu.VMEM) for x in handed]
    adv, new = pl.pallas_call(
        surface_kernel,
        name="surface",
        out_shape=(jax.ShapeDtypeStruct(SHAPE, F32), jax.ShapeDtypeStruct(SHAPE, F32)),
        in_specs=[pl.BlockSpec(memory_space=pltpu.VMEM)] * 5,
        out_specs=(pl.BlockSpec(memory_space=pltpu.HBM), pl.BlockSpec(memory_space=pltpu.HBM)),
        scratch_shapes=[
            pltpu.VMEM(SHAPE, F32),
            pltpu.VMEM(SHAPE, F32),
            pltpu.SemaphoreType.DMA((2, 8)),
        ],
        compiler_params=pltpu.CompilerParams(vmem_limit_bytes=32 * 1024 * 1024),
    )(*handed)
    full = (5, 4, 4, 4, 8, 256)
    return adv.reshape(full), new.reshape(full)


def solution(mesh):
    spec = P(None, None, None, None, "layer", "foot")
    return jax.shard_map(
        per_device,
        mesh=mesh,
        in_specs=(spec, spec, P(None, "foot"), P(None, "foot")),
        out_specs=(spec, spec),
        check_vma=False,
    )
```

```python
import functools

import jax
import jax.numpy as jnp
import numpy as np
from jax import lax
from jax.experimental import pallas as pl
from jax.experimental.pallas import tpu as pltpu
from jax.sharding import PartitionSpec as P

TIME_STEP = 0.02
SECTION_DECAY = -0.4178904745
SECTION_WEIGHT = 1.720146321549
LIFT = 3.0 * TIME_STEP
FREE_STREAM = (1.0, 0.3, 0.1, 0.0, 1.0 / 0.56 + 0.05)
MESH = pl.DeviceIdType.MESH
SLOTS = 16
BF16 = jnp.bfloat16
F32 = jnp.float32
TILES_Y = 4


def derivative_entries():
    nodes = np.array([-1.0, -1.0 / np.sqrt(5.0), 1.0 / np.sqrt(5.0), 1.0])
    products = np.array(
        [np.prod([nodes[t] - nodes[a] for a in range(4) if a != t]) for t in range(4)]
    )
    matrix = np.zeros((4, 4))
    for t in range(4):
        for s in range(4):
            if t != s:
                matrix[t, s] = products[t] / products[s] / (nodes[t] - nodes[s])
            else:
                matrix[t, t] = sum(1.0 / (nodes[t] - nodes[a]) for a in range(4) if a != t)
    return matrix


ENTRIES = -TIME_STEP * derivative_entries()
ODD = [[0.5 * float(ENTRIES[p, i] - ENTRIES[p, 3 - i]) for i in (0, 1)] for p in (0, 1)]
EVEN = [0.5 * float(ENTRIES[p, 0] + ENTRIES[p, 3]) for p in (0, 1)]


def derived(f):
    s0, d0 = f[0] + f[3], f[0] - f[3]
    s1, d1 = f[1] + f[2], f[1] - f[2]
    t = s0 - s1
    a = ODD[0][0] * d0 + ODD[0][1] * d1
    b = EVEN[0] * t
    c = ODD[1][0] * d0 + ODD[1][1] * d1
    e = EVEN[1] * t
    return a + b, c + e, c - e, a - b


def inverse(x):
    r = pl.reciprocal(x, approx=True)
    return r * (2.0 - x * r)


def split(x):
    hi = x.astype(BF16)
    lo = (x - hi.astype(F32)).astype(BF16)
    return hi, lo


def dot(a, b):
    return jnp.dot(a, b, preferred_element_type=F32)


def dot_nt(a, b):
    return lax.dot_general(a, b, (((1,), (1,)), ((), ())), preferred_element_type=F32)


def face_rows(side):
    face = (0, 3)[side % 2]
    return (slice(None), face) if side < 2 else (slice(None), slice(None), face)


def trace_of(cv, side):
    return cv[face_rows(side)].reshape(640, 256)


def primitive(q):
    r = inverse(q[0])
    kinetic = (q[1] * q[1] + q[2] * q[2] + q[3] * q[3]) * r
    pressure = 0.4 * q[4] - 0.2 * kinetic
    square = 1.4 * pressure * r
    return r, pressure, square * lax.rsqrt(square)


def gather_slots(stage, side, lane_z):
    total = stage[side, pl.ds(0, 80, stride=8), :]
    for z in range(1, 8):
        total = jnp.where(lane_z == z, stage[side, pl.ds(z, 80, stride=8), :], total)
    return total


def exchange_kernel(
    cons, reg, nb_in, kinds_in, cv, acc, ghost, vert, prim,
    nb, kinds, regv, picks, send_picks, selects, stage, packed, arrived, sendv, recvv,
    load_sem, send_sem, recv_sem, vsend_sem, vrecv_sem,
):
    foot, layer = lax.axis_index("foot"), lax.axis_index("layer")
    layers = lax.axis_size("layer")
    along, across = foot // TILES_Y, lax.rem(foot, TILES_Y)
    tiles = lax.axis_size("foot") // TILES_Y

    lower, upper = along > 0, along < tiles - 1
    left, right = across > 0, across < TILES_Y - 1
    below, above = layer > 0, layer < layers - 1
    sends = [
        ((foot + TILES_Y, layer), upper, lower),
        ((foot - TILES_Y, layer), lower, upper),
        ((foot + 1, layer), right, left),
        ((foot - 1, layer), left, right),
        ((foot, layer - 1), below, above),
        ((foot, layer + 1), above, below),
    ]

    barrier = pltpu.get_barrier_semaphore()
    partners = jnp.int32(0)
    for partner, there, _ in sends:
        partners = partners + there.astype(jnp.int32)

        @pl.when(there)
        def _():
            pl.semaphore_signal(barrier, inc=1, device_id=partner, device_id_type=MESH)

    nb_load = pltpu.make_async_copy(nb_in, nb, load_sem.at[6])
    nb_load.start()
    kinds_load = pltpu.make_async_copy(kinds_in, kinds, load_sem.at[7])
    kinds_load.start()
    loads = [
        pltpu.make_async_copy(cons.at[:, :, :, part], cv.at[:, :, :, part], load_sem.at[n])
        for n, part in enumerate((pl.ds(0, 8), pl.ds(24, 8), pl.ds(8, 16)))
    ]
    for copy in loads:
        copy.start()
    reg_load = pltpu.make_async_copy(reg, regv, load_sem.at[5])

    slot = lax.bitwise_and(lax.broadcasted_iota(jnp.int32, (128, 256), 0), SLOTS - 1)
    lane_z = lax.broadcasted_iota(jnp.int32, (80, 128), 1) // SLOTS
    rows = lax.broadcasted_iota(jnp.int32, (256, 256), 0)
    cols = lax.broadcasted_iota(jnp.int32, (256, 256), 1)
    before = jnp.where(rows < cols, 1.0, 0.0).astype(BF16)
    nb_load.wait()
    here = nb[...] - foot * 256
    away = jnp.logical_or(here < 0, here >= 256)
    mask = jnp.where(away, 1.0, 0.0)
    mask8 = jnp.concatenate([mask, jnp.zeros_like(mask)], axis=0).astype(BF16)
    rank = jnp.where(away, dot(mask8, before)[0:4], -1.0).astype(jnp.int32)

    for way in (0, 1):
        loads[way].wait()
        for h in (0, 1):
            lanes = pl.ds(h * 128, 128)
            stage[2 * way + h] = cv[:, :, :, pl.ds(24 * way, 8), lanes].reshape(640, 128)
            sendv[way, :, lanes] = stage[2 * way + h, pl.ds(7 * way, 80, stride=8), :]

    copies = []
    for side in range(4):
        copies.append(pltpu.make_async_remote_copy(
            src_ref=packed.at[side], dst_ref=arrived.at[side], send_sem=send_sem.at[side],
            recv_sem=recv_sem.at[side], device_id=sends[side][0], device_id_type=MESH,
        ))
    for way in (0, 1):
        copies.append(pltpu.make_async_remote_copy(
            src_ref=sendv.at[way], dst_ref=recvv.at[way], send_sem=vsend_sem.at[way],
            recv_sem=vrecv_sem.at[way], device_id=sends[4 + way][0], device_id_type=MESH,
        ))
    def launch(which):
        for copy, (_, there, _) in list(zip(copies, sends))[which]:

            @pl.when(there)
            def _():
                copy.start()


    names = jnp.where(away, lax.bitwise_and(nb[...], 255), 1000).astype(F32)
    names_down = jnp.transpose(jnp.concatenate([names, names], axis=0))
    for side in range(4):
        less = jnp.where(names_down[:, side:side + 1] < names[side:side + 1], 1.0, 0.0)
        order = jnp.sum(less, axis=0, keepdims=True)
        order = jnp.where(away[side:side + 1], order, -1.0).astype(jnp.int32)
        picks[side] = jnp.where(order == slot, 1.0, 0.0).astype(BF16)

    kinds_load.wait()
    loads[2].wait()
    reg_load.start()

    def open_vertical(order=(4, 5)):
        pl.semaphore_wait(barrier, partners)
        for n in order:
            launch(slice(n, n + 1))

    first = layer == layers // 2 - 1
    pl.when(first)(functools.partial(open_vertical, (5, 4)))

    for side in range(4):
        hi, lo = split(trace_of(cv, side))
        send = jnp.where(rank[side:side + 1] == slot, 1.0, 0.0).astype(BF16)
        stage[side] = dot_nt(hi, send) + dot_nt(lo, send)
        packed[side ^ 1] = gather_slots(stage, side, lane_z)

    pl.when(jnp.logical_not(first))(open_vertical)
    launch(slice(0, 4))

    def z_lines(line, carry):
        i, j = line // 4, line % 4
        q = [[cv[v, i, j, pl.ds(8 * k, 8), :] for k in range(4)] for v in range(5)]
        flux = [[], [], [], [], []]
        for k in range(4):
            rho, mx, my, mz, energy = (q[v][k] for v in range(5))
            r, pressure, sound = primitive([q[v][k] for v in range(5)])
            vz = mz * r
            rows_k = pl.ds(8 * k, 8)
            prim[0, i, j, rows_k, :] = mx * r
            prim[1, i, j, rows_k, :] = my * r
            prim[2, i, j, rows_k, :] = vz
            prim[3, i, j, rows_k, :] = pressure
            prim[4, i, j, rows_k, :] = sound
            flux[0].append(mz)
            flux[1].append(mx * vz)
            flux[2].append(my * vz)
            flux[3].append(mz * vz + pressure)
            flux[4].append((energy + pressure) * vz)
        for v in range(5):
            out = derived(flux[v])
            for k in range(4):
                rows_k = pl.ds(8 * k, 8)
                acc[v, i, j, rows_k, :] = out[k]
        return carry

    lax.fori_loop(0, 16, z_lines, 0, unroll=4)


    def lines(direction, line, carry):
        a, k = line // 4, line % 4
        rows_k = pl.ds(pl.multiple_of(8 * k, 8), 8)

        def at(node):
            return (node, a, rows_k, slice(None)) if direction == 0 else (a, node, rows_k, slice(None))

        flux = [[], [], [], [], []]
        for node in range(4):
            vd = prim[(direction,) + at(node)]
            pressure = prim[(3,) + at(node)]
            m = [cv[(1 + c,) + at(node)] for c in range(3)]
            flux[0].append(m[direction])
            for c in range(3):
                entry = m[c] * vd
                if c == direction:
                    entry = entry + pressure
                flux[1 + c].append(entry)
            flux[4].append((cv[(4,) + at(node)] + pressure) * vd)
        for v in range(5):
            out = derived(flux[v])
            for node in range(4):
                total = acc[(v,) + at(node)] + out[node]
                if direction == 1:
                    total = total + SECTION_DECAY * regv[(v,) + at(node)]
                acc[(v,) + at(node)] = total
        return carry

    lax.fori_loop(0, 16, functools.partial(lines, 0), 0, unroll=4)
    reg_load.wait()
    lax.fori_loop(0, 16, functools.partial(lines, 1), 0, unroll=4)

    for side in range(4):
        hi, lo = split(trace_of(cv, side))
        select = jnp.where(here[(side ^ 1):(side ^ 1) + 1] == rows, 1.0, 0.0).astype(BF16)
        got = dot(jnp.concatenate([hi, lo], axis=0), select)
        got = got[:640] + got[640:]
        ghost[side ^ 1] = got.reshape(5, 4, 32, 256)

    lane_z3 = lax.broadcasted_iota(jnp.int32, (80, 8, 128), 2) // SLOTS
    sub_z3 = lax.broadcasted_iota(jnp.int32, (80, 8, 128), 1)
    for side in range(4):
        _, there, comes = sends[side]

        @pl.when(there)
        def _():
            copies[side].wait_send()

        @pl.when(comes)
        def _():
            copies[side].wait_recv()

        @pl.when(jnp.logical_not(comes))
        def _():
            arrived[side] = jnp.zeros((80, 128), F32)

        spread = jnp.where(lane_z3 == sub_z3, arrived[side][:, None, :], 0.0).reshape(640, 128)
        far_hi, far_lo = split(spread)
        both = jnp.concatenate([far_hi, far_lo], axis=1)
        twice = jnp.concatenate([picks[side], picks[side]], axis=0)
        got = ghost[side].reshape(640, 256) + dot(both, twice)
        own = trace_of(cv, side)
        kind = jnp.broadcast_to(kinds[side:side + 1], (128, 256))
        flip = jnp.where(kind == 1, -1.0, 1.0)
        for v in range(5):
            part = slice(128 * v, 128 * v + 128)
            inner = own[part] * flip if v == 1 + side // 2 else own[part]
            outer = jnp.where(kind == 0, got[part], jnp.where(kind == 2, FREE_STREAM[v], inner))
            ghost[side, v] = outer.reshape(4, 32, 256)

    for way in (0, 1):
        _, there, comes = sends[4 + way]

        @pl.when(there)
        def _():
            copies[4 + way].wait_send()

        @pl.when(comes)
        def _():
            copies[4 + way].wait_recv()

        @pl.when(jnp.logical_not(comes))
        def _():
            recvv[way] = jnp.zeros((80, 256), F32)

    for v in range(5):
        part = pl.ds(16 * v, 16)
        own = sendv[0, part, :]
        vert[0, part, :] = jnp.where(below, recvv[1, part, :], -own if v == 3 else own)
        vert[1, part, :] = jnp.where(above, recvv[0, part, :], jnp.full_like(own, FREE_STREAM[v]))


def surface_kernel(cv, acc, ghost, vert, prim, adv, new, adv_v, new_v, out_sem):
    sub = lax.broadcasted_iota(jnp.int32, (8, 128), 0)
    outs = []
    for i in range(4):

        def half(js, h, carry):
            lanes = pl.ds(pl.multiple_of(h * 128, 128), 128)
            for j in js:
                for k in range(4):
                    rows_k = pl.ds(8 * k, 8)
                    q = [cv[v, i, j, rows_k, lanes] for v in range(5)]
                    total = [acc[v, i, j, rows_k, lanes] for v in range(5)]
                    faces = []
                    if i in (0, 3):
                        faces.append((0, 0 if i == 0 else 1, (j, k)))
                    if j in (0, 3):
                        faces.append((1, 2 if j == 0 else 3, (i, k)))
                    if k in (0, 3):
                        faces.append((2, 4 if k == 0 else 5, (i, j)))
                    if faces:
                        p_in, c_in = (prim[v, i, j, rows_k, lanes] for v in (3, 4))
                    for d, side, (a, b) in faces:
                        if side < 4:
                            outer = [ghost[side, v, a, pl.ds(8 * b, 8), lanes] for v in range(5)]
                        else:
                            outer = []
                            for v in range(5):
                                m = v * 16 + a * 4 + b
                                if side == 4:
                                    near = cv[v, i, j, pl.ds(24, 8), lanes]
                                    near = pltpu.roll(near, 1, 0)
                                    edge = jnp.broadcast_to(vert[0, m:m + 1, lanes], (8, 128))
                                    outer.append(jnp.where(sub == 0, edge, near))
                                else:
                                    near = cv[v, i, j, pl.ds(0, 8), lanes]
                                    near = pltpu.roll(near, 7, 0)
                                    edge = jnp.broadcast_to(vert[1, m:m + 1, lanes], (8, 128))
                                    outer.append(jnp.where(sub == 7, edge, near))
                        sign = -1.0 if side % 2 == 0 else 1.0
                        r_out, p_out, c_out = primitive(outer)
                        v_in, v_out = prim[d, i, j, rows_k, lanes], outer[1 + d] * r_out
                        lam = LIFT * jnp.maximum(jnp.abs(v_in) + c_in, jnp.abs(v_out) + c_out)
                        s_in, s_out = (sign * LIFT) * v_in, (sign * LIFT) * v_out
                        w_in, w_out = lam - s_in, lam - s_out
                        for v in range(5):
                            total[v] = total[v] + (w_out * outer[v] - w_in * q[v])
                        total[1 + d] = total[1 + d] - (sign * LIFT) * (p_out - p_in)
                        total[4] = total[4] - (p_out * s_out - p_in * s_in)
                    for v in range(5):
                        new_v[v, i, j, rows_k, lanes] = total[v]
                        adv_v[v, i, j, rows_k, lanes] = q[v] + SECTION_WEIGHT * total[v]
            return carry

        for part in range(2):
            js = (2 * part, 2 * part + 1)
            lax.fori_loop(0, 2, functools.partial(half, js), 0)
            for n, (src, dst) in enumerate(((adv_v, adv), (new_v, new))):
                js_here = pl.ds(2 * part, 2)
                copy = pltpu.make_async_copy(src.at[:, i, js_here], dst.at[:, i, js_here], out_sem.at[n, 2 * i + part])
                copy.start()
                outs.append(copy)
    for copy in outs:
        copy.wait()


SHAPE = (5, 4, 4, 32, 256)


def per_device(conserved, register, neighbour, side_type):
    inputs = [
        pltpu.with_memory_space_constraint(x, pltpu.HBM)
        for x in (conserved.reshape(SHAPE), register.reshape(SHAPE), neighbour, side_type)
    ]
    handed = pl.pallas_call(
        exchange_kernel,
        name="exchange",
        out_shape=(
            pltpu.VMEM(SHAPE, F32),
            pltpu.VMEM(SHAPE, F32),
            pltpu.VMEM((4, 5, 4, 32, 256), F32),
            pltpu.VMEM((2, 80, 256), F32),
            pltpu.VMEM(SHAPE, F32),
        ),
        in_specs=[pl.BlockSpec(memory_space=pltpu.HBM)] * 4,
        out_specs=tuple([pl.BlockSpec(memory_space=pltpu.VMEM)] * 5),
        scratch_shapes=[
            pltpu.VMEM((4, 256), jnp.int32),
            pltpu.VMEM((4, 256), jnp.int32),
            pltpu.VMEM(SHAPE, F32),
            pltpu.VMEM((4, 128, 256), BF16),
            pltpu.VMEM((4, 128, 256), BF16),
            pltpu.VMEM((4, 256, 256), BF16),
            pltpu.VMEM((4, 640, 128), F32),
            pltpu.VMEM((4, 80, 128), F32),
            pltpu.VMEM((4, 80, 128), F32),
            pltpu.VMEM((2, 80, 256), F32),
            pltpu.VMEM((2, 80, 256), F32),
            pltpu.SemaphoreType.DMA((8,)),
            pltpu.SemaphoreType.DMA((4,)),
            pltpu.SemaphoreType.DMA((4,)),
            pltpu.SemaphoreType.DMA((2,)),
            pltpu.SemaphoreType.DMA((2,)),
        ],
        compiler_params=pltpu.CompilerParams(
            collective_id=0, has_side_effects=True, vmem_limit_bytes=40 * 1024 * 1024
        ),
    )(*inputs)
    handed = [pltpu.with_memory_space_constraint(x, pltpu.VMEM) for x in handed]
    adv, new = pl.pallas_call(
        surface_kernel,
        name="surface",
        out_shape=(jax.ShapeDtypeStruct(SHAPE, F32), jax.ShapeDtypeStruct(SHAPE, F32)),
        in_specs=[pl.BlockSpec(memory_space=pltpu.VMEM)] * 5,
        out_specs=(pl.BlockSpec(memory_space=pltpu.HBM), pl.BlockSpec(memory_space=pltpu.HBM)),
        scratch_shapes=[
            pltpu.VMEM(SHAPE, F32),
            pltpu.VMEM(SHAPE, F32),
            pltpu.SemaphoreType.DMA((2, 8)),
        ],
        compiler_params=pltpu.CompilerParams(vmem_limit_bytes=32 * 1024 * 1024),
    )(*handed)
    full = (5, 4, 4, 4, 8, 256)
    return adv.reshape(full), new.reshape(full)


def solution(mesh):
    spec = P(None, None, None, None, "layer", "foot")
    return jax.shard_map(
        per_device,
        mesh=mesh,
        in_specs=(spec, spec, P(None, "foot"), P(None, "foot")),
        out_specs=(spec, spec),
        check_vma=False,
    )
```
